32 devices in a mesh: seq: 8 (over z, x), tensor: 2 (over y), dp: 2 (over core).
Axes of the slice: x: 2, y: 2, z: 4, core: 2. Of those that a mesh axis runs over, the one named last changes fastest.
Arguments:
- x_stream: bfloat16 [8192, 5120], P(('dp', 'seq'), 'tensor'), parts along dimension 0
- bc_stream: bfloat16 [8192, 256], P(('dp', 'seq')), parts along dimension 0, may hold values from -6 to 6
- z_gate: bfloat16 [8192, 5120], P(('dp', 'seq'), 'tensor'), parts along dimension 0
- dt_stream: bfloat16 [80, 8192], P('tensor', ('dp', 'seq')), parts along dimension 1, as said below
- doc_ids: int32 [8192], P(('dp', 'seq')), parts along dimension 0, may hold values from 0 to 7, never falling along the last dimension, each value on 1 to 2048 neighbouring positions
- conv_x: bfloat16 [4, 5120], P(None, 'tensor'), may hold values from -3 to 3
- conv_bc: bfloat16 [4, 256], replicated, may hold values from -3 to 3
- a_log: float32 [80], P('tensor')
- dt_bias: float32 [80], P('tensor'), as said below
- d_skip: float32 [80], P('tensor'), may hold values from 0.5 to 4
- norm_gain: float32 [5120], P('tensor'), may hold values from 0.5 to 1.5
- w_out: bfloat16 [5120, 2560], P('tensor'), may hold values from -0.078125 to 0.078125
Outputs:
- layer_out: bfloat16 [8192, 2560], P(('dp', 'seq'), 'tensor'), parts along dimension 0
The draws below stay inside these ranges and needn't reach their ends.
There are 2 independent parts, one for each index of `dp`. The reference program is written for one: setup_inputs(seed, part) draws one part's arguments, and reference() takes and returns one part's arrays. A program takes and returns all parts, laid end to end along the dimension named above; an argument that names none is the same for every part. Nothing has to cross between parts.
Inputs may be any that keep to these rules, and one draw needn't show every extreme that they name: `doc_ids`: document ids never fall along the tokens; each document has 1 to 2048 tokens and one has exactly 2048. `dt_bias`: step size bias. `dt_stream`: step size logits.
All inputs are finite; a program needn't handle non-finite values.
Results may differ from the reference program's by a relative error of at most 0.017.
Values may be sent and summed in bfloat16 or wider, within the bound.
A program may use at most 64 MiB of HBM per device.

```python
import math
import jax
import jax.numpy as jnp
import numpy as np
from jax import lax

D = 2560
HEADS = 80
HEADDIM = 64
NSTATE = 128
SPAN = 256
KCONV = 4
TOK_DEV = 512
DOCS = 8
INNER = 5120
TOKENS = 4096
MOST = 2048
N_TENSOR = 2


def head_law(key):
    folded = jax.random.fold_in(key, 7)
    chooser, step_key, rapid_key, steady_key = jax.random.split(folded, 4)
    portion = 0.5
    rapid_mask = jax.random.uniform(chooser, (HEADS,), jnp.float32) < portion
    base_step = jnp.exp(jax.random.uniform(step_key, (HEADS,), jnp.float32, math.log(0.02), math.log(0.1)))
    rapid_rate = jnp.exp(jax.random.uniform(rapid_key, (HEADS,), jnp.float32, math.log(0.02), math.log(0.033)))
    steady = jnp.exp(jax.random.uniform(steady_key, (HEADS,), jnp.float32, math.log(0.2), math.log(1.0)))
    strength = jnp.where(rapid_mask, rapid_rate / base_step, steady / (base_step * TOKENS))
    return (jnp.log(strength), jnp.log(jnp.expm1(base_step)))


def draw_a_log(key, part):
    return head_law(key)[0].astype(jnp.float32)


def draw_dt_bias(key, part):
    return head_law(key)[1].astype(jnp.float32)


def draw_dt_stream(key, part):
    noise_key, block_key, drop_key, depth_key = jax.random.split(jax.random.fold_in(key, 13), 4)
    shard_count = TOKENS // TOK_DEV
    noise = 0.4 * jax.random.normal(noise_key, (HEADS, TOKENS), jnp.float32)
    shifts = jax.random.uniform(block_key, (HEADS, shard_count), jnp.float32, -0.5, 0.5)
    lowered = jax.random.uniform(drop_key, (HEADS, shard_count), jnp.float32) < 0.7
    depth = jax.random.uniform(depth_key, (HEADS, shard_count), jnp.float32, -6.0, -3.0)
    shifts = shifts + jnp.where(lowered, depth, 0.0)
    return (noise + jnp.repeat(shifts, TOK_DEV, axis=1)).astype(jnp.bfloat16)


def draw_x_stream(key, part):
    noise_key = jax.random.fold_in(key, 19)
    shard_count = TOKENS // TOK_DEV
    noise = jnp.clip(jax.random.normal(noise_key, (TOKENS, INNER), jnp.float32), -6.0, 6.0)
    position = (jnp.arange(TOKENS, dtype=jnp.int32) // TOK_DEV).astype(jnp.float32)
    level = 0.03 * jnp.exp(-math.log(3.0) * position / max(shard_count - 1, 1))
    return (noise * level[:, None]).astype(jnp.bfloat16)


def draw_z_gate(key, part):
    noise_key, row_key = jax.random.split(jax.random.fold_in(key, 17), 2)
    columns = jnp.arange(INNER, dtype=jnp.float32) / INNER
    column_scale = 10.0 ** columns
    noise = jax.random.normal(noise_key, (TOKENS, INNER), jnp.float32)
    row_scale = 10.0 ** jax.random.uniform(row_key, (TOKENS, 1), jnp.float32)
    return (noise * column_scale[None, :] * row_scale).astype(jnp.bfloat16)


def block_levels(rng, extent, cuts, least, top_value):
    gain = 1.0
    for dim, parts in cuts:
        draws = jax.random.uniform(jax.random.fold_in(jax.random.fold_in(rng, 6), dim), (parts,), jnp.float32, least / len(cuts), top_value / len(cuts))
        gain = gain * jnp.repeat(jnp.exp(draws), extent[dim] // parts).reshape((-1,) + (1,) * (len(extent) - 1 - dim))
    return gain


def split_up(count, total, bound, slope):
    loads = [(1 << 20) // math.isqrt(rank ** slope) + 1 for rank in range(2, count + 1)]
    spare, counts = total - bound - (count - 1), [1] * (count - 1)
    while spare > 0:
        free = [i for i in range(count - 1) if counts[i] < bound]
        whole, budget = sum([loads[i] for i in free]), spare
        for i in free:
            addition = min(bound - counts[i], max(1, budget * loads[i] // whole), spare)
            counts[i] = counts[i] + addition
            spare = spare - addition
    return np.array([bound] + counts)


def uneven_parts(stream_key, amount, total, most, skew):
    if amount == 2:
        one = jax.random.randint(stream_key, (), max(1, total - most), min(most, total - 1) + 1)
        return jnp.stack([one, total - one])
    tallies = jnp.asarray(split_up(amount, total, most, skew), jnp.int32)
    twos = (amount - 1) // 2
    donor, sink = tallies[1:1 + 2 * twos:2], tallies[2:2 + 2 * twos:2]
    room = jnp.minimum(donor - 1, most - sink)
    moved = jax.random.randint(jax.random.fold_in(stream_key, 1), (twos,), 0, 1 << 20) % (room + 1)
    tallies = tallies.at[1:1 + 2 * twos:2].set(donor - moved).at[2:2 + 2 * twos:2].set(sink + moved)
    return tallies[jax.random.permutation(jax.random.fold_in(stream_key, 2), amount)]


def centred(own_key, extent, width, reach, pieces=(), held_as=jnp.bfloat16):
    gain = block_levels(own_key, extent, pieces, -0.22, 0.18) if pieces else 1.0
    result = jax.random.normal(own_key, extent, jnp.float32) * width * gain
    return jnp.minimum(jnp.maximum(result, -reach), reach).astype(held_as)


def setup_inputs(seed: int = 0, part: int = 0) -> dict:
    splits = jax.random.split(jax.random.key(seed), 13)
    part_splits = jax.random.split(jax.random.fold_in(splits[12], part), 13)
    return {
        "x_stream": draw_x_stream(jax.random.fold_in(jax.random.fold_in(splits[12], part), 71), part),
        "bc_stream": centred(part_splits[1], (TOKENS, 2 * NSTATE), 1.0, 6.0, ((0, 8),)),
        "z_gate": draw_z_gate(jax.random.fold_in(jax.random.fold_in(splits[12], part), 71), part),
        "dt_stream": draw_dt_stream(jax.random.fold_in(jax.random.fold_in(splits[12], part), 71), part),
        "doc_ids": jnp.searchsorted(jnp.cumsum(uneven_parts(part_splits[4], DOCS, TOKENS, MOST, 2)), jnp.arange(TOKENS), side="right").astype(jnp.int32),
        "conv_x": centred(splits[5], (KCONV, INNER), KCONV ** -0.5, 3.0, ((1, 2),)),
        "conv_bc": centred(splits[6], (KCONV, 2 * NSTATE), KCONV ** -0.5, 3.0),
        "a_log": draw_a_log(jax.random.fold_in(splits[12], 71), part),
        "dt_bias": draw_dt_bias(jax.random.fold_in(splits[12], 71), part),
        "d_skip": jnp.clip(jnp.exp(math.log(4.0) - 2.0794415 * jax.random.uniform(splits[9], (HEADS,), jnp.float32) ** block_levels(splits[9], (HEADS,), ((0, 2),), -0.2, 0.2)), 0.5, 4.0),
        "norm_gain": jnp.clip(0.5 + 1.0 * jax.random.uniform(splits[10], (INNER,), jnp.float32) ** block_levels(splits[10], (INNER,), ((0, 2),), -0.2, 0.2), 0.5, 1.5),
        "w_out": centred(splits[11], (INNER, D), INNER ** -0.5, 0.078125, ((0, 2),)),
    }


def causal_conv(values, weights, doc_ids):
    row_count = values.shape[0]
    total = jnp.zeros(values.shape, jnp.float32)
    for offset in range(KCONV):
        shifted = jnp.pad(values, ((offset, 0), (0, 0)))[:row_count]
        earlier = jnp.pad(doc_ids, (offset, 0), constant_values=-1)[:row_count]
        keep_mask = earlier == doc_ids
        total = total + jnp.where(keep_mask[:, None], shifted.astype(jnp.float32) * weights[offset].astype(jnp.float32), 0.0)
    return jax.nn.silu(total).astype(jnp.bfloat16)

def reference(x_stream, bc_stream, z_gate, dt_stream, doc_ids, conv_x, conv_bc, a_log, dt_bias, d_skip, norm_gain, w_out):
    highest = lax.Precision.HIGHEST
    mixed_x = lax.optimization_barrier(causal_conv(x_stream, conv_x, doc_ids))
    mixed_bc = lax.optimization_barrier(causal_conv(bc_stream, conv_bc, doc_ids))
    step_size = jax.nn.softplus(dt_stream.astype(jnp.float32) + dt_bias[:, None])
    log_rates = -jnp.exp(a_log)[:, None] * step_size
    blocks = TOKENS // SPAN
    block_x = mixed_x.reshape(blocks, SPAN, HEADS, HEADDIM)
    b_vals = mixed_bc[:, :NSTATE].reshape(blocks, SPAN, NSTATE)
    c_vals = mixed_bc[:, NSTATE:].reshape(blocks, SPAN, NSTATE)
    block_steps = step_size.reshape(HEADS, blocks, SPAN).transpose(1, 0, 2)
    block_rates = log_rates.reshape(HEADS, blocks, SPAN).transpose(1, 0, 2)
    block_ids = doc_ids.reshape(blocks, SPAN)
    before = jnp.concatenate([jnp.full((1,), -1, jnp.int32), doc_ids[SPAN - 1::SPAN][:blocks - 1].astype(jnp.int32)])
    lower_mask = jnp.tril(jnp.ones((SPAN, SPAN), jnp.bool_))

    def advance(carry_state, inputs_now):
        x_blk, b_blk, c_blk, dt_blk, rate_blk, id_blk, prior = inputs_now
        cum_rates = jnp.cumsum(rate_blk, axis=1)
        same_doc = (id_blk[:, None] == id_blk[None, :]) & lower_mask
        spread = cum_rates[:, :, None] - cum_rates[:, None, :]
        decay_now = jnp.where(same_doc[None], jnp.exp(jnp.minimum(spread, 0.0)), 0.0)
        b_wide = b_blk.astype(jnp.float32)
        c_wide = c_blk.astype(jnp.float32)
        x_wide = x_blk.astype(jnp.float32)
        scores = jnp.dot(c_wide, b_wide.T, precision=highest)
        weights = lax.optimization_barrier((scores[None] * decay_now * dt_blk[:, None, :]).astype(jnp.bfloat16)).astype(jnp.float32)
        diagonal = jnp.einsum('hts,shp->thp', weights, x_wide, precision=highest)
        carried = id_blk == prior
        entry_gain = jnp.where(carried[None], jnp.exp(cum_rates), 0.0)
        reach_term = jnp.einsum('tn,hpn->thp', c_wide, carry_state, precision=highest) * entry_gain.T[:, :, None]
        tail_weight = jnp.where((id_blk == id_blk[-1])[None], jnp.exp(cum_rates[:, -1:] - cum_rates), 0.0) * dt_blk
        fresh_state = jnp.einsum('shp,sn->hpn', x_wide * tail_weight.T[:, :, None], b_wide, precision=highest)
        block_decay = jnp.where(carried[-1], jnp.exp(cum_rates[:, -1]), 0.0)
        y_block = diagonal + reach_term + d_skip[None, :, None] * x_wide
        next_state = block_decay[:, None, None] * carry_state + fresh_state
        return (next_state, y_block.astype(jnp.bfloat16).reshape(SPAN, INNER))
    start_state = jnp.zeros((HEADS, HEADDIM, NSTATE), jnp.float32)
    final_state, y_all = lax.scan(advance, start_state, (block_x, b_vals, c_vals, block_steps, block_rates, block_ids, before))
    y_vals = lax.optimization_barrier(y_all.reshape(TOKENS, INNER))
    gated = y_vals.astype(jnp.float32) * jax.nn.silu(z_gate.astype(jnp.float32))
    inv_norm = lax.rsqrt(lax.optimization_barrier(jnp.mean(gated * gated, axis=1)) + 1e-05)
    normed = (gated * inv_norm[:, None] * norm_gain[None, :]).astype(jnp.bfloat16)
    group_width = INNER // N_TENSOR
    total = jnp.zeros((TOKENS, D), jnp.float32)
    for member in range(N_TENSOR):
        lower = member * group_width
        product = jnp.dot(normed[:, lower:lower + group_width], w_out[lower:lower + group_width], preferred_element_type=jnp.float32)
        total = total + lax.optimization_barrier(product.astype(jnp.bfloat16)).astype(jnp.float32)
    return total.astype(jnp.bfloat16)
```

```python
import jax
import jax.numpy as jnp
from jax import lax
from jax.sharding import PartitionSpec as P

SPAN = 256


def from_behind(block, axis, distance):
    devices = range(lax.axis_size(axis))
    route = [(i - distance, i) for i in devices if i - distance in devices]
    return lax.ppermute(block, axis, route)


def causal_conv(extended, weights, ext_ids, own_ids, row_count):
    tap_count = weights.shape[0]
    total = jnp.zeros((row_count, extended.shape[1]), jnp.float32)
    for offset in range(tap_count):
        first_row = tap_count - 1 - offset
        window = extended[first_row : first_row + row_count]
        keep_mask = ext_ids[first_row : first_row + row_count] == own_ids
        total = total + jnp.where(
            keep_mask[:, None],
            window.astype(jnp.float32) * weights[offset].astype(jnp.float32),
            0.0,
        )
    return jax.nn.silu(total).astype(jnp.bfloat16)


def shifted(block, axis, distance):
    count = lax.axis_size(axis)
    return lax.ppermute(block, axis, [(i, i + distance) for i in range(count - distance)])


def pass_state(decays, local_final):
    count = lax.axis_size("seq")
    me = lax.axis_index("seq")
    partner = [(i, i ^ 1) for i in range(count)]
    odd = (me % 2) == 1
    other = lax.ppermute(local_final.astype(jnp.bfloat16), "seq", partner).astype(jnp.float32)
    first = jnp.where(odd, other, local_final)
    second = jnp.where(odd, local_final, other)
    pair = me // 2
    pair_decays = decays.reshape(count // 2, 2, -1)
    whole_pair = second + pair_decays[pair, 1][:, None, None] * first
    both = pair_decays[:, 0] * pair_decays[:, 1]
    entering = shifted(whole_pair.astype(jnp.bfloat16), "seq", 2).astype(jnp.float32)
    covered = both
    reach = 1
    while reach < count // 4:
        nearer = jnp.where(pair >= 1, covered[jnp.maximum(pair - 1, 0)], 0.0)
        farther = shifted(entering.astype(jnp.bfloat16), "seq", 2 * reach).astype(jnp.float32)
        entering = entering + nearer[:, None, None] * farther
        covered = covered * jnp.concatenate([jnp.zeros_like(covered[:reach]), covered[:-reach]])
        reach *= 2
    return jnp.where(odd, other + pair_decays[pair, 0][:, None, None] * entering, entering)


def local(
    x_stream,
    bc_stream,
    z_gate,
    dt_stream,
    doc_ids,
    conv_x,
    conv_bc,
    a_log,
    dt_bias,
    d_skip,
    norm_gain,
    w_out,
):
    row_count = x_stream.shape[0]
    head_count = dt_stream.shape[0]
    inner_width = x_stream.shape[1]
    head_size = inner_width // head_count
    state_size = bc_stream.shape[1] // 2
    tap_count = conv_x.shape[0]
    blocks = row_count // SPAN
    edge_start = row_count - tap_count + 1
    own_ids = doc_ids.astype(jnp.float32)
    tail_ids = jnp.broadcast_to(
        own_ids[edge_start:].astype(jnp.bfloat16)[:, None], (tap_count - 1, 128)
    )
    rim = shifted(
        jnp.concatenate([x_stream[edge_start:], bc_stream[edge_start:], tail_ids], axis=1), "seq", 1
    )
    rim_x = rim[:, :inner_width]
    rim_bc = rim[:, inner_width : inner_width + 2 * state_size]
    rim_ids = jnp.where(
        lax.axis_index("seq") == 0, -1.0, rim[:, inner_width + 2 * state_size].astype(jnp.float32)
    )
    ext_ids = jnp.concatenate([rim_ids, own_ids])
    mixed_x = causal_conv(jnp.concatenate([rim_x, x_stream]), conv_x, ext_ids, own_ids, row_count)
    mixed_bc = causal_conv(
        jnp.concatenate([rim_bc, bc_stream]), conv_bc, ext_ids, own_ids, row_count
    )
    prior_id = ext_ids[tap_count - 2]
    step_size = jax.nn.softplus(dt_stream.astype(jnp.float32) + dt_bias[:, None])
    log_rates = -jnp.exp(a_log)[:, None] * step_size
    block_steps = step_size.reshape(head_count, blocks, SPAN)
    cum_rates = jnp.cumsum(log_rates.reshape(head_count, blocks, SPAN), axis=2)
    block_x = mixed_x.reshape(blocks, SPAN, head_count, head_size)
    b_vals = mixed_bc[:, :state_size].reshape(blocks, SPAN, state_size)
    c_vals = mixed_bc[:, state_size:].reshape(blocks, SPAN, state_size)
    block_ids = own_ids.reshape(blocks, SPAN)
    before = jnp.concatenate([prior_id[None], own_ids[SPAN - 1 :: SPAN][: blocks - 1]])
    carried = block_ids == before[:, None]
    entry_gain = jnp.where(carried[None], jnp.exp(cum_rates), 0.0)
    tail_weight = (
        jnp.where(
            (block_ids == block_ids[:, -1:])[None], jnp.exp(cum_rates[:, :, -1:] - cum_rates), 0.0
        )
        * block_steps
    )
    weighted = (
        block_x.astype(jnp.float32) * jnp.transpose(tail_weight, (1, 2, 0))[..., None]
    ).astype(jnp.bfloat16)
    block_states = jnp.einsum(
        "cshp,csn->chpn", weighted, b_vals, preferred_element_type=jnp.float32
    )
    block_decay = jnp.where(carried[:, -1][None], jnp.exp(cum_rates[:, :, -1]), 0.0)
    decays = lax.all_gather(jnp.prod(block_decay, axis=1), "seq")
    skip_term = d_skip[None, None, :, None] * block_x.astype(jnp.float32)
    zero_state = jnp.zeros((head_count, head_size, state_size), jnp.float32)

    def advance(carry_state, inputs_now):
        decay_now, fresh_state = inputs_now
        return (decay_now[:, None, None] * carry_state + fresh_state, carry_state)

    local_final, local_entries = lax.scan(advance, zero_state, (block_decay.T, block_states))
    reached = jnp.einsum("ctn,chpn->cthp", c_vals, local_entries.astype(jnp.bfloat16), preferred_element_type=jnp.float32)
    lower_mask = jnp.tril(jnp.ones((SPAN, SPAN), jnp.bool_))
    same_doc = (block_ids[:, :, None] == block_ids[:, None, :]) & lower_mask[None]
    spread = cum_rates[:, :, :, None] - cum_rates[:, :, None, :]
    decay_now = jnp.where(same_doc[None], jnp.exp(jnp.minimum(spread, 0.0)), 0.0)
    scores = jnp.einsum("ctn,csn->cts", c_vals, b_vals, preferred_element_type=jnp.float32)
    weights = (scores[None] * decay_now * block_steps[:, :, None, :]).astype(jnp.bfloat16)
    result = (
        jnp.einsum("hcts,cshp->cthp", weights, block_x, preferred_element_type=jnp.float32)
        + reached * jnp.transpose(entry_gain, (1, 2, 0))[..., None]
        + skip_term
    )
    incoming = pass_state(decays, local_final)
    prefix = jnp.cumprod(
        jnp.concatenate([jnp.ones((head_count, 1), jnp.float32), block_decay[:, :-1]], axis=1),
        axis=1,
    )
    reach_term = jnp.einsum("ctn,hpn->cthp", c_vals, incoming.astype(jnp.bfloat16), preferred_element_type=jnp.float32)
    result = (
        result + reach_term * jnp.transpose(entry_gain * prefix[:, :, None], (1, 2, 0))[..., None]
    )
    y_vals = lax.optimization_barrier(result.reshape(row_count, inner_width).astype(jnp.bfloat16))
    gated = y_vals.astype(jnp.float32) * jax.nn.silu(z_gate.astype(jnp.float32))
    squares = lax.psum(jnp.sum(gated * gated, axis=1), "tensor")
    inv_norm = lax.rsqrt(squares / (inner_width * lax.axis_size("tensor")) + 1e-05)
    scaled = (gated * norm_gain[None, :]).astype(jnp.bfloat16)
    members = lax.axis_size("tensor")
    member = lax.axis_index("tensor")
    width = w_out.shape[1] // members
    chunks = 2
    length = row_count // chunks
    pieces = []
    for chunk in range(chunks):
        rows = slice(chunk * length, (chunk + 1) * length)
        product = jnp.dot(scaled[rows], w_out, preferred_element_type=jnp.float32).astype(
            jnp.bfloat16
        )
        total = lax.dynamic_slice_in_dim(product, member * width, width, 1).astype(jnp.float32)
        for distance in range(1, members):
            target = (member + distance) % members
            block = lax.dynamic_slice_in_dim(product, target * width, width, 1)
            route = [(i, (i + distance) % members) for i in range(members)]
            total = total + lax.ppermute(block, "tensor", route).astype(jnp.float32)
        pieces.append((total * inv_norm[rows][:, None]).astype(jnp.bfloat16))
    return jnp.concatenate(pieces)


def solution(mesh):
    return jax.shard_map(
        local,
        mesh=mesh,
        in_specs=(
            P(("dp", "seq"), "tensor"),
            P(("dp", "seq"), None),
            P(("dp", "seq"), "tensor"),
            P("tensor", ("dp", "seq")),
            P(("dp", "seq")),
            P(None, "tensor"),
            P(),
            P("tensor"),
            P("tensor"),
            P("tensor"),
            P("tensor"),
            P("tensor", None),
        ),
        out_specs=P(("dp", "seq"), "tensor"),
        check_vma=False,
    )
```

```python
import functools

import jax
import jax.numpy as jnp
from jax import lax
from jax.experimental import pallas as pl
from jax.experimental.pallas import tpu as pltpu
from jax.sharding import PartitionSpec as P

SPAN = 256
HEADS_PAD = 128
EXTRA = 16
VMEM_BYTES = 48 * 1024 * 1024


def shifted(block, axis, distance):
    count = lax.axis_size(axis)
    return lax.ppermute(block, axis, [(i, i + distance) for i in range(count - distance)])


def group_lanes(width):
    return 256 if width % 256 == 0 else 128


def silu(v):
    return v / (1.0 + jnp.exp(-v))


def spread_heads(columns, width, lanes):
    rows = columns.shape[0]
    lane = lax.broadcasted_iota(jnp.int32, (rows, 128), 1)
    per_tile = 128 // width
    tiles = []
    for tile in range(lanes // 128):
        value = jnp.broadcast_to(columns[:, tile * per_tile : tile * per_tile + 1], (rows, 128))
        for k in range(1, per_tile):
            head = tile * per_tile + k
            value = jnp.where(
                lane >= k * width, jnp.broadcast_to(columns[:, head : head + 1], (rows, 128)), value
            )
        tiles.append(value)
    return jnp.concatenate(tiles, axis=1)


def conv_taps(ext, weights, keeps, rows):
    wide = weights.shape[1]
    total = weights[0:1] * ext[pl.ds(8, rows), :wide]
    for k in range(1, weights.shape[0]):
        total = total + jnp.where(keeps[k - 1][:, :wide], weights[k : k + 1] * ext[pl.ds(8 - k, rows), :wide], 0.0)
    return silu(total)


def states_kernel(
    head_size,
    x_ref, rim_x_ref, bc_ref, rim_bc_ref, step_ref, rate_ref, flags_ref, conv_x_ref, conv_bc_ref,
    mixed_ref, bc_out_ref, cum_ref, cum_t_ref, step_t_ref, gain_t_ref, fresh_ref, decay_ref, msg_ref,
    ext, tail_t, b_t,
):
    rows, width = x_ref.shape
    blocks = rows // SPAN
    size = group_lanes(width)
    per_group = size // head_size
    state_size = bc_ref.shape[1] // 2
    flags = flags_ref[...]
    taps = conv_x_ref.shape[0]
    keeps = [
        jnp.broadcast_to(flags[:, k : k + 1], (rows, ext.shape[1])) > 0.5 for k in range(taps - 1)
    ]
    carried = jnp.broadcast_to(flags[:, 3:4], (rows, HEADS_PAD)) > 0.5
    in_tail = jnp.broadcast_to(flags[:, 4:5], (rows, HEADS_PAD)) > 0.5

    ext[0:8, :] = rim_bc_ref[...]
    ext[8 : 8 + rows, :] = bc_ref[...].astype(jnp.float32)
    mixed_bc = conv_taps(ext, conv_bc_ref[...], keeps, rows)
    bc_out_ref[...] = mixed_bc.astype(jnp.bfloat16)
    row_id = lax.broadcasted_iota(jnp.int32, (SPAN, SPAN), 0)
    col_id = lax.broadcasted_iota(jnp.int32, (SPAN, SPAN), 1)
    upper = (row_id <= col_id).astype(jnp.float32)
    for b in range(blocks):
        span = slice(b * SPAN, (b + 1) * SPAN)
        b_t[:, span] = mixed_bc[span, :state_size].T.astype(jnp.bfloat16)
        cum = jnp.dot(
            rate_ref[:, span], upper,
            precision=lax.Precision.HIGHEST, preferred_element_type=jnp.float32,
        )
        cum_ref[:, span] = cum
        cum_t = cum.T
        step_t = step_ref[:, span].T
        cum_t_ref[span, :] = cum_t
        step_t_ref[span, :] = step_t
        gain_t_ref[span, :] = jnp.where(carried[span], jnp.exp(cum_t), 0.0)
        tail_t[span, :] = jnp.where(
            in_tail[span], jnp.exp(cum_t[SPAN - 1 : SPAN] - cum_t), 0.0
        ) * step_t

    def group(c, unused):
        lanes = pl.ds(pl.multiple_of(c * size, size), size)
        turn = lax.rem(HEADS_PAD - c * per_group, HEADS_PAD)
        ext[0:8, :size] = rim_x_ref[:, lanes]
        ext[8 : 8 + rows, :size] = x_ref[:, lanes].astype(jnp.float32)
        mixed = conv_taps(ext, conv_x_ref[:, lanes], keeps, rows).astype(jnp.bfloat16)
        mixed_ref[:, lanes] = mixed
        weight = spread_heads(pltpu.roll(tail_t[...], turn, 1), head_size, size)
        weighted = (mixed.astype(jnp.float32) * weight).astype(jnp.bfloat16)
        running = None
        through = None
        for b in range(blocks):
            span = slice(b * SPAN, (b + 1) * SPAN)
            fresh = jnp.dot(b_t[:, span], weighted[span], preferred_element_type=jnp.float32)
            ends = gain_t_ref[(b + 1) * SPAN - 8 : (b + 1) * SPAN, :]
            decay = spread_heads(pltpu.roll(ends, turn, 1), head_size, size)[7:8]
            fresh_ref[b, :, lanes] = fresh
            decay_ref[b, :, lanes] = jnp.broadcast_to(decay, (8, size))
            running = fresh if b == 0 else decay * running + fresh
            through = decay if b == 0 else through * decay
        msg_ref[0:state_size, lanes] = running.astype(jnp.bfloat16)
        high = through.astype(jnp.bfloat16)
        low = through - high.astype(jnp.float32)
        both = jnp.concatenate(
            [
                jnp.broadcast_to(high.astype(jnp.float32), (8, size)),
                jnp.broadcast_to(low, (8, size)),
            ]
        )
        msg_ref[state_size : state_size + EXTRA, lanes] = both.astype(jnp.bfloat16)
        return unused

    lax.fori_loop(0, width // size, group, 0)


def mix_kernel(
    head_size,
    mixed_ref, bc_ref, cum_ref, cum_t_ref, step_t_ref, ids_col_ref, ids_row_ref, skip_ref,
    out_ref,
    scores,
):
    width = mixed_ref.shape[1]
    size = group_lanes(width)
    per_group = size // head_size
    state_size = bc_ref.shape[1] // 2
    half = SPAN // 2
    row_id = lax.broadcasted_iota(jnp.int32, (SPAN, SPAN), 0)
    col_id = lax.broadcasted_iota(jnp.int32, (SPAN, SPAN), 1)
    raw = lax.dot_general(
        bc_ref[:, state_size:], bc_ref[:, :state_size], (((1,), (1,)), ((), ())),
        preferred_element_type=jnp.float32,
    )
    same = (ids_col_ref[...] == ids_row_ref[...]) & (col_id <= row_id)
    scores[...] = jnp.where(same, raw, 0.0)

    def group(c, unused):
        lanes = pl.ds(pl.multiple_of(c * size, size), size)
        turn = lax.rem(HEADS_PAD - c * per_group, HEADS_PAD)
        cum_t = pltpu.roll(cum_t_ref[...], turn, 1)
        steps = spread_heads(pltpu.roll(step_t_ref[...], turn, 1), head_size, size)
        x = mixed_ref[:, lanes].astype(jnp.float32)
        stepped = (x * steps).astype(jnp.bfloat16)
        tops, bottoms = [], []
        for k in range(per_group):
            own = slice(k * head_size, (k + 1) * head_size)
            column = cum_t[:, k : k + 1]
            row = cum_ref[pl.ds(c * per_group + k, 1), :]
            top = scores[:half, :half] * jnp.exp(jnp.minimum(column[:half] - row[:, :half], 0.0))
            bottom = scores[half:, :] * jnp.exp(jnp.minimum(column[half:] - row, 0.0))
            tops.append(
                jnp.dot(
                    top.astype(jnp.bfloat16), stepped[:half, own],
                    preferred_element_type=jnp.float32,
                )
            )
            bottoms.append(
                jnp.dot(
                    bottom.astype(jnp.bfloat16), stepped[:, own],
                    preferred_element_type=jnp.float32,
                )
            )
        skip = skip_ref[:, lanes]
        out_ref[:half, lanes] = jnp.concatenate(tops, axis=1) + skip * x[:half]
        out_ref[half:, lanes] = jnp.concatenate(bottoms, axis=1) + skip * x[half:]
        return unused

    lax.fori_loop(0, width // size, group, 0)


def gate_kernel(
    head_size,
    state_ref, bc_ref, gain_t_ref, part_ref, z_ref, norm_ref,
    out_ref, squares_ref,
):
    width = part_ref.shape[1]
    size = group_lanes(width)
    per_group = size // head_size
    state_size = bc_ref.shape[1] // 2
    c_vals = bc_ref[:, state_size:]

    def group(c, squares):
        lanes = pl.ds(pl.multiple_of(c * size, size), size)
        turn = lax.rem(HEADS_PAD - c * per_group, HEADS_PAD)
        gain = spread_heads(pltpu.roll(gain_t_ref[...], turn, 1), head_size, size)
        reached = jnp.dot(c_vals, state_ref[:, lanes], preferred_element_type=jnp.float32)
        y = (part_ref[:, lanes] + gain * reached).astype(jnp.bfloat16).astype(jnp.float32)
        gated = y * silu(z_ref[:, lanes].astype(jnp.float32))
        out_ref[:, lanes] = (gated * norm_ref[:, lanes]).astype(jnp.bfloat16)
        square = gated * gated
        for tile in range(size // 128):
            squares = squares + square[:, tile * 128 : (tile + 1) * 128]
        return squares

    squares_ref[...] = lax.fori_loop(
        0, width // size, group, jnp.zeros((SPAN, 128), jnp.float32)
    )


def call(kernel, out_shape, scratch, flops, moved, *operands):
    return pl.pallas_call(
        kernel,
        out_shape=out_shape,
        in_specs=[pl.BlockSpec(memory_space=pltpu.VMEM)] * len(operands),
        out_specs=jax.tree.map(lambda _: pl.BlockSpec(memory_space=pltpu.VMEM), out_shape),
        scratch_shapes=scratch,
        compiler_params=pltpu.CompilerParams(vmem_limit_bytes=VMEM_BYTES),
        cost_estimate=pl.CostEstimate(flops=flops, bytes_accessed=moved, transcendentals=0),
    )(*operands)


def split_message(message):
    state_size = message.shape[0] - EXTRA
    wide = message.astype(jnp.float32)
    return wide[:state_size], wide[state_size : state_size + 1] + wide[state_size + 8 : state_size + 9]


def merge(near, far):
    near_state, near_decay = near
    far_state, far_decay = far
    return near_state + near_decay * far_state, near_decay * far_decay


def pack_message(pair):
    state, decay = pair
    width = state.shape[1]
    high = decay.astype(jnp.bfloat16)
    low = (decay - high.astype(jnp.float32)).astype(jnp.bfloat16)
    return jnp.concatenate(
        [
            state.astype(jnp.bfloat16),
            jnp.broadcast_to(high, (8, width)),
            jnp.broadcast_to(low, (8, width)),
        ]
    )


def pass_state(message):
    count = lax.axis_size("seq")
    odd = (lax.axis_index("seq") % 2) == 1
    other = lax.ppermute(message, "seq", [(i, i ^ 1) for i in range(count)])
    first = split_message(jnp.where(odd, other, message))
    second = split_message(jnp.where(odd, message, other))
    entering = shifted(pack_message(merge(second, first)), "seq", 2)
    reach = 1
    while reach < count // 4:
        farther = shifted(entering, "seq", 2 * reach)
        joined = merge(split_message(entering), split_message(farther))
        reach *= 2
        if reach < count // 4:
            entering = pack_message(joined)
        else:
            entering = joined
    if reach == 1:
        entering = split_message(entering)
    alone = split_message(other)
    return jnp.where(odd, merge(alone, entering)[0], entering[0])


def local(
    x_stream,
    bc_stream,
    z_gate,
    dt_stream,
    doc_ids,
    conv_x,
    conv_bc,
    a_log,
    dt_bias,
    d_skip,
    norm_gain,
    w_out,
):
    rows, width = x_stream.shape
    heads = dt_stream.shape[0]
    head_size = width // heads
    bc_width = bc_stream.shape[1]
    state_size = bc_width // 2
    taps = conv_x.shape[0]
    blocks = rows // SPAN
    edge = rows - taps + 1
    f32, bf16 = jnp.float32, jnp.bfloat16
    own_ids = doc_ids.astype(f32)
    tail_ids = jnp.broadcast_to(own_ids[edge:].astype(bf16)[:, None], (taps - 1, 128))
    rim = shifted(
        jnp.concatenate([x_stream[edge:], bc_stream[edge:], tail_ids], axis=1), "seq", 1
    )
    step = jax.nn.softplus(dt_stream.astype(f32) + dt_bias[:, None])
    rate = -jnp.exp(a_log)[:, None] * step
    step = jnp.pad(step, ((0, HEADS_PAD - heads), (0, 0)))
    rate = jnp.pad(rate, ((0, HEADS_PAD - heads), (0, 0)))
    rim_wide = jnp.pad(rim.astype(f32), ((8 - taps + 1, 0), (0, 0)))
    rim_ids = jnp.where(lax.axis_index("seq") == 0, -1.0, rim[:, width + bc_width].astype(f32))
    ext_ids = jnp.concatenate([rim_ids, own_ids])
    block_ids = own_ids.reshape(blocks, SPAN)
    prior = jnp.concatenate([ext_ids[taps - 2][None], own_ids[SPAN - 1 :: SPAN][: blocks - 1]])
    columns = [(ext_ids[taps - 1 - k : taps - 1 - k + rows] == own_ids) for k in range(1, taps)]
    columns.append((block_ids == prior[:, None]).reshape(rows))
    columns.append((block_ids == block_ids[:, -1:]).reshape(rows))
    flags = jnp.stack([c.astype(f32) for c in columns], axis=1)

    shape = jax.ShapeDtypeStruct
    mixed, mixed_bc, cum, cum_t, step_t, gain_t, fresh, decay, message = call(
        functools.partial(states_kernel, head_size),
        (
            shape((rows, width), bf16),
            shape((rows, bc_width), bf16),
            shape((HEADS_PAD, rows), f32),
            shape((rows, HEADS_PAD), f32),
            shape((rows, HEADS_PAD), f32),
            shape((rows, HEADS_PAD), f32),
            shape((blocks, state_size, width), f32),
            shape((blocks, 8, width), f32),
            shape((state_size + EXTRA, width), bf16),
        ),
        [
            pltpu.VMEM((rows + 8, max(bc_width, group_lanes(width))), f32),
            pltpu.VMEM((rows, HEADS_PAD), f32),
            pltpu.VMEM((state_size, rows), bf16),
        ],
        2 * rows * state_size * width,
        8 * rows * width,
        x_stream, rim_wide[:, :width], bc_stream, rim_wide[:, width : width + bc_width], step, rate,
        flags, conv_x.astype(f32), conv_bc.astype(f32),
    )
    skip_row = jnp.repeat(d_skip, head_size)[None, :]
    parts = []
    for b in range(blocks):
        span = slice(b * SPAN, (b + 1) * SPAN)
        parts.append(
            call(
                functools.partial(mix_kernel, head_size),
                shape((SPAN, width), f32),
                [pltpu.VMEM((SPAN, SPAN), f32)],
                2 * SPAN * SPAN * width * 16,
                8 * SPAN * width,
                mixed[span], mixed_bc[span], cum[:, span], cum_t[span], step_t[span],
                own_ids[span][:, None], own_ids[span][None, :], skip_row,
            )
        )
    state = pass_state(message)

    members = lax.axis_size("tensor")
    member = lax.axis_index("tensor")
    out_width = w_out.shape[1] // members
    pieces = []
    for b in range(blocks):
        span = slice(b * SPAN, (b + 1) * SPAN)
        scaled, squares = call(
            functools.partial(gate_kernel, head_size),
            (shape((SPAN, width), bf16), shape((SPAN, 128), f32)),
            [],
            2 * SPAN * state_size * width,
            12 * SPAN * width,
            state.astype(bf16), mixed_bc[span], gain_t[span], parts[b], z_gate[span],
            norm_gain[None, :],
        )
        if b + 1 < blocks:
            state = decay[b, 0:1] * state + fresh[b]
        product = jnp.dot(scaled, w_out, preferred_element_type=f32).astype(bf16)
        total = lax.dynamic_slice_in_dim(product, member * out_width, out_width, 1).astype(f32)
        square = jnp.sum(squares, axis=1, keepdims=True)
        high = square.astype(bf16)
        low = (square - high.astype(f32)).astype(bf16)
        lane = lax.broadcasted_iota(jnp.int32, (SPAN, 128), 1)
        aside = jnp.where(lane == 0, high, jnp.where(lane == 1, low, jnp.zeros_like(low)))
        for distance in range(1, members):
            target = (member + distance) % members
            block = lax.dynamic_slice_in_dim(product, target * out_width, out_width, 1)
            route = [(i, (i + distance) % members) for i in range(members)]
            got = lax.ppermute(jnp.concatenate([block, aside], axis=1), "tensor", route)
            total = total + got[:, :out_width].astype(f32)
            square = square + jnp.sum(got[:, out_width : out_width + 2].astype(f32), axis=1, keepdims=True)
        inv_norm = lax.rsqrt(square / (width * members) + 1e-05)
        pieces.append((total * inv_norm).astype(bf16))
    return jnp.concatenate(pieces)


def solution(mesh):
    return jax.shard_map(
        local,
        mesh=mesh,
        in_specs=(
            P(("dp", "seq"), "tensor"),
            P(("dp", "seq"), None),
            P(("dp", "seq"), "tensor"),
            P("tensor", ("dp", "seq")),
            P(("dp", "seq")),
            P(None, "tensor"),
            P(),
            P("tensor"),
            P("tensor"),
            P("tensor"),
            P("tensor"),
            P("tensor", None),
        ),
        out_specs=P(("dp", "seq"), "tensor"),
        check_vma=False,
    )
```

```python
import functools

import jax
import jax.numpy as jnp
from jax import lax
from jax.experimental import pallas as pl
from jax.experimental.pallas import tpu as pltpu
from jax.sharding import PartitionSpec as P

SPAN = 256
HEADS_PAD = 128
EXTRA = 16
VMEM_BYTES = 48 * 1024 * 1024


def shifted(block, axis, distance):
    count = lax.axis_size(axis)
    return lax.ppermute(block, axis, [(i, i + distance) for i in range(count - distance)])


def group_lanes(width):
    return 256 if width % 256 == 0 else 128


def silu(v):
    return v / (1.0 + jnp.exp(-v))


def spread_heads(columns, width, lanes):
    rows = columns.shape[0]
    lane = lax.broadcasted_iota(jnp.int32, (rows, 128), 1)
    per_tile = 128 // width
    tiles = []
    for tile in range(lanes // 128):
        value = jnp.broadcast_to(columns[:, tile * per_tile : tile * per_tile + 1], (rows, 128))
        for k in range(1, per_tile):
            head = tile * per_tile + k
            value = jnp.where(
                lane >= k * width, jnp.broadcast_to(columns[:, head : head + 1], (rows, 128)), value
            )
        tiles.append(value)
    return jnp.concatenate(tiles, axis=1)


def conv_taps(ext, weights, keeps, rows):
    wide = weights.shape[1]
    total = weights[0:1] * ext[pl.ds(8, rows), :wide]
    for k in range(1, weights.shape[0]):
        total = total + jnp.where(keeps[k - 1][:, :wide], weights[k : k + 1] * ext[pl.ds(8 - k, rows), :wide], 0.0)
    return silu(total)


def states_kernel(
    head_size,
    x_ref, rim_x_ref, bc_ref, rim_bc_ref, step_ref, rate_ref, flags_ref, conv_x_ref, conv_bc_ref,
    mixed_ref, bc_out_ref, cum_ref, cum_t_ref, step_t_ref, gain_t_ref, fresh_ref, decay_ref, msg_ref,
    ext, tail_t, b_t,
):
    rows, width = x_ref.shape
    blocks = rows // SPAN
    size = group_lanes(width)
    per_group = size // head_size
    state_size = bc_ref.shape[1] // 2
    flags = flags_ref[...]
    taps = conv_x_ref.shape[0]
    keeps = [
        jnp.broadcast_to(flags[:, k : k + 1], (rows, ext.shape[1])) > 0.5 for k in range(taps - 1)
    ]
    carried = jnp.broadcast_to(flags[:, 3:4], (rows, HEADS_PAD)) > 0.5
    in_tail = jnp.broadcast_to(flags[:, 4:5], (rows, HEADS_PAD)) > 0.5

    ext[0:8, :] = rim_bc_ref[...]
    ext[8 : 8 + rows, :] = bc_ref[...].astype(jnp.float32)
    mixed_bc = conv_taps(ext, conv_bc_ref[...], keeps, rows)
    bc_out_ref[...] = mixed_bc.astype(jnp.bfloat16)
    row_id = lax.broadcasted_iota(jnp.int32, (SPAN, SPAN), 0)
    col_id = lax.broadcasted_iota(jnp.int32, (SPAN, SPAN), 1)
    upper = (row_id <= col_id).astype(jnp.float32)
    for b in range(blocks):
        span = slice(b * SPAN, (b + 1) * SPAN)
        b_t[:, span] = mixed_bc[span, :state_size].T.astype(jnp.bfloat16)
        cum = jnp.dot(
            rate_ref[:, span], upper,
            precision=lax.Precision.HIGHEST, preferred_element_type=jnp.float32,
        )
        cum_ref[:, span] = cum
        cum_t = cum.T
        step_t = step_ref[:, span].T
        cum_t_ref[span, :] = cum_t
        step_t_ref[span, :] = step_t
        gain_t_ref[span, :] = jnp.where(carried[span], jnp.exp(cum_t), 0.0)
        tail_t[span, :] = jnp.where(
            in_tail[span], jnp.exp(cum_t[SPAN - 1 : SPAN] - cum_t), 0.0
        ) * step_t

    def group(c, unused):
        lanes = pl.ds(pl.multiple_of(c * size, size), size)
        turn = lax.rem(HEADS_PAD - c * per_group, HEADS_PAD)
        ext[0:8, :size] = rim_x_ref[:, lanes]
        ext[8 : 8 + rows, :size] = x_ref[:, lanes].astype(jnp.float32)
        mixed = conv_taps(ext, conv_x_ref[:, lanes], keeps, rows).astype(jnp.bfloat16)
        mixed_ref[:, lanes] = mixed
        weight = spread_heads(pltpu.roll(tail_t[...], turn, 1), head_size, size)
        weighted = (mixed.astype(jnp.float32) * weight).astype(jnp.bfloat16)
        running = None
        through = None
        for b in range(blocks):
            span = slice(b * SPAN, (b + 1) * SPAN)
            fresh = jnp.dot(b_t[:, span], weighted[span], preferred_element_type=jnp.float32)
            ends = gain_t_ref[(b + 1) * SPAN - 8 : (b + 1) * SPAN, :]
            decay = spread_heads(pltpu.roll(ends, turn, 1), head_size, size)[7:8]
            fresh_ref[b, :, lanes] = fresh
            decay_ref[b, :, lanes] = jnp.broadcast_to(decay, (8, size))
            running = fresh if b == 0 else decay * running + fresh
            through = decay if b == 0 else through * decay
        msg_ref[0:state_size, lanes] = running.astype(jnp.bfloat16)
        high = through.astype(jnp.bfloat16)
        low = through - high.astype(jnp.float32)
        both = jnp.concatenate(
            [
                jnp.broadcast_to(high.astype(jnp.float32), (8, size)),
                jnp.broadcast_to(low, (8, size)),
            ]
        )
        msg_ref[state_size : state_size + EXTRA, lanes] = both.astype(jnp.bfloat16)
        return unused

    lax.fori_loop(0, width // size, group, 0)


def mix_kernel(
    head_size,
    mixed_ref, bc_ref, cum_ref, cum_t_ref, step_t_ref, ids_col_ref, ids_row_ref, skip_ref,
    out_ref,
    scores,
):
    width = mixed_ref.shape[1]
    size = group_lanes(width)
    per_group = size // head_size
    state_size = bc_ref.shape[1] // 2
    half = SPAN // 2
    row_id = lax.broadcasted_iota(jnp.int32, (SPAN, SPAN), 0)
    col_id = lax.broadcasted_iota(jnp.int32, (SPAN, SPAN), 1)
    raw = lax.dot_general(
        bc_ref[:, state_size:], bc_ref[:, :state_size], (((1,), (1,)), ((), ())),
        preferred_element_type=jnp.float32,
    )
    same = (ids_col_ref[...] == ids_row_ref[...]) & (col_id <= row_id)
    scores[...] = jnp.where(same, raw, 0.0)

    def group(c, unused):
        lanes = pl.ds(pl.multiple_of(c * size, size), size)
        turn = lax.rem(HEADS_PAD - c * per_group, HEADS_PAD)
        cum_t = pltpu.roll(cum_t_ref[...], turn, 1)
        steps = spread_heads(pltpu.roll(step_t_ref[...], turn, 1), head_size, size)
        x = mixed_ref[:, lanes].astype(jnp.float32)
        stepped = (x * steps).astype(jnp.bfloat16)
        tops, bottoms = [], []
        for k in range(per_group):
            own = slice(k * head_size, (k + 1) * head_size)
            column = cum_t[:, k : k + 1]
            row = cum_ref[pl.ds(c * per_group + k, 1), :]
            top = scores[:half, :half] * jnp.exp(jnp.minimum(column[:half] - row[:, :half], 0.0))
            bottom = scores[half:, :] * jnp.exp(jnp.minimum(column[half:] - row, 0.0))
            tops.append(
                jnp.dot(
                    top.astype(jnp.bfloat16), stepped[:half, own],
                    preferred_element_type=jnp.float32,
                )
            )
            bottoms.append(
                jnp.dot(
                    bottom.astype(jnp.bfloat16), stepped[:, own],
                    preferred_element_type=jnp.float32,
                )
            )
        skip = skip_ref[:, lanes]
        out_ref[:half, lanes] = jnp.concatenate(tops, axis=1) + skip * x[:half]
        out_ref[half:, lanes] = jnp.concatenate(bottoms, axis=1) + skip * x[half:]
        return unused

    lax.fori_loop(0, width // size, group, 0)


def gate_kernel(
    head_size,
    state_ref, bc_ref, gain_t_ref, part_ref, z_ref, norm_ref,
    out_ref, squares_ref,
):
    width = part_ref.shape[1]
    size = group_lanes(width)
    per_group = size // head_size
    state_size = bc_ref.shape[1] // 2
    c_vals = bc_ref[:, state_size:]

    def group(c, squares):
        lanes = pl.ds(pl.multiple_of(c * size, size), size)
        turn = lax.rem(HEADS_PAD - c * per_group, HEADS_PAD)
        gain = spread_heads(pltpu.roll(gain_t_ref[...], turn, 1), head_size, size)
        reached = jnp.dot(c_vals, state_ref[:, lanes], preferred_element_type=jnp.float32)
        y = (part_ref[:, lanes] + gain * reached).astype(jnp.bfloat16).astype(jnp.float32)
        gated = y * silu(z_ref[:, lanes].astype(jnp.float32))
        out_ref[:, lanes] = (gated * norm_ref[:, lanes]).astype(jnp.bfloat16)
        square = gated * gated
        for tile in range(size // 128):
            squares = squares + square[:, tile * 128 : (tile + 1) * 128]
        return squares

    squares_ref[...] = lax.fori_loop(
        0, width // size, group, jnp.zeros((SPAN, 128), jnp.float32)
    )


def tail_kernel(head_size, chunk, blocks, *refs):
    state_ref, fresh_ref, decay_ref, bc_ref, gain_t_ref, z_ref, norm_ref, w_ref = refs[:8]
    part_refs = refs[8 : 8 + blocks]
    out_ref = refs[8 + blocks]
    (
        w_far, w_near, scaled, state, sums, sends, gots, row_sends, row_gots,
        w_sems, send_sems, got_sems, row_send_sems, row_got_sems,
    ) = refs[9 + blocks :]
    rows, width = z_ref.shape
    out_width = out_ref.shape[1]
    count = rows // chunk
    per_block = SPAN // chunk
    size = group_lanes(width)
    per_group = size // head_size
    state_size = bc_ref.shape[1] // 2
    me = lax.axis_index("tensor")
    peer = 1 - me
    barrier = pltpu.get_barrier_semaphore()
    pl.semaphore_signal(
        barrier, inc=1, device_id={"tensor": peer}, device_id_type=pl.DeviceIdType.MESH
    )
    loads = [
        pltpu.make_async_copy(
            w_ref.at[:, pl.ds(pl.multiple_of(who * out_width, 128), out_width)],
            place,
            w_sems.at[k],
        )
        for k, (who, place) in enumerate(((peer, w_far), (me, w_near)))
    ]
    for load in loads:
        load.start()
    tile = 256 if out_width % 256 == 0 else 128

    def product(q, weights, store):
        def columns(j, unused):
            lanes = pl.ds(pl.multiple_of(j * tile, tile), tile)
            store(
                lanes,
                jnp.dot(
                    scaled[q * chunk : (q + 1) * chunk, :], weights[:, lanes],
                    preferred_element_type=jnp.float32,
                ).astype(jnp.bfloat16),
            )
            return unused

        lax.fori_loop(0, out_width // tile, columns, 0)

    copies = []
    for q in range(count):
        b, within = q // per_block, q % per_block
        here = slice(q * chunk, (q + 1) * chunk)
        inner = slice(within * chunk, (within + 1) * chunk)

        def group(c, squares):
            lanes = pl.ds(pl.multiple_of(c * size, size), size)
            turn = lax.rem(HEADS_PAD - c * per_group, HEADS_PAD)
            if q == 0:
                state[:, lanes] = state_ref[:, lanes].astype(jnp.bfloat16)
            elif within == 0:
                state[:, lanes] = (
                    decay_ref[b - 1, 0:1, lanes] * state[:, lanes].astype(jnp.float32)
                    + fresh_ref[b - 1, :, lanes]
                ).astype(jnp.bfloat16)
            gain = spread_heads(pltpu.roll(gain_t_ref[here, :], turn, 1), head_size, size)
            reached = jnp.dot(
                bc_ref[here, state_size:], state[:, lanes], preferred_element_type=jnp.float32
            )
            y = part_refs[b][inner, lanes] + gain * reached
            y = y.astype(jnp.bfloat16).astype(jnp.float32)
            gated = y * silu(z_ref[here, lanes].astype(jnp.float32))
            scaled[here, lanes] = (gated * norm_ref[:, lanes]).astype(jnp.bfloat16)
            square = gated * gated
            for k in range(size // 128):
                squares = squares + square[:, k * 128 : (k + 1) * 128]
            return squares

        squares = lax.fori_loop(0, width // size, group, jnp.zeros((chunk, 128), jnp.float32))
        row = jnp.sum(squares.T, axis=0, keepdims=True)
        row_sends[q] = jnp.broadcast_to(row, (8, chunk))
        if q == 0:
            loads[0].wait()

        def put(lanes, value):
            sends[q, :, lanes] = value

        product(q, w_far, put)
        if q == 0:
            pl.semaphore_wait(barrier, 1)
        pair = [
            pltpu.make_async_remote_copy(
                src_ref=source.at[q],
                dst_ref=landing.at[q],
                send_sem=out_sems.at[q],
                recv_sem=in_sems.at[q],
                device_id={"tensor": peer},
                device_id_type=pl.DeviceIdType.MESH,
            )
            for source, landing, out_sems, in_sems in (
                (row_sends, row_gots, row_send_sems, row_got_sems),
                (sends, gots, send_sems, got_sems),
            )
        ]
        for copy in pair:
            copy.start()
        copies.append(pair)

    loads[1].wait()
    for q in range(count):
        here = slice(q * chunk, (q + 1) * chunk)

        def keep(lanes, value):
            sums[:, lanes] = value

        product(q, w_near, keep)
        for copy in copies[q]:
            copy.wait_recv()
        row = row_sends[q, 0:1, :] + row_gots[q, 0:1, :]
        inv_row = lax.rsqrt(row / (2 * width) + 1e-05)
        inv = jnp.broadcast_to(inv_row, (128, chunk)).T
        for j in range(out_width // 128):
            lanes = slice(j * 128, (j + 1) * 128)
            total = sums[:, lanes].astype(jnp.float32) + gots[q, :, lanes].astype(jnp.float32)
            out_ref[here, lanes] = (total * inv).astype(jnp.bfloat16)
    for pair in copies:
        for copy in pair:
            copy.wait_send()


def call(kernel, out_shape, scratch, flops, moved, *operands):
    return pl.pallas_call(
        kernel,
        out_shape=out_shape,
        in_specs=[pl.BlockSpec(memory_space=pltpu.VMEM)] * len(operands),
        out_specs=jax.tree.map(lambda _: pl.BlockSpec(memory_space=pltpu.VMEM), out_shape),
        scratch_shapes=scratch,
        compiler_params=pltpu.CompilerParams(vmem_limit_bytes=VMEM_BYTES),
        cost_estimate=pl.CostEstimate(flops=flops, bytes_accessed=moved, transcendentals=0),
    )(*operands)


def split_message(message):
    state_size = message.shape[0] - EXTRA
    wide = message.astype(jnp.float32)
    return wide[:state_size], wide[state_size : state_size + 1] + wide[state_size + 8 : state_size + 9]


def merge(near, far):
    near_state, near_decay = near
    far_state, far_decay = far
    return near_state + near_decay * far_state, near_decay * far_decay


def pack_message(pair):
    state, decay = pair
    width = state.shape[1]
    high = decay.astype(jnp.bfloat16)
    low = (decay - high.astype(jnp.float32)).astype(jnp.bfloat16)
    return jnp.concatenate(
        [
            state.astype(jnp.bfloat16),
            jnp.broadcast_to(high, (8, width)),
            jnp.broadcast_to(low, (8, width)),
        ]
    )


def pass_state(message):
    count = lax.axis_size("seq")
    odd = (lax.axis_index("seq") % 2) == 1
    other = lax.ppermute(message, "seq", [(i, i ^ 1) for i in range(count)])
    first = split_message(jnp.where(odd, other, message))
    second = split_message(jnp.where(odd, message, other))
    entering = shifted(pack_message(merge(second, first)), "seq", 2)
    reach = 1
    while reach < count // 4:
        farther = shifted(entering, "seq", 2 * reach)
        joined = merge(split_message(entering), split_message(farther))
        reach *= 2
        if reach < count // 4:
            entering = pack_message(joined)
        else:
            entering = joined
    if reach == 1:
        entering = split_message(entering)
    alone = split_message(other)
    return jnp.where(odd, merge(alone, entering)[0], entering[0])


def local(
    x_stream,
    bc_stream,
    z_gate,
    dt_stream,
    doc_ids,
    conv_x,
    conv_bc,
    a_log,
    dt_bias,
    d_skip,
    norm_gain,
    w_out,
):
    rows, width = x_stream.shape
    heads = dt_stream.shape[0]
    head_size = width // heads
    bc_width = bc_stream.shape[1]
    state_size = bc_width // 2
    taps = conv_x.shape[0]
    blocks = rows // SPAN
    edge = rows - taps + 1
    f32, bf16 = jnp.float32, jnp.bfloat16
    own_ids = doc_ids.astype(f32)
    tail_ids = jnp.broadcast_to(own_ids[edge:].astype(bf16)[:, None], (taps - 1, 128))
    rim = shifted(
        jnp.concatenate([x_stream[edge:], bc_stream[edge:], tail_ids], axis=1), "seq", 1
    )
    step = jax.nn.softplus(dt_stream.astype(f32) + dt_bias[:, None])
    rate = -jnp.exp(a_log)[:, None] * step
    step = jnp.pad(step, ((0, HEADS_PAD - heads), (0, 0)))
    rate = jnp.pad(rate, ((0, HEADS_PAD - heads), (0, 0)))
    rim_wide = jnp.pad(rim.astype(f32), ((8 - taps + 1, 0), (0, 0)))
    rim_ids = jnp.where(lax.axis_index("seq") == 0, -1.0, rim[:, width + bc_width].astype(f32))
    ext_ids = jnp.concatenate([rim_ids, own_ids])
    block_ids = own_ids.reshape(blocks, SPAN)
    prior = jnp.concatenate([ext_ids[taps - 2][None], own_ids[SPAN - 1 :: SPAN][: blocks - 1]])
    columns = [(ext_ids[taps - 1 - k : taps - 1 - k + rows] == own_ids) for k in range(1, taps)]
    columns.append((block_ids == prior[:, None]).reshape(rows))
    columns.append((block_ids == block_ids[:, -1:]).reshape(rows))
    flags = jnp.stack([c.astype(f32) for c in columns], axis=1)

    shape = jax.ShapeDtypeStruct
    mixed, mixed_bc, cum, cum_t, step_t, gain_t, fresh, decay, message = call(
        functools.partial(states_kernel, head_size),
        (
            shape((rows, width), bf16),
            shape((rows, bc_width), bf16),
            shape((HEADS_PAD, rows), f32),
            shape((rows, HEADS_PAD), f32),
            shape((rows, HEADS_PAD), f32),
            shape((rows, HEADS_PAD), f32),
            shape((blocks, state_size, width), f32),
            shape((blocks, 8, width), f32),
            shape((state_size + EXTRA, width), bf16),
        ),
        [
            pltpu.VMEM((rows + 8, max(bc_width, group_lanes(width))), f32),
            pltpu.VMEM((rows, HEADS_PAD), f32),
            pltpu.VMEM((state_size, rows), bf16),
        ],
        2 * rows * state_size * width,
        8 * rows * width,
        x_stream, rim_wide[:, :width], bc_stream, rim_wide[:, width : width + bc_width], step, rate,
        flags, conv_x.astype(f32), conv_bc.astype(f32),
    )
    skip_row = jnp.repeat(d_skip, head_size)[None, :]
    parts = []
    for b in range(blocks):
        span = slice(b * SPAN, (b + 1) * SPAN)
        parts.append(
            call(
                functools.partial(mix_kernel, head_size),
                shape((SPAN, width), f32),
                [pltpu.VMEM((SPAN, SPAN), f32)],
                2 * SPAN * SPAN * width * 16,
                8 * SPAN * width,
                mixed[span], mixed_bc[span], cum[:, span], cum_t[span], step_t[span],
                own_ids[span][:, None], own_ids[span][None, :], skip_row,
            )
        )
    state = pass_state(message)

    members = lax.axis_size("tensor")
    member = lax.axis_index("tensor")
    out_width = w_out.shape[1] // members
    if members == 2 and out_width % 128 == 0:
        chunk = 128
        count = rows // chunk
        vmem = pl.BlockSpec(memory_space=pltpu.VMEM)
        return pl.pallas_call(
            functools.partial(tail_kernel, head_size, chunk, blocks),
            out_shape=shape((rows, out_width), bf16),
            in_specs=[vmem] * 7 + [pl.BlockSpec(memory_space=pl.ANY)] + [vmem] * blocks,
            out_specs=vmem,
            scratch_shapes=[
                pltpu.VMEM((width, out_width), bf16),
                pltpu.VMEM((width, out_width), bf16),
                pltpu.VMEM((rows, width), bf16),
                pltpu.VMEM((state_size, width), bf16),
                pltpu.VMEM((chunk, out_width), bf16),
                pltpu.VMEM((count, chunk, out_width), bf16),
                pltpu.VMEM((count, chunk, out_width), bf16),
                pltpu.VMEM((count, 8, chunk), f32),
                pltpu.VMEM((count, 8, chunk), f32),
                pltpu.SemaphoreType.DMA((2,)),
                pltpu.SemaphoreType.DMA((count,)),
                pltpu.SemaphoreType.DMA((count,)),
                pltpu.SemaphoreType.DMA((count,)),
                pltpu.SemaphoreType.DMA((count,)),
            ],
            compiler_params=pltpu.CompilerParams(
                collective_id=0, has_side_effects=True, vmem_limit_bytes=VMEM_BYTES
            ),
            cost_estimate=pl.CostEstimate(
                flops=2 * rows * width * w_out.shape[1],
                bytes_accessed=2 * width * w_out.shape[1],
                transcendentals=0,
            ),
        )(state, fresh, decay, mixed_bc, gain_t, z_gate, norm_gain[None, :], w_out, *parts)
    pieces = []
    for b in range(blocks):
        span = slice(b * SPAN, (b + 1) * SPAN)
        scaled, squares = call(
            functools.partial(gate_kernel, head_size),
            (shape((SPAN, width), bf16), shape((SPAN, 128), f32)),
            [],
            2 * SPAN * state_size * width,
            12 * SPAN * width,
            state.astype(bf16), mixed_bc[span], gain_t[span], parts[b], z_gate[span],
            norm_gain[None, :],
        )
        if b + 1 < blocks:
            state = decay[b, 0:1] * state + fresh[b]
        product = jnp.dot(scaled, w_out, preferred_element_type=f32).astype(bf16)
        total = lax.dynamic_slice_in_dim(product, member * out_width, out_width, 1).astype(f32)
        square = jnp.sum(squares, axis=1, keepdims=True)
        high = square.astype(bf16)
        low = (square - high.astype(f32)).astype(bf16)
        lane = lax.broadcasted_iota(jnp.int32, (SPAN, 128), 1)
        aside = jnp.where(lane == 0, high, jnp.where(lane == 1, low, jnp.zeros_like(low)))
        for distance in range(1, members):
            target = (member + distance) % members
            block = lax.dynamic_slice_in_dim(product, target * out_width, out_width, 1)
            route = [(i, (i + distance) % members) for i in range(members)]
            got = lax.ppermute(jnp.concatenate([block, aside], axis=1), "tensor", route)
            total = total + got[:, :out_width].astype(f32)
            square = square + jnp.sum(got[:, out_width : out_width + 2].astype(f32), axis=1, keepdims=True)
        inv_norm = lax.rsqrt(square / (width * members) + 1e-05)
        pieces.append((total * inv_norm).astype(bf16))
    return jnp.concatenate(pieces)


def solution(mesh):
    return jax.shard_map(
        local,
        mesh=mesh,
        in_specs=(
            P(("dp", "seq"), "tensor"),
            P(("dp", "seq"), None),
            P(("dp", "seq"), "tensor"),
            P("tensor", ("dp", "seq")),
            P(("dp", "seq")),
            P(None, "tensor"),
            P(),
            P("tensor"),
            P("tensor"),
            P("tensor"),
            P("tensor"),
            P("tensor", None),
        ),
        out_specs=P(("dp", "seq"), "tensor"),
        check_vma=False,
    )
```

```python
import functools

import jax
import jax.numpy as jnp
from jax import lax
from jax.experimental import pallas as pl
from jax.experimental.pallas import tpu as pltpu
from jax.sharding import PartitionSpec as P

SPAN = 256
HEADS_PAD = 128
EXTRA = 16
VMEM_BYTES = 48 * 1024 * 1024


def shifted(block, axis, distance):
    count = lax.axis_size(axis)
    return lax.ppermute(block, axis, [(i, i + distance) for i in range(count - distance)])


def group_lanes(width):
    return 256 if width % 256 == 0 else 128


def silu(v):
    return v / (1.0 + jnp.exp(-v))


def spread_heads(columns, width, lanes):
    rows = columns.shape[0]
    lane = lax.broadcasted_iota(jnp.int32, (rows, 128), 1)
    per_tile = 128 // width
    tiles = []
    for tile in range(lanes // 128):
        value = jnp.broadcast_to(columns[:, tile * per_tile : tile * per_tile + 1], (rows, 128))
        for k in range(1, per_tile):
            head = tile * per_tile + k
            value = jnp.where(
                lane >= k * width, jnp.broadcast_to(columns[:, head : head + 1], (rows, 128)), value
            )
        tiles.append(value)
    return jnp.concatenate(tiles, axis=1)


def conv_taps(ext, weights, keeps, rows):
    wide = weights.shape[1]
    total = weights[0:1] * ext[pl.ds(8, rows), :wide]
    for k in range(1, weights.shape[0]):
        total = total + jnp.where(keeps[k - 1][:, :wide], weights[k : k + 1] * ext[pl.ds(8 - k, rows), :wide], 0.0)
    return silu(total)


def states_kernel(
    head_size,
    x_ref, rim_x_ref, bc_ref, rim_bc_ref, step_ref, rate_ref, flags_ref, conv_x_ref, conv_bc_ref,
    mixed_ref, bc_out_ref, cum_ref, cum_t_ref, step_t_ref, gain_t_ref, fresh_ref, decay_ref, msg_ref,
    ext, tail_t, b_t,
):
    rows, width = x_ref.shape
    blocks = rows // SPAN
    size = group_lanes(width)
    per_group = size // head_size
    state_size = bc_ref.shape[1] // 2
    flags = flags_ref[...]
    taps = conv_x_ref.shape[0]
    keeps = [
        jnp.broadcast_to(flags[:, k : k + 1], (rows, ext.shape[1])) > 0.5 for k in range(taps - 1)
    ]
    carried = jnp.broadcast_to(flags[:, 3:4], (rows, HEADS_PAD)) > 0.5
    in_tail = jnp.broadcast_to(flags[:, 4:5], (rows, HEADS_PAD)) > 0.5

    ext[0:8, :] = rim_bc_ref[...]
    ext[8 : 8 + rows, :] = bc_ref[...].astype(jnp.float32)
    mixed_bc = conv_taps(ext, conv_bc_ref[...], keeps, rows)
    bc_out_ref[...] = mixed_bc.astype(jnp.bfloat16)
    row_id = lax.broadcasted_iota(jnp.int32, (SPAN, SPAN), 0)
    col_id = lax.broadcasted_iota(jnp.int32, (SPAN, SPAN), 1)
    upper = (row_id <= col_id).astype(jnp.float32)
    for b in range(blocks):
        span = slice(b * SPAN, (b + 1) * SPAN)
        b_t[:, span] = mixed_bc[span, :state_size].T.astype(jnp.bfloat16)
        cum = jnp.dot(
            rate_ref[:, span], upper,
            precision=lax.Precision.HIGHEST, preferred_element_type=jnp.float32,
        )
        cum_ref[:, span] = cum
        cum_t = cum.T
        step_t = step_ref[:, span].T
        cum_t_ref[span, :] = cum_t
        step_t_ref[span, :] = step_t
        gain_t_ref[span, :] = jnp.where(carried[span], jnp.exp(cum_t), 0.0)
        tail_t[span, :] = jnp.where(
            in_tail[span], jnp.exp(cum_t[SPAN - 1 : SPAN] - cum_t), 0.0
        ) * step_t

    def group(c, unused):
        lanes = pl.ds(pl.multiple_of(c * size, size), size)
        turn = lax.rem(HEADS_PAD - c * per_group, HEADS_PAD)
        ext[0:8, :size] = rim_x_ref[:, lanes]
        ext[8 : 8 + rows, :size] = x_ref[:, lanes].astype(jnp.float32)
        mixed = conv_taps(ext, conv_x_ref[:, lanes], keeps, rows).astype(jnp.bfloat16)
        mixed_ref[:, lanes] = mixed
        weight = spread_heads(pltpu.roll(tail_t[...], turn, 1), head_size, size)
        weighted = (mixed.astype(jnp.float32) * weight).astype(jnp.bfloat16)
        running = None
        through = None
        for b in range(blocks):
            span = slice(b * SPAN, (b + 1) * SPAN)
            fresh = jnp.dot(b_t[:, span], weighted[span], preferred_element_type=jnp.float32)
            ends = gain_t_ref[(b + 1) * SPAN - 8 : (b + 1) * SPAN, :]
            decay = spread_heads(pltpu.roll(ends, turn, 1), head_size, size)[7:8]
            fresh_ref[b, :, lanes] = fresh
            decay_ref[b, :, lanes] = jnp.broadcast_to(decay, (8, size))
            running = fresh if b == 0 else decay * running + fresh
            through = decay if b == 0 else through * decay
        msg_ref[0:state_size, lanes] = running.astype(jnp.bfloat16)
        high = through.astype(jnp.bfloat16)
        low = through - high.astype(jnp.float32)
        both = jnp.concatenate(
            [
                jnp.broadcast_to(high.astype(jnp.float32), (8, size)),
                jnp.broadcast_to(low, (8, size)),
            ]
        )
        msg_ref[state_size : state_size + EXTRA, lanes] = both.astype(jnp.bfloat16)
        return unused

    lax.fori_loop(0, width // size, group, 0)


def mix_kernel(
    head_size,
    mixed_ref, bc_ref, cum_ref, cum_t_ref, step_t_ref, ids_col_ref, ids_row_ref, skip_ref,
    out_ref,
    scores,
):
    width = mixed_ref.shape[1]
    size = group_lanes(width)
    per_group = size // head_size
    state_size = bc_ref.shape[1] // 2
    half = SPAN // 2
    row_id = lax.broadcasted_iota(jnp.int32, (SPAN, SPAN), 0)
    col_id = lax.broadcasted_iota(jnp.int32, (SPAN, SPAN), 1)
    raw = lax.dot_general(
        bc_ref[:, state_size:], bc_ref[:, :state_size], (((1,), (1,)), ((), ())),
        preferred_element_type=jnp.float32,
    )
    same = (ids_col_ref[...] == ids_row_ref[...]) & (col_id <= row_id)
    scores[...] = jnp.where(same, raw, 0.0)

    def group(c, unused):
        lanes = pl.ds(pl.multiple_of(c * size, size), size)
        turn = lax.rem(HEADS_PAD - c * per_group, HEADS_PAD)
        cum_t = pltpu.roll(cum_t_ref[...], turn, 1)
        steps = spread_heads(pltpu.roll(step_t_ref[...], turn, 1), head_size, size)
        x = mixed_ref[:, lanes].astype(jnp.float32)
        stepped = (x * steps).astype(jnp.bfloat16)
        tops, bottoms = [], []
        for k in range(per_group):
            own = slice(k * head_size, (k + 1) * head_size)
            column = cum_t[:, k : k + 1]
            row = cum_ref[pl.ds(c * per_group + k, 1), :]
            top = scores[:half, :half] * jnp.exp(jnp.minimum(column[:half] - row[:, :half], 0.0))
            bottom = scores[half:, :] * jnp.exp(jnp.minimum(column[half:] - row, 0.0))
            tops.append(
                jnp.dot(
                    top.astype(jnp.bfloat16), stepped[:half, own],
                    preferred_element_type=jnp.float32,
                )
            )
            bottoms.append(
                jnp.dot(
                    bottom.astype(jnp.bfloat16), stepped[:, own],
                    preferred_element_type=jnp.float32,
                )
            )
        skip = skip_ref[:, lanes]
        out_ref[:half, lanes] = jnp.concatenate(tops, axis=1) + skip * x[:half]
        out_ref[half:, lanes] = jnp.concatenate(bottoms, axis=1) + skip * x[half:]
        return unused

    lax.fori_loop(0, width // size, group, 0)


def chain_kernel(
    head_size,
    state_ref, mixed_ref, bc_ref, cum_ref, cum_t_ref, step_t_ref, gain_t_ref, ids_col_ref,
    ids_row_ref, skip_ref,
    part_ref, enter_ref,
    scores, got, whole, near, far, sent, landed, own_decay, got_decay, pair_decay, near_decay,
    decay_sems, got_sems, whole_sems, far_sems, land_sems,
):
    rows, width = mixed_ref.shape
    size = group_lanes(width)
    per_group = size // head_size
    groups = width // size
    pieces = groups // 2
    blocks = rows // SPAN
    state_size = bc_ref.shape[1] // 2
    half = SPAN // 2
    f32, bf16 = jnp.float32, jnp.bfloat16
    count = lax.axis_size("seq")
    me = lax.axis_index("seq")
    parity = lax.rem(me, 2)
    odd = parity == 1
    partner = me + 1 - 2 * parity
    has_up = me < count - 2
    has_down = me >= 2
    has_far = me >= 4
    above = lax.rem(me + 2, count)
    below = lax.rem(me + count - 2, count)
    mesh_type = pl.DeviceIdType.MESH

    barrier = pltpu.get_barrier_semaphore()
    pl.semaphore_signal(barrier, inc=1, device_id={"seq": partner}, device_id_type=mesh_type)

    @pl.when(has_up)
    def greet_above():
        pl.semaphore_signal(barrier, inc=1, device_id={"seq": above}, device_id_type=mesh_type)

    @pl.when(has_down)
    def greet_below():
        pl.semaphore_signal(barrier, inc=1, device_id={"seq": below}, device_id_type=mesh_type)

    decay = gain_t_ref[SPAN - 1 : SPAN, :]
    for b in range(1, blocks):
        decay = decay * gain_t_ref[(b + 1) * SPAN - 1 : (b + 1) * SPAN, :]
    own_decay[...] = jnp.broadcast_to(decay, own_decay.shape)

    @pl.when(jnp.logical_not(has_down))
    def clear_near():
        near[...] = jnp.zeros_like(near)
        near_decay[...] = jnp.zeros_like(near_decay)

    @pl.when(jnp.logical_not(has_far))
    def clear_far():
        far[...] = jnp.zeros_like(far)

    @pl.when(has_up & has_down)
    def meet_three():
        pl.semaphore_wait(barrier, 3)

    @pl.when(jnp.logical_not(has_up & has_down))
    def meet_two():
        pl.semaphore_wait(barrier, 2)

    def lanes_of(which, k):
        return pl.ds(pl.multiple_of((which * pieces + k) * size, size), size)

    def remote(source, landing, send_sem, recv_sem, device):
        return pltpu.make_async_remote_copy(
            src_ref=source, dst_ref=landing, send_sem=send_sem, recv_sem=recv_sem,
            device_id={"seq": device}, device_id_type=mesh_type,
        )

    def decay_copy():
        return remote(own_decay, got_decay, decay_sems.at[0], decay_sems.at[1], partner)

    def pair_decay_copy():
        return remote(pair_decay, near_decay, decay_sems.at[2], decay_sems.at[3], above)

    def state_copy(k):
        return remote(
            state_ref.at[:, lanes_of(1 - parity, k)], got.at[k], got_sems.at[0, k],
            got_sems.at[1, k], partner,
        )

    def whole_copy(k):
        return remote(whole.at[k], near.at[k], whole_sems.at[0, k], whole_sems.at[1, k], above)

    def far_copy(k):
        return remote(near.at[k], far.at[k], far_sems.at[0, k], far_sems.at[1, k], above)

    def land_copy(k):
        return remote(sent.at[k], landed.at[k], land_sems.at[0, k], land_sems.at[1, k], partner)

    decay_copy().start()
    for k in range(pieces):
        state_copy(k).start()

    row_id = lax.broadcasted_iota(jnp.int32, (SPAN, SPAN), 0)
    col_id = lax.broadcasted_iota(jnp.int32, (SPAN, SPAN), 1)
    for b in range(blocks):
        span = slice(b * SPAN, (b + 1) * SPAN)
        raw = lax.dot_general(
            bc_ref[span, state_size:], bc_ref[span, :state_size], (((1,), (1,)), ((), ())),
            preferred_element_type=f32,
        )
        same = (ids_col_ref[span, :] == ids_row_ref[:, span]) & (col_id <= row_id)
        scores[b] = jnp.where(same, raw, 0.0)

    def mix(c, b):
        lanes = pl.ds(pl.multiple_of(c * size, size), size)
        span = pl.ds(b * SPAN, SPAN)
        turn = lax.rem(HEADS_PAD - c * per_group, HEADS_PAD)
        cum_t = pltpu.roll(cum_t_ref[span, :], turn, 1)
        steps = spread_heads(pltpu.roll(step_t_ref[span, :], turn, 1), head_size, size)
        x = mixed_ref[span, lanes].astype(f32)
        stepped = (x * steps).astype(bf16)
        tops, bottoms = [], []
        for k in range(per_group):
            own = slice(k * head_size, (k + 1) * head_size)
            column = cum_t[:, k : k + 1]
            row = cum_ref[pl.ds(c * per_group + k, 1), span]
            top = scores[b, :half, :half] * jnp.exp(
                jnp.minimum(column[:half] - row[:, :half], 0.0)
            )
            bottom = scores[b, half:, :] * jnp.exp(jnp.minimum(column[half:] - row, 0.0))
            tops.append(
                jnp.dot(top.astype(bf16), stepped[:half, own], preferred_element_type=f32)
            )
            bottoms.append(
                jnp.dot(bottom.astype(bf16), stepped[:, own], preferred_element_type=f32)
            )
        both = jnp.concatenate(
            [jnp.concatenate(tops, axis=1), jnp.concatenate(bottoms, axis=1)], axis=0
        )
        part_ref[span, lanes] = both + skip_ref[:, lanes] * x

    def decay_row(ref, k):
        turn = lax.rem(HEADS_PAD - (parity * pieces + k) * per_group, HEADS_PAD)
        turn = lax.rem(turn + HEADS_PAD, HEADS_PAD)
        return spread_heads(pltpu.roll(ref[...], turn, 1), head_size, size)[0:1]

    def first_state(k):
        mine = state_ref[:, lanes_of(parity, k)].astype(f32)
        theirs = got[k].astype(f32)
        return jnp.where(odd, theirs, mine), jnp.where(odd, mine, theirs)

    def step(j, unused):
        @pl.when(j == 0)
        def take_decay():
            decay_copy().wait_recv()
            pair_decay[...] = own_decay[...] * got_decay[...]

            @pl.when(has_up)
            def pass_decay():
                pair_decay_copy().start()

        @pl.when(j < pieces)
        def join():
            state_copy(j).wait_recv()

            @pl.when(has_up)
            def send_whole():
                first, second = first_state(j)
                odd_decay = jnp.where(odd, decay_row(own_decay, j), decay_row(got_decay, j))
                whole[j] = (second + odd_decay * first).astype(bf16)
                whole_copy(j).start()

        @pl.when((j >= 2) & (j < pieces + 2))
        def forward():
            @pl.when(has_down)
            def take_near():
                whole_copy(j - 2).wait_recv()

                @pl.when(has_up)
                def pass_near():
                    far_copy(j - 2).start()

        @pl.when(j >= pieces)
        def close():
            k = j - pieces

            @pl.when((k == 0) & has_down)
            def take_near_decay():
                pair_decay_copy().wait_recv()

            @pl.when(has_far)
            def take_far():
                far_copy(k).wait_recv()

            entering = near[k].astype(f32) + decay_row(near_decay, k) * far[k].astype(f32)
            first, _ = first_state(k)
            even_decay = jnp.where(odd, decay_row(got_decay, k), decay_row(own_decay, k))
            later = first + even_decay * entering
            enter_ref[:, lanes_of(parity, k)] = jnp.where(odd, later, entering).astype(bf16)
            sent[k] = jnp.where(odd, entering, later).astype(bf16)
            land_copy(k).start()

        for b in range(blocks):
            mix(j, b)
        return unused

    lax.fori_loop(0, groups, step, 0)

    decay_copy().wait_send()
    for k in range(pieces):
        land_copy(k).wait_recv()
        enter_ref[:, lanes_of(1 - parity, k)] = landed[k]
    for k in range(pieces):
        state_copy(k).wait_send()
        land_copy(k).wait_send()

    @pl.when(has_up)
    def finish():
        pair_decay_copy().wait_send()
        for k in range(pieces):
            whole_copy(k).wait_send()

    @pl.when(has_up & has_down)
    def finish_far():
        for k in range(pieces):
            far_copy(k).wait_send()


def gate_kernel(
    head_size,
    state_ref, bc_ref, gain_t_ref, part_ref, z_ref, norm_ref,
    out_ref, squares_ref,
):
    width = part_ref.shape[1]
    size = group_lanes(width)
    per_group = size // head_size
    state_size = bc_ref.shape[1] // 2
    c_vals = bc_ref[:, state_size:]

    def group(c, squares):
        lanes = pl.ds(pl.multiple_of(c * size, size), size)
        turn = lax.rem(HEADS_PAD - c * per_group, HEADS_PAD)
        gain = spread_heads(pltpu.roll(gain_t_ref[...], turn, 1), head_size, size)
        reached = jnp.dot(c_vals, state_ref[:, lanes], preferred_element_type=jnp.float32)
        y = (part_ref[:, lanes] + gain * reached).astype(jnp.bfloat16).astype(jnp.float32)
        gated = y * silu(z_ref[:, lanes].astype(jnp.float32))
        out_ref[:, lanes] = (gated * norm_ref[:, lanes]).astype(jnp.bfloat16)
        square = gated * gated
        for tile in range(size // 128):
            squares = squares + square[:, tile * 128 : (tile + 1) * 128]
        return squares

    squares_ref[...] = lax.fori_loop(
        0, width // size, group, jnp.zeros((SPAN, 128), jnp.float32)
    )


def tail_kernel(head_size, chunk, parts, *refs):
    state_ref, fresh_ref, decay_ref, bc_ref, gain_t_ref, z_ref, norm_ref, w_ref = refs[:8]
    part_refs = refs[8 : 8 + parts]
    out_ref = refs[8 + parts]
    (
        w_far, w_near, scaled, state, sums, sends, gots, row_sends, row_gots,
        w_sems, send_sems, got_sems, row_send_sems, row_got_sems,
    ) = refs[9 + parts :]
    rows, width = z_ref.shape
    out_width = out_ref.shape[1]
    count = rows // chunk
    per_block = SPAN // chunk
    size = group_lanes(width)
    per_group = size // head_size
    state_size = bc_ref.shape[1] // 2
    me = lax.axis_index("tensor")
    peer = 1 - me
    barrier = pltpu.get_barrier_semaphore()
    pl.semaphore_signal(
        barrier, inc=1, device_id={"tensor": peer}, device_id_type=pl.DeviceIdType.MESH
    )
    loads = [
        pltpu.make_async_copy(
            w_ref.at[:, pl.ds(pl.multiple_of(who * out_width, 128), out_width)],
            place,
            w_sems.at[k],
        )
        for k, (who, place) in enumerate(((peer, w_far), (me, w_near)))
    ]
    for load in loads:
        load.start()
    tile = 256 if out_width % 256 == 0 else 128

    def product(q, weights, store):
        def columns(j, unused):
            lanes = pl.ds(pl.multiple_of(j * tile, tile), tile)
            store(
                lanes,
                jnp.dot(
                    scaled[q * chunk : (q + 1) * chunk, :], weights[:, lanes],
                    preferred_element_type=jnp.float32,
                ).astype(jnp.bfloat16),
            )
            return unused

        lax.fori_loop(0, out_width // tile, columns, 0)

    copies = []
    for q in range(count):
        b, within = q // per_block, q % per_block
        here = slice(q * chunk, (q + 1) * chunk)
        inner = slice(within * chunk, (within + 1) * chunk)

        def group(c, squares):
            lanes = pl.ds(pl.multiple_of(c * size, size), size)
            turn = lax.rem(HEADS_PAD - c * per_group, HEADS_PAD)
            if q == 0:
                state[:, lanes] = state_ref[:, lanes].astype(jnp.bfloat16)
            elif within == 0:
                state[:, lanes] = (
                    decay_ref[b - 1, 0:1, lanes] * state[:, lanes].astype(jnp.float32)
                    + fresh_ref[b - 1, :, lanes]
                ).astype(jnp.bfloat16)
            gain = spread_heads(pltpu.roll(gain_t_ref[here, :], turn, 1), head_size, size)
            reached = jnp.dot(
                bc_ref[here, state_size:], state[:, lanes], preferred_element_type=jnp.float32
            )
            part = part_refs[0][here, lanes] if parts == 1 else part_refs[b][inner, lanes]
            y = part + gain * reached
            y = y.astype(jnp.bfloat16).astype(jnp.float32)
            gated = y * silu(z_ref[here, lanes].astype(jnp.float32))
            scaled[here, lanes] = (gated * norm_ref[:, lanes]).astype(jnp.bfloat16)
            square = gated * gated
            for k in range(size // 128):
                squares = squares + square[:, k * 128 : (k + 1) * 128]
            return squares

        squares = lax.fori_loop(0, width // size, group, jnp.zeros((chunk, 128), jnp.float32))
        row = jnp.sum(squares.T, axis=0, keepdims=True)
        row_sends[q] = jnp.broadcast_to(row, (8, chunk))
        if q == 0:
            loads[0].wait()

        def put(lanes, value):
            sends[q, :, lanes] = value

        product(q, w_far, put)
        if q == 0:
            pl.semaphore_wait(barrier, 1)
        pair = [
            pltpu.make_async_remote_copy(
                src_ref=source.at[q],
                dst_ref=landing.at[q],
                send_sem=out_sems.at[q],
                recv_sem=in_sems.at[q],
                device_id={"tensor": peer},
                device_id_type=pl.DeviceIdType.MESH,
            )
            for source, landing, out_sems, in_sems in (
                (row_sends, row_gots, row_send_sems, row_got_sems),
                (sends, gots, send_sems, got_sems),
            )
        ]
        for copy in pair:
            copy.start()
        copies.append(pair)

    loads[1].wait()
    for q in range(count):
        here = slice(q * chunk, (q + 1) * chunk)

        def keep(lanes, value):
            sums[:, lanes] = value

        product(q, w_near, keep)
        for copy in copies[q]:
            copy.wait_recv()
        row = row_sends[q, 0:1, :] + row_gots[q, 0:1, :]
        inv_row = lax.rsqrt(row / (2 * width) + 1e-05)
        inv = jnp.broadcast_to(inv_row, (128, chunk)).T
        for j in range(out_width // 128):
            lanes = slice(j * 128, (j + 1) * 128)
            total = sums[:, lanes].astype(jnp.float32) + gots[q, :, lanes].astype(jnp.float32)
            out_ref[here, lanes] = (total * inv).astype(jnp.bfloat16)
    for pair in copies:
        for copy in pair:
            copy.wait_send()


def call(kernel, out_shape, scratch, flops, moved, *operands):
    return pl.pallas_call(
        kernel,
        out_shape=out_shape,
        in_specs=[pl.BlockSpec(memory_space=pltpu.VMEM)] * len(operands),
        out_specs=jax.tree.map(lambda _: pl.BlockSpec(memory_space=pltpu.VMEM), out_shape),
        scratch_shapes=scratch,
        compiler_params=pltpu.CompilerParams(vmem_limit_bytes=VMEM_BYTES),
        cost_estimate=pl.CostEstimate(flops=flops, bytes_accessed=moved, transcendentals=0),
    )(*operands)


def split_message(message):
    state_size = message.shape[0] - EXTRA
    wide = message.astype(jnp.float32)
    return wide[:state_size], wide[state_size : state_size + 1] + wide[state_size + 8 : state_size + 9]


def merge(near, far):
    near_state, near_decay = near
    far_state, far_decay = far
    return near_state + near_decay * far_state, near_decay * far_decay


def pack_message(pair):
    state, decay = pair
    width = state.shape[1]
    high = decay.astype(jnp.bfloat16)
    low = (decay - high.astype(jnp.float32)).astype(jnp.bfloat16)
    return jnp.concatenate(
        [
            state.astype(jnp.bfloat16),
            jnp.broadcast_to(high, (8, width)),
            jnp.broadcast_to(low, (8, width)),
        ]
    )


def pass_state(message):
    count = lax.axis_size("seq")
    odd = (lax.axis_index("seq") % 2) == 1
    other = lax.ppermute(message, "seq", [(i, i ^ 1) for i in range(count)])
    first = split_message(jnp.where(odd, other, message))
    second = split_message(jnp.where(odd, message, other))
    entering = shifted(pack_message(merge(second, first)), "seq", 2)
    reach = 1
    while reach < count // 4:
        farther = shifted(entering, "seq", 2 * reach)
        joined = merge(split_message(entering), split_message(farther))
        reach *= 2
        if reach < count // 4:
            entering = pack_message(joined)
        else:
            entering = joined
    if reach == 1:
        entering = split_message(entering)
    alone = split_message(other)
    return jnp.where(odd, merge(alone, entering)[0], entering[0])


def local(
    x_stream,
    bc_stream,
    z_gate,
    dt_stream,
    doc_ids,
    conv_x,
    conv_bc,
    a_log,
    dt_bias,
    d_skip,
    norm_gain,
    w_out,
):
    rows, width = x_stream.shape
    heads = dt_stream.shape[0]
    head_size = width // heads
    bc_width = bc_stream.shape[1]
    state_size = bc_width // 2
    taps = conv_x.shape[0]
    blocks = rows // SPAN
    edge = rows - taps + 1
    f32, bf16 = jnp.float32, jnp.bfloat16
    own_ids = doc_ids.astype(f32)
    tail_ids = jnp.broadcast_to(own_ids[edge:].astype(bf16)[:, None], (taps - 1, 128))
    rim = shifted(
        jnp.concatenate([x_stream[edge:], bc_stream[edge:], tail_ids], axis=1), "seq", 1
    )
    step = jax.nn.softplus(dt_stream.astype(f32) + dt_bias[:, None])
    rate = -jnp.exp(a_log)[:, None] * step
    step = jnp.pad(step, ((0, HEADS_PAD - heads), (0, 0)))
    rate = jnp.pad(rate, ((0, HEADS_PAD - heads), (0, 0)))
    rim_wide = jnp.pad(rim.astype(f32), ((8 - taps + 1, 0), (0, 0)))
    rim_ids = jnp.where(lax.axis_index("seq") == 0, -1.0, rim[:, width + bc_width].astype(f32))
    ext_ids = jnp.concatenate([rim_ids, own_ids])
    block_ids = own_ids.reshape(blocks, SPAN)
    prior = jnp.concatenate([ext_ids[taps - 2][None], own_ids[SPAN - 1 :: SPAN][: blocks - 1]])
    columns = [(ext_ids[taps - 1 - k : taps - 1 - k + rows] == own_ids) for k in range(1, taps)]
    columns.append((block_ids == prior[:, None]).reshape(rows))
    columns.append((block_ids == block_ids[:, -1:]).reshape(rows))
    flags = jnp.stack([c.astype(f32) for c in columns], axis=1)

    shape = jax.ShapeDtypeStruct
    mixed, mixed_bc, cum, cum_t, step_t, gain_t, fresh, decay, message = call(
        functools.partial(states_kernel, head_size),
        (
            shape((rows, width), bf16),
            shape((rows, bc_width), bf16),
            shape((HEADS_PAD, rows), f32),
            shape((rows, HEADS_PAD), f32),
            shape((rows, HEADS_PAD), f32),
            shape((rows, HEADS_PAD), f32),
            shape((blocks, state_size, width), f32),
            shape((blocks, 8, width), f32),
            shape((state_size + EXTRA, width), bf16),
        ),
        [
            pltpu.VMEM((rows + 8, max(bc_width, group_lanes(width))), f32),
            pltpu.VMEM((rows, HEADS_PAD), f32),
            pltpu.VMEM((state_size, rows), bf16),
        ],
        2 * rows * state_size * width,
        8 * rows * width,
        x_stream, rim_wide[:, :width], bc_stream, rim_wide[:, width : width + bc_width], step, rate,
        flags, conv_x.astype(f32), conv_bc.astype(f32),
    )
    skip_row = jnp.repeat(d_skip, head_size)[None, :]
    vmem = pl.BlockSpec(memory_space=pltpu.VMEM)
    pieces = width // 512
    if lax.axis_size("seq") == 8 and width % 512 == 0 and pieces >= 3:
        piece = (pieces, state_size, 256)
        part, state = pl.pallas_call(
            functools.partial(chain_kernel, head_size),
            out_shape=(shape((rows, width), f32), shape((state_size, width), bf16)),
            in_specs=[vmem] * 10,
            out_specs=(vmem, vmem),
            scratch_shapes=[pltpu.VMEM((blocks, SPAN, SPAN), f32)]
            + [pltpu.VMEM(piece, bf16)] * 6
            + [pltpu.VMEM((8, HEADS_PAD), f32)] * 4
            + [pltpu.SemaphoreType.DMA((4,))]
            + [pltpu.SemaphoreType.DMA((2, pieces))] * 4,
            compiler_params=pltpu.CompilerParams(
                collective_id=1, has_side_effects=True, vmem_limit_bytes=VMEM_BYTES
            ),
            cost_estimate=pl.CostEstimate(
                flops=2 * rows * SPAN * width * 16, bytes_accessed=8 * rows * width,
                transcendentals=0,
            ),
        )(
            message[:state_size], mixed, mixed_bc, cum, cum_t, step_t, gain_t,
            own_ids[:, None], own_ids[None, :], skip_row,
        )
        parts = [part]
    else:
        parts = []
        for b in range(blocks):
            span = slice(b * SPAN, (b + 1) * SPAN)
            parts.append(
                call(
                    functools.partial(mix_kernel, head_size),
                    shape((SPAN, width), f32),
                    [pltpu.VMEM((SPAN, SPAN), f32)],
                    2 * SPAN * SPAN * width * 16,
                    8 * SPAN * width,
                    mixed[span], mixed_bc[span], cum[:, span], cum_t[span], step_t[span],
                    own_ids[span][:, None], own_ids[span][None, :], skip_row,
                )
            )
        state = pass_state(message)

    members = lax.axis_size("tensor")
    member = lax.axis_index("tensor")
    out_width = w_out.shape[1] // members
    if members == 2 and out_width % 128 == 0:
        chunk = 128
        count = rows // chunk
        return pl.pallas_call(
            functools.partial(tail_kernel, head_size, chunk, len(parts)),
            out_shape=shape((rows, out_width), bf16),
            in_specs=[vmem] * 7 + [pl.BlockSpec(memory_space=pl.ANY)] + [vmem] * len(parts),
            out_specs=vmem,
            scratch_shapes=[
                pltpu.VMEM((width, out_width), bf16),
                pltpu.VMEM((width, out_width), bf16),
                pltpu.VMEM((rows, width), bf16),
                pltpu.VMEM((state_size, width), bf16),
                pltpu.VMEM((chunk, out_width), bf16),
                pltpu.VMEM((count, chunk, out_width), bf16),
                pltpu.VMEM((count, chunk, out_width), bf16),
                pltpu.VMEM((count, 8, chunk), f32),
                pltpu.VMEM((count, 8, chunk), f32),
                pltpu.SemaphoreType.DMA((2,)),
                pltpu.SemaphoreType.DMA((count,)),
                pltpu.SemaphoreType.DMA((count,)),
                pltpu.SemaphoreType.DMA((count,)),
                pltpu.SemaphoreType.DMA((count,)),
            ],
            compiler_params=pltpu.CompilerParams(
                collective_id=0, has_side_effects=True, vmem_limit_bytes=VMEM_BYTES
            ),
            cost_estimate=pl.CostEstimate(
                flops=2 * rows * width * w_out.shape[1],
                bytes_accessed=2 * width * w_out.shape[1],
                transcendentals=0,
            ),
        )(state, fresh, decay, mixed_bc, gain_t, z_gate, norm_gain[None, :], w_out, *parts)
    if len(parts) != blocks:
        parts = [parts[0][b * SPAN : (b + 1) * SPAN] for b in range(blocks)]
    pieces = []
    for b in range(blocks):
        span = slice(b * SPAN, (b + 1) * SPAN)
        scaled, squares = call(
            functools.partial(gate_kernel, head_size),
            (shape((SPAN, width), bf16), shape((SPAN, 128), f32)),
            [],
            2 * SPAN * state_size * width,
            12 * SPAN * width,
            state.astype(bf16), mixed_bc[span], gain_t[span], parts[b], z_gate[span],
            norm_gain[None, :],
        )
        if b + 1 < blocks:
            state = decay[b, 0:1] * state + fresh[b]
        product = jnp.dot(scaled, w_out, preferred_element_type=f32).astype(bf16)
        total = lax.dynamic_slice_in_dim(product, member * out_width, out_width, 1).astype(f32)
        square = jnp.sum(squares, axis=1, keepdims=True)
        high = square.astype(bf16)
        low = (square - high.astype(f32)).astype(bf16)
        lane = lax.broadcasted_iota(jnp.int32, (SPAN, 128), 1)
        aside = jnp.where(lane == 0, high, jnp.where(lane == 1, low, jnp.zeros_like(low)))
        for distance in range(1, members):
            target = (member + distance) % members
            block = lax.dynamic_slice_in_dim(product, target * out_width, out_width, 1)
            route = [(i, (i + distance) % members) for i in range(members)]
            got = lax.ppermute(jnp.concatenate([block, aside], axis=1), "tensor", route)
            total = total + got[:, :out_width].astype(f32)
            square = square + jnp.sum(got[:, out_width : out_width + 2].astype(f32), axis=1, keepdims=True)
        inv_norm = lax.rsqrt(square / (width * members) + 1e-05)
        pieces.append((total * inv_norm).astype(bf16))
    return jnp.concatenate(pieces)


def solution(mesh):
    return jax.shard_map(
        local,
        mesh=mesh,
        in_specs=(
            P(("dp", "seq"), "tensor"),
            P(("dp", "seq"), None),
            P(("dp", "seq"), "tensor"),
            P("tensor", ("dp", "seq")),
            P(("dp", "seq")),
            P(None, "tensor"),
            P(),
            P("tensor"),
            P("tensor"),
            P("tensor"),
            P("tensor"),
            P("tensor", None),
        ),
        out_specs=P(("dp", "seq"), "tensor"),
        check_vma=False,
    )
```

```python
import functools

import jax
import jax.numpy as jnp
from jax import lax
from jax.experimental import pallas as pl
from jax.experimental.pallas import tpu as pltpu
from jax.sharding import PartitionSpec as P

SPAN = 256
HEADS_PAD = 128
EXTRA = 16
VMEM_BYTES = 48 * 1024 * 1024


def shifted(block, axis, distance):
    count = lax.axis_size(axis)
    return lax.ppermute(block, axis, [(i, i + distance) for i in range(count - distance)])


def group_lanes(width):
    return 256 if width % 256 == 0 else 128


def silu(v):
    return v / (1.0 + jnp.exp(-v))


def spread_heads(columns, width, lanes):
    rows = columns.shape[0]
    lane = lax.broadcasted_iota(jnp.int32, (rows, 128), 1)
    per_tile = 128 // width
    tiles = []
    for tile in range(lanes // 128):
        value = jnp.broadcast_to(columns[:, tile * per_tile : tile * per_tile + 1], (rows, 128))
        for k in range(1, per_tile):
            head = tile * per_tile + k
            value = jnp.where(
                lane >= k * width, jnp.broadcast_to(columns[:, head : head + 1], (rows, 128)), value
            )
        tiles.append(value)
    return jnp.concatenate(tiles, axis=1)


def conv_taps(ext, weights, keeps, rows):
    wide = weights.shape[1]
    total = weights[0:1] * ext[pl.ds(8, rows), :wide]
    for k in range(1, weights.shape[0]):
        total = total + jnp.where(keeps[k - 1][:, :wide], weights[k : k + 1] * ext[pl.ds(8 - k, rows), :wide], 0.0)
    return silu(total)


def states_kernel(
    head_size,
    x_ref, rim_x_ref, bc_ref, rim_bc_ref, step_ref, rate_ref, flags_ref, conv_x_ref, conv_bc_ref,
    mixed_ref, bc_out_ref, cum_ref, cum_t_ref, step_t_ref, gain_t_ref, fresh_ref, decay_ref, msg_ref,
    ext, tail_t, b_t,
):
    rows, width = x_ref.shape
    blocks = rows // SPAN
    size = group_lanes(width)
    per_group = size // head_size
    state_size = bc_ref.shape[1] // 2
    flags = flags_ref[...]
    taps = conv_x_ref.shape[0]
    keeps = [
        jnp.broadcast_to(flags[:, k : k + 1], (rows, ext.shape[1])) > 0.5 for k in range(taps - 1)
    ]
    carried = jnp.broadcast_to(flags[:, 3:4], (rows, HEADS_PAD)) > 0.5
    in_tail = jnp.broadcast_to(flags[:, 4:5], (rows, HEADS_PAD)) > 0.5

    ext[0:8, :] = rim_bc_ref[...]
    ext[8 : 8 + rows, :] = bc_ref[...].astype(jnp.float32)
    mixed_bc = conv_taps(ext, conv_bc_ref[...], keeps, rows)
    bc_out_ref[...] = mixed_bc.astype(jnp.bfloat16)
    row_id = lax.broadcasted_iota(jnp.int32, (SPAN, SPAN), 0)
    col_id = lax.broadcasted_iota(jnp.int32, (SPAN, SPAN), 1)
    upper = (row_id <= col_id).astype(jnp.float32)
    for b in range(blocks):
        span = slice(b * SPAN, (b + 1) * SPAN)
        b_t[:, span] = mixed_bc[span, :state_size].T.astype(jnp.bfloat16)
        cum = jnp.dot(
            rate_ref[:, span], upper,
            precision=lax.Precision.HIGHEST, preferred_element_type=jnp.float32,
        )
        cum_ref[:, span] = cum
        cum_t = cum.T
        step_t = step_ref[:, span].T
        cum_t_ref[span, :] = cum_t
        step_t_ref[span, :] = step_t
        gain_t_ref[span, :] = jnp.where(carried[span], jnp.exp(cum_t), 0.0)
        tail_t[span, :] = jnp.where(
            in_tail[span], jnp.exp(cum_t[SPAN - 1 : SPAN] - cum_t), 0.0
        ) * step_t

    def group(c, unused):
        lanes = pl.ds(pl.multiple_of(c * size, size), size)
        turn = lax.rem(HEADS_PAD - c * per_group, HEADS_PAD)
        ext[0:8, :size] = rim_x_ref[:, lanes]
        ext[8 : 8 + rows, :size] = x_ref[:, lanes].astype(jnp.float32)
        mixed = conv_taps(ext, conv_x_ref[:, lanes], keeps, rows).astype(jnp.bfloat16)
        mixed_ref[:, lanes] = mixed
        weight = spread_heads(pltpu.roll(tail_t[...], turn, 1), head_size, size)
        weighted = (mixed.astype(jnp.float32) * weight).astype(jnp.bfloat16)
        running = None
        through = None
        for b in range(blocks):
            span = slice(b * SPAN, (b + 1) * SPAN)
            fresh = jnp.dot(b_t[:, span], weighted[span], preferred_element_type=jnp.float32)
            ends = gain_t_ref[(b + 1) * SPAN - 8 : (b + 1) * SPAN, :]
            decay = spread_heads(pltpu.roll(ends, turn, 1), head_size, size)[7:8]
            fresh_ref[b, :, lanes] = fresh
            decay_ref[b, :, lanes] = jnp.broadcast_to(decay, (8, size))
            running = fresh if b == 0 else decay * running + fresh
            through = decay if b == 0 else through * decay
        msg_ref[0:state_size, lanes] = running.astype(jnp.bfloat16)
        high = through.astype(jnp.bfloat16)
        low = through - high.astype(jnp.float32)
        both = jnp.concatenate(
            [
                jnp.broadcast_to(high.astype(jnp.float32), (8, size)),
                jnp.broadcast_to(low, (8, size)),
            ]
        )
        msg_ref[state_size : state_size + EXTRA, lanes] = both.astype(jnp.bfloat16)
        return unused

    lax.fori_loop(0, width // size, group, 0)


def mix_kernel(
    head_size,
    mixed_ref, bc_ref, cum_ref, cum_t_ref, step_t_ref, ids_col_ref, ids_row_ref, skip_ref,
    out_ref,
    scores,
):
    width = mixed_ref.shape[1]
    size = group_lanes(width)
    per_group = size // head_size
    state_size = bc_ref.shape[1] // 2
    half = SPAN // 2
    row_id = lax.broadcasted_iota(jnp.int32, (SPAN, SPAN), 0)
    col_id = lax.broadcasted_iota(jnp.int32, (SPAN, SPAN), 1)
    raw = lax.dot_general(
        bc_ref[:, state_size:], bc_ref[:, :state_size], (((1,), (1,)), ((), ())),
        preferred_element_type=jnp.float32,
    )
    same = (ids_col_ref[...] == ids_row_ref[...]) & (col_id <= row_id)
    scores[...] = jnp.where(same, raw, 0.0)

    def group(c, unused):
        lanes = pl.ds(pl.multiple_of(c * size, size), size)
        turn = lax.rem(HEADS_PAD - c * per_group, HEADS_PAD)
        cum_t = pltpu.roll(cum_t_ref[...], turn, 1)
        steps = spread_heads(pltpu.roll(step_t_ref[...], turn, 1), head_size, size)
        x = mixed_ref[:, lanes].astype(jnp.float32)
        stepped = (x * steps).astype(jnp.bfloat16)
        tops, bottoms = [], []
        for k in range(per_group):
            own = slice(k * head_size, (k + 1) * head_size)
            column = cum_t[:, k : k + 1]
            row = cum_ref[pl.ds(c * per_group + k, 1), :]
            top = scores[:half, :half] * jnp.exp(jnp.minimum(column[:half] - row[:, :half], 0.0))
            bottom = scores[half:, :] * jnp.exp(jnp.minimum(column[half:] - row, 0.0))
            tops.append(
                jnp.dot(
                    top.astype(jnp.bfloat16), stepped[:half, own],
                    preferred_element_type=jnp.float32,
                )
            )
            bottoms.append(
                jnp.dot(
                    bottom.astype(jnp.bfloat16), stepped[:, own],
                    preferred_element_type=jnp.float32,
                )
            )
        skip = skip_ref[:, lanes]
        out_ref[:half, lanes] = jnp.concatenate(tops, axis=1) + skip * x[:half]
        out_ref[half:, lanes] = jnp.concatenate(bottoms, axis=1) + skip * x[half:]
        return unused

    lax.fori_loop(0, width // size, group, 0)


def gate_kernel(
    head_size,
    state_ref, bc_ref, gain_t_ref, part_ref, z_ref, norm_ref,
    out_ref, squares_ref,
):
    width = part_ref.shape[1]
    size = group_lanes(width)
    per_group = size // head_size
    state_size = bc_ref.shape[1] // 2
    c_vals = bc_ref[:, state_size:]

    def group(c, squares):
        lanes = pl.ds(pl.multiple_of(c * size, size), size)
        turn = lax.rem(HEADS_PAD - c * per_group, HEADS_PAD)
        gain = spread_heads(pltpu.roll(gain_t_ref[...], turn, 1), head_size, size)
        reached = jnp.dot(c_vals, state_ref[:, lanes], preferred_element_type=jnp.float32)
        y = (part_ref[:, lanes] + gain * reached).astype(jnp.bfloat16).astype(jnp.float32)
        gated = y * silu(z_ref[:, lanes].astype(jnp.float32))
        out_ref[:, lanes] = (gated * norm_ref[:, lanes]).astype(jnp.bfloat16)
        square = gated * gated
        for tile in range(size // 128):
            squares = squares + square[:, tile * 128 : (tile + 1) * 128]
        return squares

    squares_ref[...] = lax.fori_loop(
        0, width // size, group, jnp.zeros((SPAN, 128), jnp.float32)
    )


def fused_kernel(
    head_size, chunk,
    x_ref, bc_in_ref, z_hbm, dt_ref, ids_row_ref, conv_x_ref, conv_bc_ref, a_log_ref, bias_ref,
    skip_heads_ref, norm_ref, w_ref,
    out_ref,
    ext, ids_ext, rim_x, rim_bc, rim_ids, ids_sent, mixed_ref, bc_ref, cum_ref, cum_t_ref,
    step_t_ref, gain_t_ref, tail_t, b_t, fresh_ref, decay_ref, state_ref, part_ref, enter_ref,
    scores, got, whole, near, far, sent, landed, own_decay, got_decay, pair_decay, near_decay,
    z_ref, w_far, w_near, scaled, state, sums, sends, gots, row_sends, row_gots,
    halo_sems, load_sems, decay_sems, got_sems, whole_sems, far_sems, land_sems,
    send_sems, got_out_sems, row_send_sems, row_got_sems,
):
    rows, width = x_ref.shape
    size = group_lanes(width)
    per_group = size // head_size
    groups = width // size
    pieces = groups // 2
    blocks = rows // SPAN
    state_size = bc_in_ref.shape[1] // 2
    half = SPAN // 2
    out_width = out_ref.shape[1]
    heads = dt_ref.shape[0]
    f32, bf16 = jnp.float32, jnp.bfloat16
    seq_count = lax.axis_size("seq")
    me = lax.axis_index("seq")
    parity = lax.rem(me, 2)
    odd = parity == 1
    partner = me + 1 - 2 * parity
    beyond = lax.rem(me + seq_count - 1 + 2 * parity, seq_count)
    has_up = me < seq_count - 2
    has_down = me >= 2
    has_far = me >= 4
    has_next = me < seq_count - 1
    has_prev = me >= 1
    inside = has_next & has_prev
    above = lax.rem(me + 2, seq_count)
    below = lax.rem(me + seq_count - 2, seq_count)
    following = lax.rem(me + 1, seq_count)
    member = lax.axis_index("tensor")
    peer = 1 - member
    mesh_type = pl.DeviceIdType.MESH

    barrier = pltpu.get_barrier_semaphore()
    pl.semaphore_signal(barrier, inc=1, device_id={"seq": partner}, device_id_type=mesh_type)
    pl.semaphore_signal(barrier, inc=1, device_id={"tensor": peer}, device_id_type=mesh_type)

    @pl.when(has_up)
    def greet_above():
        pl.semaphore_signal(barrier, inc=1, device_id={"seq": above}, device_id_type=mesh_type)

    @pl.when(has_down)
    def greet_below():
        pl.semaphore_signal(barrier, inc=1, device_id={"seq": below}, device_id_type=mesh_type)

    @pl.when(inside)
    def greet_beyond():
        pl.semaphore_signal(barrier, inc=1, device_id={"seq": beyond}, device_id_type=mesh_type)

    loads = [pltpu.make_async_copy(z_hbm, z_ref, load_sems.at[0])]
    for k, (who, place) in enumerate(((peer, w_far), (member, w_near))):
        loads.append(
            pltpu.make_async_copy(
                w_ref.at[:, pl.ds(pl.multiple_of(who * out_width, 128), out_width)],
                place,
                load_sems.at[k + 1],
            )
        )
    for load in loads:
        load.start()
    ids_row = ids_row_ref[...].astype(f32)
    ids_sent[...] = jnp.broadcast_to(ids_row[:, rows - 128 :], ids_sent.shape)

    @pl.when(jnp.logical_not(has_down))
    def clear_near():
        near[...] = jnp.zeros_like(near)
        near_decay[...] = jnp.zeros_like(near_decay)

    @pl.when(jnp.logical_not(has_far))
    def clear_far():
        far[...] = jnp.zeros_like(far)

    @pl.when(jnp.logical_not(has_prev))
    def clear_rim():
        rim_x[...] = jnp.zeros_like(rim_x)
        rim_bc[...] = jnp.zeros_like(rim_bc)
        rim_ids[...] = jnp.full(rim_ids.shape, -1.0, f32)

    @pl.when(has_up & has_down)
    def meet_five():
        pl.semaphore_wait(barrier, 5)

    @pl.when(inside & jnp.logical_not(has_up & has_down))
    def meet_four():
        pl.semaphore_wait(barrier, 4)

    @pl.when(jnp.logical_not(inside))
    def meet_three():
        pl.semaphore_wait(barrier, 3)

    def lanes_of(which, k):
        return pl.ds(pl.multiple_of((which * pieces + k) * size, size), size)

    def remote(source, landing, send_sem, recv_sem, device):
        return pltpu.make_async_remote_copy(
            src_ref=source, dst_ref=landing, send_sem=send_sem, recv_sem=recv_sem,
            device_id={"seq": device}, device_id_type=mesh_type,
        )

    def decay_copy():
        return remote(own_decay, got_decay, decay_sems.at[0], decay_sems.at[1], partner)

    def pair_decay_copy():
        return remote(pair_decay, near_decay, decay_sems.at[2], decay_sems.at[3], above)

    def state_copy(k):
        return remote(
            state_ref.at[:, lanes_of(1 - parity, k)], got.at[k], got_sems.at[0, k],
            got_sems.at[1, k], partner,
        )

    def whole_copy(k):
        return remote(whole.at[k], near.at[k], whole_sems.at[0, k], whole_sems.at[1, k], above)

    def far_copy(k):
        return remote(near.at[k], far.at[k], far_sems.at[0, k], far_sems.at[1, k], above)

    def land_copy(k):
        return remote(sent.at[k], landed.at[k], land_sems.at[0, k], land_sems.at[1, k], partner)

    def halo_copies():
        last = pl.ds(rows - 16, 16)
        return [
            remote(x_ref.at[last, :], rim_x, halo_sems.at[0, 0], halo_sems.at[1, 0], following),
            remote(bc_in_ref.at[last, :], rim_bc, halo_sems.at[0, 1], halo_sems.at[1, 1], following),
            remote(ids_sent, rim_ids, halo_sems.at[0, 2], halo_sems.at[1, 2], following),
        ]

    @pl.when(has_next)
    def send_halo():
        for copy in halo_copies():
            copy.start()

    def column(row):
        return jnp.broadcast_to(row, (128, row.shape[1])).T

    logits = dt_ref[...].astype(f32) + column(bias_ref[...])[:heads, 0:1]
    step_size = jnp.maximum(logits, 0.0) + jnp.log1p(jnp.exp(-jnp.abs(logits)))
    rates = -jnp.exp(column(a_log_ref[...])[:heads, 0:1]) * step_size
    spare = jnp.zeros((HEADS_PAD - heads, rows), f32)
    step_size = jnp.concatenate([step_size, spare])
    rates = jnp.concatenate([rates, spare])
    ids_ext[8 : 8 + rows, :] = column(ids_row)
    ids = ids_ext[8 : 8 + rows, :]

    @pl.when(has_prev)
    def take_halo():
        for copy in halo_copies():
            copy.wait_recv()

    ids_ext[0:8, :] = column(rim_ids[0:1, :])[120:128, :]
    taps = conv_x_ref.shape[0]
    keeps = []
    for k in range(1, taps):
        same = ids_ext[8 - k : 8 - k + rows, :] == ids
        keeps.append(jnp.concatenate([same.astype(f32)] * (size // 128), axis=1) > 0.5)
    ext[0:8, :] = rim_bc[...].astype(f32)[8:16]
    ext[8 : 8 + rows, :] = bc_in_ref[...].astype(f32)
    mixed_bc = conv_taps(ext, conv_bc_ref[...].astype(f32), keeps, rows)
    bc_ref[...] = mixed_bc.astype(bf16)
    row_id = lax.broadcasted_iota(jnp.int32, (SPAN, SPAN), 0)
    col_id = lax.broadcasted_iota(jnp.int32, (SPAN, SPAN), 1)
    upper = (row_id <= col_id).astype(f32)
    for b in range(blocks):
        span = slice(b * SPAN, (b + 1) * SPAN)
        b_t[:, span] = mixed_bc[span, :state_size].T.astype(bf16)
        cum = jnp.dot(
            rates[:, span], upper,
            precision=lax.Precision.HIGHEST, preferred_element_type=f32,
        )
        cum_ref[:, span] = cum
        cum_t = cum.T
        step_t = step_size[:, span].T
        cum_t_ref[span, :] = cum_t
        step_t_ref[span, :] = step_t
        prior = ids_ext[8 + b * SPAN - 1 : 8 + b * SPAN, :]
        final = ids_ext[8 + (b + 1) * SPAN - 1 : 8 + (b + 1) * SPAN, :]
        gain_t_ref[span, :] = jnp.where(ids[span] == prior, jnp.exp(cum_t), 0.0)
        tail_t[span, :] = jnp.where(
            ids[span] == final, jnp.exp(cum_t[SPAN - 1 : SPAN] - cum_t), 0.0
        ) * step_t
    decay = gain_t_ref[SPAN - 1 : SPAN, :]
    for b in range(1, blocks):
        decay = decay * gain_t_ref[(b + 1) * SPAN - 1 : (b + 1) * SPAN, :]
    own_decay[...] = jnp.broadcast_to(decay, own_decay.shape)
    decay_copy().start()

    def decay_row(ref, k):
        turn = lax.rem(HEADS_PAD - (parity * pieces + k) * per_group, HEADS_PAD)
        turn = lax.rem(turn + HEADS_PAD, HEADS_PAD)
        return spread_heads(pltpu.roll(ref[...], turn, 1), head_size, size)[0:1]

    def first_state(k):
        mine = state_ref[:, lanes_of(parity, k)].astype(f32)
        theirs = got[k].astype(f32)
        return jnp.where(odd, theirs, mine), jnp.where(odd, mine, theirs)

    def states(j, unused):
        c = lax.rem(j + (1 - parity) * pieces, groups)
        lanes = pl.ds(pl.multiple_of(c * size, size), size)
        turn = lax.rem(HEADS_PAD - c * per_group, HEADS_PAD)
        ext[0:8, :] = rim_x[:, lanes].astype(f32)[8:16]
        ext[8 : 8 + rows, :] = x_ref[:, lanes].astype(f32)
        mixed = conv_taps(ext, conv_x_ref[:, lanes].astype(f32), keeps, rows).astype(bf16)
        mixed_ref[:, lanes] = mixed
        weight = spread_heads(pltpu.roll(tail_t[...], turn, 1), head_size, size)
        weighted = (mixed.astype(f32) * weight).astype(bf16)
        running = None
        for b in range(blocks):
            span = slice(b * SPAN, (b + 1) * SPAN)
            fresh = jnp.dot(b_t[:, span], weighted[span], preferred_element_type=f32)
            ends = gain_t_ref[(b + 1) * SPAN - 8 : (b + 1) * SPAN, :]
            block_decay = spread_heads(pltpu.roll(ends, turn, 1), head_size, size)[7:8]
            if b + 1 < blocks:
                fresh_ref[b, :, lanes] = fresh
                decay_ref[b, :, lanes] = jnp.broadcast_to(block_decay, (8, size))
            running = fresh if b == 0 else block_decay * running + fresh
        state_ref[:, lanes] = running.astype(bf16)

        @pl.when(j < pieces)
        def send_state():
            state_copy(j).start()

        @pl.when(j == pieces)
        def take_decay():
            decay_copy().wait_recv()
            pair_decay[...] = own_decay[...] * got_decay[...]

            @pl.when(has_up)
            def pass_decay():
                pair_decay_copy().start()

        @pl.when(j >= pieces)
        def join():
            k = j - pieces
            state_copy(k).wait_recv()

            @pl.when(has_up)
            def send_whole():
                first, second = first_state(k)
                odd_decay = jnp.where(odd, decay_row(own_decay, k), decay_row(got_decay, k))
                whole[k] = (second + odd_decay * first).astype(bf16)
                whole_copy(k).start()

        return unused

    lax.fori_loop(0, groups, states, 0)
    ids_wide = jnp.concatenate([ids] * (SPAN // 128), axis=1)
    skip_tile = jnp.broadcast_to(skip_heads_ref[...], (8, HEADS_PAD))
    for b in range(blocks):
        span = slice(b * SPAN, (b + 1) * SPAN)
        raw = lax.dot_general(
            bc_ref[span, state_size:], bc_ref[span, :state_size], (((1,), (1,)), ((), ())),
            preferred_element_type=f32,
        )
        same = (ids_wide[span] == ids_row[:, span]) & (col_id <= row_id)
        scores[b] = jnp.where(same, raw, 0.0)

    def mix(c, b):
        lanes = pl.ds(pl.multiple_of(c * size, size), size)
        span = pl.ds(b * SPAN, SPAN)
        turn = lax.rem(HEADS_PAD - c * per_group, HEADS_PAD)
        cum_t = pltpu.roll(cum_t_ref[span, :], turn, 1)
        steps = spread_heads(pltpu.roll(step_t_ref[span, :], turn, 1), head_size, size)
        x = mixed_ref[span, lanes].astype(f32)
        stepped = (x * steps).astype(bf16)
        skip = spread_heads(pltpu.roll(skip_tile, turn, 1), head_size, size)[0:1]
        tops, bottoms = [], []
        for k in range(per_group):
            own = slice(k * head_size, (k + 1) * head_size)
            column = cum_t[:, k : k + 1]
            row = cum_ref[pl.ds(c * per_group + k, 1), span]
            top = scores[b, :half, :half] * jnp.exp(
                jnp.minimum(column[:half] - row[:, :half], 0.0)
            )
            bottom = scores[b, half:, :] * jnp.exp(jnp.minimum(column[half:] - row, 0.0))
            tops.append(
                jnp.dot(top.astype(bf16), stepped[:half, own], preferred_element_type=f32)
            )
            bottoms.append(
                jnp.dot(bottom.astype(bf16), stepped[:, own], preferred_element_type=f32)
            )
        both = jnp.concatenate(
            [jnp.concatenate(tops, axis=1), jnp.concatenate(bottoms, axis=1)], axis=0
        )
        part_ref[span, lanes] = both + skip * x

    def step(j, unused):
        @pl.when(j < pieces)
        def forward():
            @pl.when(has_down)
            def take_near():
                whole_copy(j).wait_recv()

                @pl.when(has_up)
                def pass_near():
                    far_copy(j).start()

        @pl.when(j >= pieces)
        def close():
            k = j - pieces

            @pl.when((k == 0) & has_down)
            def take_near_decay():
                pair_decay_copy().wait_recv()

            @pl.when(has_far)
            def take_far():
                far_copy(k).wait_recv()

            entering = near[k].astype(f32) + decay_row(near_decay, k) * far[k].astype(f32)
            first, _ = first_state(k)
            even_decay = jnp.where(odd, decay_row(got_decay, k), decay_row(own_decay, k))
            later = first + even_decay * entering
            enter_ref[:, lanes_of(parity, k)] = jnp.where(odd, later, entering).astype(bf16)
            sent[k] = jnp.where(odd, entering, later).astype(bf16)
            land_copy(k).start()

        for b in range(blocks):
            mix(j, b)
        return unused

    lax.fori_loop(0, groups, step, 0)
    for k in range(pieces):
        land_copy(k).wait_recv()
        enter_ref[:, lanes_of(1 - parity, k)] = landed[k]
    loads[0].wait()
    count = rows // chunk
    per_block = SPAN // chunk
    tile = 256 if out_width % 256 == 0 else 128

    def product(q, weights, store):
        def columns(j, unused):
            lanes = pl.ds(pl.multiple_of(j * tile, tile), tile)
            store(
                lanes,
                jnp.dot(
                    scaled[q * chunk : (q + 1) * chunk, :], weights[:, lanes],
                    preferred_element_type=jnp.float32,
                ).astype(jnp.bfloat16),
            )
            return unused

        lax.fori_loop(0, out_width // tile, columns, 0)

    copies = []
    for q in range(count):
        b, within = q // per_block, q % per_block
        here = slice(q * chunk, (q + 1) * chunk)

        def group(c, squares):
            lanes = pl.ds(pl.multiple_of(c * size, size), size)
            turn = lax.rem(HEADS_PAD - c * per_group, HEADS_PAD)
            if q == 0:
                state[:, lanes] = enter_ref[:, lanes]
            elif within == 0:
                state[:, lanes] = (
                    decay_ref[b - 1, 0:1, lanes] * state[:, lanes].astype(jnp.float32)
                    + fresh_ref[b - 1, :, lanes]
                ).astype(jnp.bfloat16)
            gain = spread_heads(pltpu.roll(gain_t_ref[here, :], turn, 1), head_size, size)
            reached = jnp.dot(
                bc_ref[here, state_size:], state[:, lanes], preferred_element_type=jnp.float32
            )
            y = part_ref[here, lanes] + gain * reached
            y = y.astype(jnp.bfloat16).astype(jnp.float32)
            gated = y * silu(z_ref[here, lanes].astype(jnp.float32))
            scaled[here, lanes] = (gated * norm_ref[:, lanes]).astype(jnp.bfloat16)
            square = gated * gated
            for k in range(size // 128):
                squares = squares + square[:, k * 128 : (k + 1) * 128]
            return squares

        squares = lax.fori_loop(0, width // size, group, jnp.zeros((chunk, 128), jnp.float32))
        row = jnp.sum(squares.T, axis=0, keepdims=True)
        row_sends[q] = jnp.broadcast_to(row, (8, chunk))
        if q == 0:
            loads[1].wait()

        def put(lanes, value):
            sends[q, :, lanes] = value

        product(q, w_far, put)
        pair = [
            pltpu.make_async_remote_copy(
                src_ref=source.at[q],
                dst_ref=landing.at[q],
                send_sem=out_sems.at[q],
                recv_sem=in_sems.at[q],
                device_id={"tensor": peer},
                device_id_type=pl.DeviceIdType.MESH,
            )
            for source, landing, out_sems, in_sems in (
                (row_sends, row_gots, row_send_sems, row_got_sems),
                (sends, gots, send_sems, got_out_sems),
            )
        ]
        for copy in pair:
            copy.start()
        copies.append(pair)

    loads[2].wait()
    for q in range(count):
        here = slice(q * chunk, (q + 1) * chunk)

        def keep(lanes, value):
            sums[:, lanes] = value

        product(q, w_near, keep)
        for copy in copies[q]:
            copy.wait_recv()
        row = row_sends[q, 0:1, :] + row_gots[q, 0:1, :]
        inv_row = lax.rsqrt(row / (2 * width) + 1e-05)
        inv = jnp.broadcast_to(inv_row, (128, chunk)).T
        for j in range(out_width // 128):
            lanes = slice(j * 128, (j + 1) * 128)
            total = sums[:, lanes].astype(jnp.float32) + gots[q, :, lanes].astype(jnp.float32)
            out_ref[here, lanes] = (total * inv).astype(jnp.bfloat16)
    for pair in copies:
        for copy in pair:
            copy.wait_send()

    @pl.when(has_next)
    def finish_halo():
        for copy in halo_copies():
            copy.wait_send()

    decay_copy().wait_send()
    for k in range(pieces):
        state_copy(k).wait_send()
        land_copy(k).wait_send()

    @pl.when(has_up)
    def finish():
        pair_decay_copy().wait_send()
        for k in range(pieces):
            whole_copy(k).wait_send()

    @pl.when(has_up & has_down)
    def finish_far():
        for k in range(pieces):
            far_copy(k).wait_send()


def call(kernel, out_shape, scratch, flops, moved, *operands):
    return pl.pallas_call(
        kernel,
        out_shape=out_shape,
        in_specs=[pl.BlockSpec(memory_space=pltpu.VMEM)] * len(operands),
        out_specs=jax.tree.map(lambda _: pl.BlockSpec(memory_space=pltpu.VMEM), out_shape),
        scratch_shapes=scratch,
        compiler_params=pltpu.CompilerParams(vmem_limit_bytes=VMEM_BYTES),
        cost_estimate=pl.CostEstimate(flops=flops, bytes_accessed=moved, transcendentals=0),
    )(*operands)


def split_message(message):
    state_size = message.shape[0] - EXTRA
    wide = message.astype(jnp.float32)
    return wide[:state_size], wide[state_size : state_size + 1] + wide[state_size + 8 : state_size + 9]


def merge(near, far):
    near_state, near_decay = near
    far_state, far_decay = far
    return near_state + near_decay * far_state, near_decay * far_decay


def pack_message(pair):
    state, decay = pair
    width = state.shape[1]
    high = decay.astype(jnp.bfloat16)
    low = (decay - high.astype(jnp.float32)).astype(jnp.bfloat16)
    return jnp.concatenate(
        [
            state.astype(jnp.bfloat16),
            jnp.broadcast_to(high, (8, width)),
            jnp.broadcast_to(low, (8, width)),
        ]
    )


def pass_state(message):
    count = lax.axis_size("seq")
    odd = (lax.axis_index("seq") % 2) == 1
    other = lax.ppermute(message, "seq", [(i, i ^ 1) for i in range(count)])
    first = split_message(jnp.where(odd, other, message))
    second = split_message(jnp.where(odd, message, other))
    entering = shifted(pack_message(merge(second, first)), "seq", 2)
    reach = 1
    while reach < count // 4:
        farther = shifted(entering, "seq", 2 * reach)
        joined = merge(split_message(entering), split_message(farther))
        reach *= 2
        if reach < count // 4:
            entering = pack_message(joined)
        else:
            entering = joined
    if reach == 1:
        entering = split_message(entering)
    alone = split_message(other)
    return jnp.where(odd, merge(alone, entering)[0], entering[0])


def local(
    x_stream,
    bc_stream,
    z_gate,
    dt_stream,
    doc_ids,
    conv_x,
    conv_bc,
    a_log,
    dt_bias,
    d_skip,
    norm_gain,
    w_out,
):
    rows, width = x_stream.shape
    heads = dt_stream.shape[0]
    head_size = width // heads
    bc_width = bc_stream.shape[1]
    state_size = bc_width // 2
    taps = conv_x.shape[0]
    blocks = rows // SPAN
    edge = rows - taps + 1
    f32, bf16 = jnp.float32, jnp.bfloat16
    shape = jax.ShapeDtypeStruct
    out_width = w_out.shape[1] // lax.axis_size("tensor")
    if (
        lax.axis_size("seq") == 8
        and lax.axis_size("tensor") == 2
        and width % 512 == 0
        and width >= 1536
        and out_width % 128 == 0
        and bc_width == group_lanes(width)
        and heads <= HEADS_PAD
        and heads % 8 == 0
    ):
        vmem = pl.BlockSpec(memory_space=pltpu.VMEM)
        hbm = pl.BlockSpec(memory_space=pl.ANY)
        pieces = width // 512
        chunk = 128
        count = rows // chunk
        piece = (pieces, state_size, 256)

        def head_row(values):
            return jnp.pad(values, (0, HEADS_PAD - heads))[None, :]

        return pl.pallas_call(
            functools.partial(fused_kernel, head_size, chunk),
            out_shape=shape((rows, out_width), bf16),
            in_specs=[vmem, vmem, hbm] + [vmem] * 8 + [hbm],
            out_specs=vmem,
            scratch_shapes=[
                pltpu.VMEM((rows + 8, 256), f32),
                pltpu.VMEM((rows + 8, 128), f32),
                pltpu.VMEM((16, width), bf16),
                pltpu.VMEM((16, bc_width), bf16),
                pltpu.VMEM((8, 128), f32),
                pltpu.VMEM((8, 128), f32),
                pltpu.VMEM((rows, width), bf16),
                pltpu.VMEM((rows, bc_width), bf16),
                pltpu.VMEM((HEADS_PAD, rows), f32),
                pltpu.VMEM((rows, HEADS_PAD), f32),
                pltpu.VMEM((rows, HEADS_PAD), f32),
                pltpu.VMEM((rows, HEADS_PAD), f32),
                pltpu.VMEM((rows, HEADS_PAD), f32),
                pltpu.VMEM((state_size, rows), bf16),
                pltpu.VMEM((blocks, state_size, width), f32),
                pltpu.VMEM((blocks, 8, width), f32),
                pltpu.VMEM((state_size, width), bf16),
                pltpu.VMEM((rows, width), f32),
                pltpu.VMEM((state_size, width), bf16),
                pltpu.VMEM((blocks, SPAN, SPAN), f32),
            ]
            + [pltpu.VMEM(piece, bf16)] * 6
            + [pltpu.VMEM((8, HEADS_PAD), f32)] * 4
            + [
                pltpu.VMEM((rows, width), bf16),
                pltpu.VMEM((width, out_width), bf16),
                pltpu.VMEM((width, out_width), bf16),
                pltpu.VMEM((rows, width), bf16),
                pltpu.VMEM((state_size, width), bf16),
                pltpu.VMEM((chunk, out_width), bf16),
                pltpu.VMEM((count, chunk, out_width), bf16),
                pltpu.VMEM((count, chunk, out_width), bf16),
                pltpu.VMEM((count, 8, chunk), f32),
                pltpu.VMEM((count, 8, chunk), f32),
                pltpu.SemaphoreType.DMA((2, 3)),
                pltpu.SemaphoreType.DMA((3,)),
                pltpu.SemaphoreType.DMA((4,)),
            ]
            + [pltpu.SemaphoreType.DMA((2, pieces))] * 4
            + [pltpu.SemaphoreType.DMA((count,))] * 4,
            compiler_params=pltpu.CompilerParams(
                collective_id=0, has_side_effects=True, vmem_limit_bytes=VMEM_BYTES
            ),
            cost_estimate=pl.CostEstimate(
                flops=2 * rows * width * w_out.shape[1],
                bytes_accessed=2 * width * w_out.shape[1],
                transcendentals=0,
            ),
        )(
            x_stream, bc_stream, z_gate, dt_stream, doc_ids[None, :], conv_x, conv_bc,
            head_row(a_log), head_row(dt_bias), head_row(d_skip), norm_gain[None, :], w_out,
        )
    own_ids = doc_ids.astype(f32)
    tail_ids = jnp.broadcast_to(own_ids[edge:].astype(bf16)[:, None], (taps - 1, 128))
    rim = shifted(
        jnp.concatenate([x_stream[edge:], bc_stream[edge:], tail_ids], axis=1), "seq", 1
    )
    step = jax.nn.softplus(dt_stream.astype(f32) + dt_bias[:, None])
    rate = -jnp.exp(a_log)[:, None] * step
    step = jnp.pad(step, ((0, HEADS_PAD - heads), (0, 0)))
    rate = jnp.pad(rate, ((0, HEADS_PAD - heads), (0, 0)))
    rim_wide = jnp.pad(rim.astype(f32), ((8 - taps + 1, 0), (0, 0)))
    rim_ids = jnp.where(lax.axis_index("seq") == 0, -1.0, rim[:, width + bc_width].astype(f32))
    ext_ids = jnp.concatenate([rim_ids, own_ids])
    block_ids = own_ids.reshape(blocks, SPAN)
    prior = jnp.concatenate([ext_ids[taps - 2][None], own_ids[SPAN - 1 :: SPAN][: blocks - 1]])
    columns = [(ext_ids[taps - 1 - k : taps - 1 - k + rows] == own_ids) for k in range(1, taps)]
    columns.append((block_ids == prior[:, None]).reshape(rows))
    columns.append((block_ids == block_ids[:, -1:]).reshape(rows))
    flags = jnp.stack([c.astype(f32) for c in columns], axis=1)

    mixed, mixed_bc, cum, cum_t, step_t, gain_t, fresh, decay, message = call(
        functools.partial(states_kernel, head_size),
        (
            shape((rows, width), bf16),
            shape((rows, bc_width), bf16),
            shape((HEADS_PAD, rows), f32),
            shape((rows, HEADS_PAD), f32),
            shape((rows, HEADS_PAD), f32),
            shape((rows, HEADS_PAD), f32),
            shape((blocks, state_size, width), f32),
            shape((blocks, 8, width), f32),
            shape((state_size + EXTRA, width), bf16),
        ),
        [
            pltpu.VMEM((rows + 8, max(bc_width, group_lanes(width))), f32),
            pltpu.VMEM((rows, HEADS_PAD), f32),
            pltpu.VMEM((state_size, rows), bf16),
        ],
        2 * rows * state_size * width,
        8 * rows * width,
        x_stream, rim_wide[:, :width], bc_stream, rim_wide[:, width : width + bc_width], step, rate,
        flags, conv_x.astype(f32), conv_bc.astype(f32),
    )
    skip_row = jnp.repeat(d_skip, head_size)[None, :]
    parts = []
    for b in range(blocks):
        span = slice(b * SPAN, (b + 1) * SPAN)
        parts.append(
            call(
                functools.partial(mix_kernel, head_size),
                shape((SPAN, width), f32),
                [pltpu.VMEM((SPAN, SPAN), f32)],
                2 * SPAN * SPAN * width * 16,
                8 * SPAN * width,
                mixed[span], mixed_bc[span], cum[:, span], cum_t[span], step_t[span],
                own_ids[span][:, None], own_ids[span][None, :], skip_row,
            )
        )
    state = pass_state(message)

    members = lax.axis_size("tensor")
    member = lax.axis_index("tensor")
    pieces = []
    for b in range(blocks):
        span = slice(b * SPAN, (b + 1) * SPAN)
        scaled, squares = call(
            functools.partial(gate_kernel, head_size),
            (shape((SPAN, width), bf16), shape((SPAN, 128), f32)),
            [],
            2 * SPAN * state_size * width,
            12 * SPAN * width,
            state.astype(bf16), mixed_bc[span], gain_t[span], parts[b], z_gate[span],
            norm_gain[None, :],
        )
        if b + 1 < blocks:
            state = decay[b, 0:1] * state + fresh[b]
        product = jnp.dot(scaled, w_out, preferred_element_type=f32).astype(bf16)
        total = lax.dynamic_slice_in_dim(product, member * out_width, out_width, 1).astype(f32)
        square = jnp.sum(squares, axis=1, keepdims=True)
        high = square.astype(bf16)
        low = (square - high.astype(f32)).astype(bf16)
        lane = lax.broadcasted_iota(jnp.int32, (SPAN, 128), 1)
        aside = jnp.where(lane == 0, high, jnp.where(lane == 1, low, jnp.zeros_like(low)))
        for distance in range(1, members):
            target = (member + distance) % members
            block = lax.dynamic_slice_in_dim(product, target * out_width, out_width, 1)
            route = [(i, (i + distance) % members) for i in range(members)]
            got = lax.ppermute(jnp.concatenate([block, aside], axis=1), "tensor", route)
            total = total + got[:, :out_width].astype(f32)
            square = square + jnp.sum(got[:, out_width : out_width + 2].astype(f32), axis=1, keepdims=True)
        inv_norm = lax.rsqrt(square / (width * members) + 1e-05)
        pieces.append((total * inv_norm).astype(bf16))
    return jnp.concatenate(pieces)


def solution(mesh):
    return jax.shard_map(
        local,
        mesh=mesh,
        in_specs=(
            P(("dp", "seq"), "tensor"),
            P(("dp", "seq"), None),
            P(("dp", "seq"), "tensor"),
            P("tensor", ("dp", "seq")),
            P(("dp", "seq")),
            P(None, "tensor"),
            P(),
            P("tensor"),
            P("tensor"),
            P("tensor"),
            P("tensor"),
            P("tensor", None),
        ),
        out_specs=P(("dp", "seq"), "tensor"),
        check_vma=False,
    )
```

```python
import functools

import jax
import jax.numpy as jnp
from jax import lax
from jax.experimental import pallas as pl
from jax.experimental.pallas import tpu as pltpu
from jax.sharding import PartitionSpec as P

SPAN = 256
HEADS_PAD = 128
EXTRA = 16
VMEM_BYTES = 48 * 1024 * 1024
FUSED_VMEM_BYTES = 61 * 1024 * 1024


def shifted(block, axis, distance):
    count = lax.axis_size(axis)
    return lax.ppermute(block, axis, [(i, i + distance) for i in range(count - distance)])


def group_lanes(width):
    return 256 if width % 256 == 0 else 128


def silu(v):
    return v / (1.0 + jnp.exp(-v))


def spread_heads(columns, width, lanes):
    rows = columns.shape[0]
    lane = lax.broadcasted_iota(jnp.int32, (rows, 128), 1)
    per_tile = 128 // width
    tiles = []
    for tile in range(lanes // 128):
        value = jnp.broadcast_to(columns[:, tile * per_tile : tile * per_tile + 1], (rows, 128))
        for k in range(1, per_tile):
            head = tile * per_tile + k
            value = jnp.where(
                lane >= k * width, jnp.broadcast_to(columns[:, head : head + 1], (rows, 128)), value
            )
        tiles.append(value)
    return jnp.concatenate(tiles, axis=1)


def conv_taps(ext, weights, keeps, rows):
    wide = weights.shape[1]
    total = weights[0:1] * ext[pl.ds(8, rows), :wide]
    for k in range(1, weights.shape[0]):
        total = total + jnp.where(keeps[k - 1][:, :wide], weights[k : k + 1] * ext[pl.ds(8 - k, rows), :wide], 0.0)
    return silu(total)


def states_kernel(
    head_size,
    x_ref, rim_x_ref, bc_ref, rim_bc_ref, step_ref, rate_ref, flags_ref, conv_x_ref, conv_bc_ref,
    mixed_ref, bc_out_ref, cum_ref, cum_t_ref, step_t_ref, gain_t_ref, fresh_ref, decay_ref, msg_ref,
    ext, tail_t, b_t,
):
    rows, width = x_ref.shape
    blocks = rows // SPAN
    size = group_lanes(width)
    per_group = size // head_size
    state_size = bc_ref.shape[1] // 2
    flags = flags_ref[...]
    taps = conv_x_ref.shape[0]
    keeps = [
        jnp.broadcast_to(flags[:, k : k + 1], (rows, ext.shape[1])) > 0.5 for k in range(taps - 1)
    ]
    carried = jnp.broadcast_to(flags[:, 3:4], (rows, HEADS_PAD)) > 0.5
    in_tail = jnp.broadcast_to(flags[:, 4:5], (rows, HEADS_PAD)) > 0.5

    ext[0:8, :] = rim_bc_ref[...]
    ext[8 : 8 + rows, :] = bc_ref[...].astype(jnp.float32)
    mixed_bc = conv_taps(ext, conv_bc_ref[...], keeps, rows)
    bc_out_ref[...] = mixed_bc.astype(jnp.bfloat16)
    row_id = lax.broadcasted_iota(jnp.int32, (SPAN, SPAN), 0)
    col_id = lax.broadcasted_iota(jnp.int32, (SPAN, SPAN), 1)
    upper = (row_id <= col_id).astype(jnp.float32)
    for b in range(blocks):
        span = slice(b * SPAN, (b + 1) * SPAN)
        b_t[:, span] = mixed_bc[span, :state_size].T.astype(jnp.bfloat16)
        cum = jnp.dot(
            rate_ref[:, span], upper,
            precision=lax.Precision.HIGHEST, preferred_element_type=jnp.float32,
        )
        cum_ref[:, span] = cum
        cum_t = cum.T
        step_t = step_ref[:, span].T
        cum_t_ref[span, :] = cum_t
        step_t_ref[span, :] = step_t
        gain_t_ref[span, :] = jnp.where(carried[span], jnp.exp(cum_t), 0.0)
        tail_t[span, :] = jnp.where(
            in_tail[span], jnp.exp(cum_t[SPAN - 1 : SPAN] - cum_t), 0.0
        ) * step_t

    def group(c, unused):
        lanes = pl.ds(pl.multiple_of(c * size, size), size)
        turn = lax.rem(HEADS_PAD - c * per_group, HEADS_PAD)
        ext[0:8, :size] = rim_x_ref[:, lanes]
        ext[8 : 8 + rows, :size] = x_ref[:, lanes].astype(jnp.float32)
        mixed = conv_taps(ext, conv_x_ref[:, lanes], keeps, rows).astype(jnp.bfloat16)
        mixed_ref[:, lanes] = mixed
        weight = spread_heads(pltpu.roll(tail_t[...], turn, 1), head_size, size)
        weighted = (mixed.astype(jnp.float32) * weight).astype(jnp.bfloat16)
        running = None
        through = None
        for b in range(blocks):
            span = slice(b * SPAN, (b + 1) * SPAN)
            fresh = jnp.dot(b_t[:, span], weighted[span], preferred_element_type=jnp.float32)
            ends = gain_t_ref[(b + 1) * SPAN - 8 : (b + 1) * SPAN, :]
            decay = spread_heads(pltpu.roll(ends, turn, 1), head_size, size)[7:8]
            fresh_ref[b, :, lanes] = fresh
            decay_ref[b, :, lanes] = jnp.broadcast_to(decay, (8, size))
            running = fresh if b == 0 else decay * running + fresh
            through = decay if b == 0 else through * decay
        msg_ref[0:state_size, lanes] = running.astype(jnp.bfloat16)
        high = through.astype(jnp.bfloat16)
        low = through - high.astype(jnp.float32)
        both = jnp.concatenate(
            [
                jnp.broadcast_to(high.astype(jnp.float32), (8, size)),
                jnp.broadcast_to(low, (8, size)),
            ]
        )
        msg_ref[state_size : state_size + EXTRA, lanes] = both.astype(jnp.bfloat16)
        return unused

    lax.fori_loop(0, width // size, group, 0)


def mix_kernel(
    head_size,
    mixed_ref, bc_ref, cum_ref, cum_t_ref, step_t_ref, ids_col_ref, ids_row_ref, skip_ref,
    out_ref,
    scores,
):
    width = mixed_ref.shape[1]
    size = group_lanes(width)
    per_group = size // head_size
    state_size = bc_ref.shape[1] // 2
    half = SPAN // 2
    row_id = lax.broadcasted_iota(jnp.int32, (SPAN, SPAN), 0)
    col_id = lax.broadcasted_iota(jnp.int32, (SPAN, SPAN), 1)
    raw = lax.dot_general(
        bc_ref[:, state_size:], bc_ref[:, :state_size], (((1,), (1,)), ((), ())),
        preferred_element_type=jnp.float32,
    )
    same = (ids_col_ref[...] == ids_row_ref[...]) & (col_id <= row_id)
    scores[...] = jnp.where(same, raw, 0.0)

    def group(c, unused):
        lanes = pl.ds(pl.multiple_of(c * size, size), size)
        turn = lax.rem(HEADS_PAD - c * per_group, HEADS_PAD)
        cum_t = pltpu.roll(cum_t_ref[...], turn, 1)
        steps = spread_heads(pltpu.roll(step_t_ref[...], turn, 1), head_size, size)
        x = mixed_ref[:, lanes].astype(jnp.float32)
        stepped = (x * steps).astype(jnp.bfloat16)
        tops, bottoms = [], []
        for k in range(per_group):
            own = slice(k * head_size, (k + 1) * head_size)
            column = cum_t[:, k : k + 1]
            row = cum_ref[pl.ds(c * per_group + k, 1), :]
            top = scores[:half, :half] * jnp.exp(jnp.minimum(column[:half] - row[:, :half], 0.0))
            bottom = scores[half:, :] * jnp.exp(jnp.minimum(column[half:] - row, 0.0))
            tops.append(
                jnp.dot(
                    top.astype(jnp.bfloat16), stepped[:half, own],
                    preferred_element_type=jnp.float32,
                )
            )
            bottoms.append(
                jnp.dot(
                    bottom.astype(jnp.bfloat16), stepped[:, own],
                    preferred_element_type=jnp.float32,
                )
            )
        skip = skip_ref[:, lanes]
        out_ref[:half, lanes] = jnp.concatenate(tops, axis=1) + skip * x[:half]
        out_ref[half:, lanes] = jnp.concatenate(bottoms, axis=1) + skip * x[half:]
        return unused

    lax.fori_loop(0, width // size, group, 0)


def gate_kernel(
    head_size,
    state_ref, bc_ref, gain_t_ref, part_ref, z_ref, norm_ref,
    out_ref, squares_ref,
):
    width = part_ref.shape[1]
    size = group_lanes(width)
    per_group = size // head_size
    state_size = bc_ref.shape[1] // 2
    c_vals = bc_ref[:, state_size:]

    def group(c, squares):
        lanes = pl.ds(pl.multiple_of(c * size, size), size)
        turn = lax.rem(HEADS_PAD - c * per_group, HEADS_PAD)
        gain = spread_heads(pltpu.roll(gain_t_ref[...], turn, 1), head_size, size)
        reached = jnp.dot(c_vals, state_ref[:, lanes], preferred_element_type=jnp.float32)
        y = (part_ref[:, lanes] + gain * reached).astype(jnp.bfloat16).astype(jnp.float32)
        gated = y * silu(z_ref[:, lanes].astype(jnp.float32))
        out_ref[:, lanes] = (gated * norm_ref[:, lanes]).astype(jnp.bfloat16)
        square = gated * gated
        for tile in range(size // 128):
            squares = squares + square[:, tile * 128 : (tile + 1) * 128]
        return squares

    squares_ref[...] = lax.fori_loop(
        0, width // size, group, jnp.zeros((SPAN, 128), jnp.float32)
    )


def fused_kernel(
    head_size, chunk,
    x_hbm, bc_hbm, z_hbm, w_ref, dt_ref, ids_row_ref, conv_x_ref, conv_bc_ref, rows_ref,
    out_ref,
    x_ref, bc_in_ref,
    ext, ids_ext, rim_x, rim_bc, rim_ids, ids_sent, mixed_ref, bc_ref, cum_ref, cum_t_ref,
    step_t_ref, gain_t_ref, tail_t, b_t, fresh_ref, decay_ref, state_ref, part_ref, enter_ref,
    scores, got, whole, near, far, sent, landed, own_decay, got_decay, pair_decay, near_decay,
    z_ref, w_far, w_near, scaled, state, sums, sends, gots, row_sends, row_gots,
    halo_sems, load_sems, decay_sems, got_sems, whole_sems, far_sems, land_sems,
    send_sems, got_out_sems, row_send_sems, row_got_sems,
):
    rows, width = x_ref.shape
    size = group_lanes(width)
    per_group = size // head_size
    groups = width // size
    pieces = groups // 2
    blocks = rows // SPAN
    state_size = bc_in_ref.shape[1] // 2
    half = SPAN // 2
    out_width = out_ref.shape[1]
    heads = dt_ref.shape[0]
    f32, bf16 = jnp.float32, jnp.bfloat16
    seq_count = lax.axis_size("seq")
    me = lax.axis_index("seq")
    parity = lax.rem(me, 2)
    odd = parity == 1
    partner = me + 1 - 2 * parity
    beyond = lax.rem(me + seq_count - 1 + 2 * parity, seq_count)
    has_up = me < seq_count - 2
    has_down = me >= 2
    has_far = me >= 4
    has_next = me < seq_count - 1
    has_prev = me >= 1
    inside = has_next & has_prev
    above = lax.rem(me + 2, seq_count)
    below = lax.rem(me + seq_count - 2, seq_count)
    following = lax.rem(me + 1, seq_count)
    member = lax.axis_index("tensor")
    peer = 1 - member
    mesh_type = pl.DeviceIdType.MESH

    barrier = pltpu.get_barrier_semaphore()
    pl.semaphore_signal(barrier, inc=1, device_id={"seq": partner}, device_id_type=mesh_type)
    pl.semaphore_signal(barrier, inc=1, device_id={"tensor": peer}, device_id_type=mesh_type)

    @pl.when(has_up)
    def greet_above():
        pl.semaphore_signal(barrier, inc=1, device_id={"seq": above}, device_id_type=mesh_type)

    @pl.when(has_down)
    def greet_below():
        pl.semaphore_signal(barrier, inc=1, device_id={"seq": below}, device_id_type=mesh_type)

    @pl.when(inside)
    def greet_beyond():
        pl.semaphore_signal(barrier, inc=1, device_id={"seq": beyond}, device_id_type=mesh_type)

    first_loads = [
        pltpu.make_async_copy(source, place, load_sems.at[3 + k])
        for k, (source, place) in enumerate(
            ((bc_hbm, bc_in_ref), (x_hbm, x_ref))
        )
    ]
    for load in first_loads:
        load.start()
    loads = [pltpu.make_async_copy(z_hbm, z_ref, load_sems.at[0])]
    for k, (who, place) in enumerate(((peer, w_far), (member, w_near))):
        loads.append(
            pltpu.make_async_copy(
                w_ref.at[:, pl.ds(pl.multiple_of(who * out_width, 128), out_width)],
                place,
                load_sems.at[k + 1],
            )
        )
    for load in loads:
        load.start()
    ids_row = ids_row_ref[...].astype(f32)
    ids_sent[...] = jnp.broadcast_to(ids_row[:, rows - 128 :], ids_sent.shape)

    @pl.when(jnp.logical_not(has_down))
    def clear_near():
        near[...] = jnp.zeros_like(near)
        near_decay[...] = jnp.zeros_like(near_decay)

    @pl.when(jnp.logical_not(has_far))
    def clear_far():
        far[...] = jnp.zeros_like(far)

    @pl.when(jnp.logical_not(has_prev))
    def clear_rim():
        rim_x[...] = jnp.zeros_like(rim_x)
        rim_bc[...] = jnp.zeros_like(rim_bc)
        rim_ids[...] = jnp.full(rim_ids.shape, -1.0, f32)

    @pl.when(has_up & has_down)
    def meet_five():
        pl.semaphore_wait(barrier, 5)

    @pl.when(inside & jnp.logical_not(has_up & has_down))
    def meet_four():
        pl.semaphore_wait(barrier, 4)

    @pl.when(jnp.logical_not(inside))
    def meet_three():
        pl.semaphore_wait(barrier, 3)

    def lanes_of(which, k):
        return pl.ds(pl.multiple_of((which * pieces + k) * size, size), size)

    def remote(source, landing, send_sem, recv_sem, device):
        return pltpu.make_async_remote_copy(
            src_ref=source, dst_ref=landing, send_sem=send_sem, recv_sem=recv_sem,
            device_id={"seq": device}, device_id_type=mesh_type,
        )

    def decay_copy():
        return remote(own_decay, got_decay, decay_sems.at[0], decay_sems.at[1], partner)

    def pair_decay_copy():
        return remote(pair_decay, near_decay, decay_sems.at[2], decay_sems.at[3], above)

    def state_copy(k):
        return remote(
            state_ref.at[:, lanes_of(1 - parity, k)], got.at[k], got_sems.at[0, k],
            got_sems.at[1, k], partner,
        )

    def whole_copy(k):
        return remote(whole.at[k], near.at[k], whole_sems.at[0, k], whole_sems.at[1, k], above)

    def far_copy(k):
        return remote(near.at[k], far.at[k], far_sems.at[0, k], far_sems.at[1, k], above)

    def land_copy(k):
        return remote(sent.at[k], landed.at[k], land_sems.at[0, k], land_sems.at[1, k], partner)

    def halo_copies():
        last = pl.ds(rows - 16, 16)
        return [
            remote(x_hbm.at[last, :], rim_x, halo_sems.at[0, 0], halo_sems.at[1, 0], following),
            remote(bc_hbm.at[last, :], rim_bc, halo_sems.at[0, 1], halo_sems.at[1, 1], following),
            remote(ids_sent, rim_ids, halo_sems.at[0, 2], halo_sems.at[1, 2], following),
        ]

    @pl.when(has_next)
    def send_halo():
        for copy in halo_copies():
            copy.start()

    def column(row):
        return jnp.broadcast_to(row, (128, row.shape[1])).T

    logits = dt_ref[...].astype(f32) + column(rows_ref[:, HEADS_PAD : 2 * HEADS_PAD])[:heads, 0:1]
    step_size = jnp.maximum(logits, 0.0) + jnp.log1p(jnp.exp(-jnp.abs(logits)))
    rates = -jnp.exp(column(rows_ref[:, :HEADS_PAD])[:heads, 0:1]) * step_size
    spare = jnp.zeros((HEADS_PAD - heads, rows), f32)
    step_size = jnp.concatenate([step_size, spare])
    rates = jnp.concatenate([rates, spare])
    ids_ext[8 : 8 + rows, :] = column(ids_row)
    ids = ids_ext[8 : 8 + rows, :]

    for load in first_loads:
        load.wait()

    @pl.when(has_prev)
    def take_halo():
        for copy in halo_copies():
            copy.wait_recv()

    ids_ext[0:8, :] = column(rim_ids[0:1, :])[120:128, :]
    taps = conv_x_ref.shape[0]
    keeps = []
    for k in range(1, taps):
        same = ids_ext[8 - k : 8 - k + rows, :] == ids
        keeps.append(jnp.concatenate([same.astype(f32)] * (size // 128), axis=1) > 0.5)
    ext[0:8, :] = rim_bc[...].astype(f32)[8:16]
    ext[8 : 8 + rows, :] = bc_in_ref[...].astype(f32)
    mixed_bc = conv_taps(ext, conv_bc_ref[...].astype(f32), keeps, rows)
    bc_ref[...] = mixed_bc.astype(bf16)
    row_id = lax.broadcasted_iota(jnp.int32, (SPAN, SPAN), 0)
    col_id = lax.broadcasted_iota(jnp.int32, (SPAN, SPAN), 1)
    upper = (row_id <= col_id).astype(f32)
    for b in range(blocks):
        span = slice(b * SPAN, (b + 1) * SPAN)
        b_t[:, span] = mixed_bc[span, :state_size].T.astype(bf16)
        cum = jnp.dot(
            rates[:, span], upper,
            precision=lax.Precision.HIGHEST, preferred_element_type=f32,
        )
        cum_ref[:, span] = cum
        cum_t = cum.T
        step_t = step_size[:, span].T
        cum_t_ref[span, :] = cum_t
        step_t_ref[span, :] = step_t
        prior = ids_ext[8 + b * SPAN - 1 : 8 + b * SPAN, :]
        final = ids_ext[8 + (b + 1) * SPAN - 1 : 8 + (b + 1) * SPAN, :]
        gain_t_ref[span, :] = jnp.where(ids[span] == prior, jnp.exp(cum_t), 0.0)
        tail_t[span, :] = jnp.where(
            ids[span] == final, jnp.exp(cum_t[SPAN - 1 : SPAN] - cum_t), 0.0
        ) * step_t
    decay = gain_t_ref[SPAN - 1 : SPAN, :]
    for b in range(1, blocks):
        decay = decay * gain_t_ref[(b + 1) * SPAN - 1 : (b + 1) * SPAN, :]
    own_decay[...] = jnp.broadcast_to(decay, own_decay.shape)
    decay_copy().start()

    def decay_row(ref, k):
        turn = lax.rem(HEADS_PAD - (parity * pieces + k) * per_group, HEADS_PAD)
        turn = lax.rem(turn + HEADS_PAD, HEADS_PAD)
        return spread_heads(pltpu.roll(ref[...], turn, 1), head_size, size)[0:1]

    def first_state(k):
        mine = state_ref[:, lanes_of(parity, k)].astype(f32)
        theirs = got[k].astype(f32)
        return jnp.where(odd, theirs, mine), jnp.where(odd, mine, theirs)

    def states(j, unused):
        c = lax.rem(j + (1 - parity) * pieces, groups)
        lanes = pl.ds(pl.multiple_of(c * size, size), size)
        turn = lax.rem(HEADS_PAD - c * per_group, HEADS_PAD)
        ext[0:8, :] = rim_x[:, lanes].astype(f32)[8:16]
        ext[8 : 8 + rows, :] = x_ref[:, lanes].astype(f32)
        mixed = conv_taps(ext, conv_x_ref[:, lanes].astype(f32), keeps, rows).astype(bf16)
        mixed_ref[:, lanes] = mixed
        weight = spread_heads(pltpu.roll(tail_t[...], turn, 1), head_size, size)
        weighted = (mixed.astype(f32) * weight).astype(bf16)
        running = None
        for b in range(blocks):
            span = slice(b * SPAN, (b + 1) * SPAN)
            fresh = jnp.dot(b_t[:, span], weighted[span], preferred_element_type=f32)
            ends = gain_t_ref[(b + 1) * SPAN - 8 : (b + 1) * SPAN, :]
            block_decay = spread_heads(pltpu.roll(ends, turn, 1), head_size, size)[7:8]
            if b + 1 < blocks:
                fresh_ref[b, :, lanes] = fresh
                decay_ref[b, :, lanes] = jnp.broadcast_to(block_decay, (8, size))
            running = fresh if b == 0 else block_decay * running + fresh
        state_ref[:, lanes] = running.astype(bf16)

        @pl.when(j < pieces)
        def send_state():
            state_copy(j).start()

        @pl.when(j == pieces)
        def take_decay():
            decay_copy().wait_recv()
            pair_decay[...] = own_decay[...] * got_decay[...]

            @pl.when(has_up)
            def pass_decay():
                pair_decay_copy().start()

        @pl.when(j >= pieces)
        def join():
            k = j - pieces
            state_copy(k).wait_recv()

            @pl.when(has_up)
            def send_whole():
                first, second = first_state(k)
                odd_decay = jnp.where(odd, decay_row(own_decay, k), decay_row(got_decay, k))
                whole[k] = (second + odd_decay * first).astype(bf16)
                whole_copy(k).start()

        return unused

    lax.fori_loop(0, groups, states, 0)
    ids_wide = jnp.concatenate([ids] * (SPAN // 128), axis=1)
    skip_tile = jnp.broadcast_to(rows_ref[:, 2 * HEADS_PAD : 3 * HEADS_PAD], (8, HEADS_PAD))
    for b in range(blocks):
        span = slice(b * SPAN, (b + 1) * SPAN)
        raw = lax.dot_general(
            bc_ref[span, state_size:], bc_ref[span, :state_size], (((1,), (1,)), ((), ())),
            preferred_element_type=f32,
        )
        same = (ids_wide[span] == ids_row[:, span]) & (col_id <= row_id)
        scores[b] = jnp.where(same, raw, 0.0)

    def mix(c, b):
        lanes = pl.ds(pl.multiple_of(c * size, size), size)
        span = pl.ds(b * SPAN, SPAN)
        turn = lax.rem(HEADS_PAD - c * per_group, HEADS_PAD)
        cum_t = pltpu.roll(cum_t_ref[span, :], turn, 1)
        steps = spread_heads(pltpu.roll(step_t_ref[span, :], turn, 1), head_size, size)
        x = mixed_ref[span, lanes].astype(f32)
        stepped = (x * steps).astype(bf16)
        skip = spread_heads(pltpu.roll(skip_tile, turn, 1), head_size, size)[0:1]
        tops, bottoms = [], []
        for k in range(per_group):
            own = slice(k * head_size, (k + 1) * head_size)
            column = cum_t[:, k : k + 1]
            row = cum_ref[pl.ds(c * per_group + k, 1), span]
            top = scores[b, :half, :half] * jnp.exp(
                jnp.minimum(column[:half] - row[:, :half], 0.0)
            )
            bottom = scores[b, half:, :] * jnp.exp(jnp.minimum(column[half:] - row, 0.0))
            tops.append(
                jnp.dot(top.astype(bf16), stepped[:half, own], preferred_element_type=f32)
            )
            bottoms.append(
                jnp.dot(bottom.astype(bf16), stepped[:, own], preferred_element_type=f32)
            )
        both = jnp.concatenate(
            [jnp.concatenate(tops, axis=1), jnp.concatenate(bottoms, axis=1)], axis=0
        )
        part_ref[span, lanes] = both + skip * x

    def step(j, unused):
        @pl.when(j < pieces)
        def forward():
            @pl.when(has_down)
            def take_near():
                whole_copy(j).wait_recv()

                @pl.when(has_up)
                def pass_near():
                    far_copy(j).start()

        @pl.when(j >= pieces)
        def close():
            k = j - pieces

            @pl.when((k == 0) & has_down)
            def take_near_decay():
                pair_decay_copy().wait_recv()

            @pl.when(has_far)
            def take_far():
                far_copy(k).wait_recv()

            entering = near[k].astype(f32) + decay_row(near_decay, k) * far[k].astype(f32)
            first, _ = first_state(k)
            even_decay = jnp.where(odd, decay_row(got_decay, k), decay_row(own_decay, k))
            later = first + even_decay * entering
            enter_ref[:, lanes_of(parity, k)] = jnp.where(odd, later, entering).astype(bf16)
            sent[k] = jnp.where(odd, entering, later).astype(bf16)
            land_copy(k).start()

        for b in range(blocks):
            mix(j, b)
        return unused

    lax.fori_loop(0, groups, step, 0)
    for k in range(pieces):
        land_copy(k).wait_recv()
        enter_ref[:, lanes_of(1 - parity, k)] = landed[k]
    loads[0].wait()
    count = rows // chunk
    per_block = SPAN // chunk
    gate_size = 512
    gate_heads = gate_size // head_size
    tile = 256 if out_width % 256 == 0 else 128

    def product(here, weights, store):
        def columns(j, unused):
            lanes = pl.ds(pl.multiple_of(j * tile, tile), tile)
            store(
                lanes,
                jnp.dot(
                    scaled[here, :], weights[:, lanes],
                    preferred_element_type=jnp.float32,
                ).astype(jnp.bfloat16),
            )
            return unused

        lax.fori_loop(0, out_width // tile, columns, 0)

    copies = []
    for q in range(count):
        b, within = q // per_block, q % per_block
        here = slice(q * chunk, (q + 1) * chunk)

        def group(c, squares):
            lanes = pl.ds(pl.multiple_of(c * gate_size, gate_size), gate_size)
            turn = lax.rem(HEADS_PAD - c * gate_heads, HEADS_PAD)
            if q == 0:
                state[:, lanes] = enter_ref[:, lanes]
            elif within == 0:
                state[:, lanes] = (
                    decay_ref[b - 1, 0:1, lanes] * state[:, lanes].astype(jnp.float32)
                    + fresh_ref[b - 1, :, lanes]
                ).astype(jnp.bfloat16)
            gains = rows_ref[:, pl.ds(pl.multiple_of(3 * HEADS_PAD + c * gate_size, 128), gate_size)]
            gain = spread_heads(pltpu.roll(gain_t_ref[here, :], turn, 1), head_size, gate_size)
            reached = jnp.dot(
                bc_ref[here, state_size:], state[:, lanes], preferred_element_type=jnp.float32
            )
            y = part_ref[here, lanes] + gain * reached
            y = y.astype(jnp.bfloat16).astype(jnp.float32)
            gated = y * silu(z_ref[here, lanes].astype(jnp.float32))
            scaled[here, lanes] = (gated * gains).astype(jnp.bfloat16)
            square = gated * gated
            for k in range(gate_size // 128):
                squares = squares + square[:, k * 128 : (k + 1) * 128]
            return squares

        squares = lax.fori_loop(0, width // gate_size, group, jnp.zeros((chunk, 128), jnp.float32))
        row = jnp.sum(squares.T, axis=0, keepdims=True)
        row_sends[q] = jnp.broadcast_to(row, (8, chunk))
        if q == 0:
            loads[1].wait()

        def put(lanes, value):
            sends[q, :, lanes] = value

        product(here, w_far, put)
        pair = [
            pltpu.make_async_remote_copy(
                src_ref=source.at[q],
                dst_ref=landing.at[q],
                send_sem=out_sems.at[q],
                recv_sem=in_sems.at[q],
                device_id={"tensor": peer},
                device_id_type=pl.DeviceIdType.MESH,
            )
            for source, landing, out_sems, in_sems in (
                (row_sends, row_gots, row_send_sems, row_got_sems),
                (sends, gots, send_sems, got_out_sems),
            )
        ]
        for copy in pair:
            copy.start()
        copies.append(pair)

    loads[2].wait()

    def keep(lanes, value):
        sums[:, lanes] = value

    product(slice(0, rows), w_near, keep)
    for q in range(count):
        here = slice(q * chunk, (q + 1) * chunk)
        for copy in copies[q]:
            copy.wait_recv()
        row = row_sends[q, 0:1, :] + row_gots[q, 0:1, :]
        inv_row = lax.rsqrt(row / (2 * width) + 1e-05)
        inv = jnp.broadcast_to(inv_row, (128, chunk)).T
        for j in range(out_width // 128):
            lanes = slice(j * 128, (j + 1) * 128)
            total = sums[here, lanes].astype(jnp.float32) + gots[q, :, lanes].astype(jnp.float32)
            out_ref[here, lanes] = (total * inv).astype(jnp.bfloat16)
    for pair in copies:
        for copy in pair:
            copy.wait_send()

    @pl.when(has_next)
    def finish_halo():
        for copy in halo_copies():
            copy.wait_send()

    decay_copy().wait_send()
    for k in range(pieces):
        state_copy(k).wait_send()
        land_copy(k).wait_send()

    @pl.when(has_up)
    def finish():
        pair_decay_copy().wait_send()
        for k in range(pieces):
            whole_copy(k).wait_send()

    @pl.when(has_up & has_down)
    def finish_far():
        for k in range(pieces):
            far_copy(k).wait_send()


def call(kernel, out_shape, scratch, flops, moved, *operands):
    return pl.pallas_call(
        kernel,
        out_shape=out_shape,
        in_specs=[pl.BlockSpec(memory_space=pltpu.VMEM)] * len(operands),
        out_specs=jax.tree.map(lambda _: pl.BlockSpec(memory_space=pltpu.VMEM), out_shape),
        scratch_shapes=scratch,
        compiler_params=pltpu.CompilerParams(vmem_limit_bytes=VMEM_BYTES),
        cost_estimate=pl.CostEstimate(flops=flops, bytes_accessed=moved, transcendentals=0),
    )(*operands)


def split_message(message):
    state_size = message.shape[0] - EXTRA
    wide = message.astype(jnp.float32)
    return wide[:state_size], wide[state_size : state_size + 1] + wide[state_size + 8 : state_size + 9]


def merge(near, far):
    near_state, near_decay = near
    far_state, far_decay = far
    return near_state + near_decay * far_state, near_decay * far_decay


def pack_message(pair):
    state, decay = pair
    width = state.shape[1]
    high = decay.astype(jnp.bfloat16)
    low = (decay - high.astype(jnp.float32)).astype(jnp.bfloat16)
    return jnp.concatenate(
        [
            state.astype(jnp.bfloat16),
            jnp.broadcast_to(high, (8, width)),
            jnp.broadcast_to(low, (8, width)),
        ]
    )


def pass_state(message):
    count = lax.axis_size("seq")
    odd = (lax.axis_index("seq") % 2) == 1
    other = lax.ppermute(message, "seq", [(i, i ^ 1) for i in range(count)])
    first = split_message(jnp.where(odd, other, message))
    second = split_message(jnp.where(odd, message, other))
    entering = shifted(pack_message(merge(second, first)), "seq", 2)
    reach = 1
    while reach < count // 4:
        farther = shifted(entering, "seq", 2 * reach)
        joined = merge(split_message(entering), split_message(farther))
        reach *= 2
        if reach < count // 4:
            entering = pack_message(joined)
        else:
            entering = joined
    if reach == 1:
        entering = split_message(entering)
    alone = split_message(other)
    return jnp.where(odd, merge(alone, entering)[0], entering[0])


def local(
    x_stream,
    bc_stream,
    z_gate,
    dt_stream,
    doc_ids,
    conv_x,
    conv_bc,
    a_log,
    dt_bias,
    d_skip,
    norm_gain,
    w_out,
):
    rows, width = x_stream.shape
    heads = dt_stream.shape[0]
    head_size = width // heads
    bc_width = bc_stream.shape[1]
    state_size = bc_width // 2
    taps = conv_x.shape[0]
    blocks = rows // SPAN
    edge = rows - taps + 1
    f32, bf16 = jnp.float32, jnp.bfloat16
    shape = jax.ShapeDtypeStruct
    out_width = w_out.shape[1] // lax.axis_size("tensor")
    if (
        lax.axis_size("seq") == 8
        and lax.axis_size("tensor") == 2
        and width % 512 == 0
        and width >= 1536
        and out_width % 128 == 0
        and bc_width == group_lanes(width)
        and heads <= HEADS_PAD
        and heads % 8 == 0
    ):
        vmem = pl.BlockSpec(memory_space=pltpu.VMEM)
        hbm = pl.BlockSpec(memory_space=pl.ANY)
        pieces = width // 512
        chunk = 128
        count = rows // chunk
        piece = (pieces, state_size, 256)

        def padded(values):
            return jnp.pad(values, (0, HEADS_PAD - heads))

        return pl.pallas_call(
            functools.partial(fused_kernel, head_size, chunk),
            out_shape=shape((rows, out_width), bf16),
            in_specs=[hbm] * 4 + [vmem] * 5,
            out_specs=vmem,
            scratch_shapes=[
                pltpu.VMEM((rows, width), bf16),
                pltpu.VMEM((rows, bc_width), bf16),
                pltpu.VMEM((rows + 8, 256), f32),
                pltpu.VMEM((rows + 8, 128), f32),
                pltpu.VMEM((16, width), bf16),
                pltpu.VMEM((16, bc_width), bf16),
                pltpu.VMEM((8, 128), f32),
                pltpu.VMEM((8, 128), f32),
                pltpu.VMEM((rows, width), bf16),
                pltpu.VMEM((rows, bc_width), bf16),
                pltpu.VMEM((HEADS_PAD, rows), f32),
                pltpu.VMEM((rows, HEADS_PAD), f32),
                pltpu.VMEM((rows, HEADS_PAD), f32),
                pltpu.VMEM((rows, HEADS_PAD), f32),
                pltpu.VMEM((rows, HEADS_PAD), f32),
                pltpu.VMEM((state_size, rows), bf16),
                pltpu.VMEM((blocks, state_size, width), f32),
                pltpu.VMEM((blocks, 8, width), f32),
                pltpu.VMEM((state_size, width), bf16),
                pltpu.VMEM((rows, width), f32),
                pltpu.VMEM((state_size, width), bf16),
                pltpu.VMEM((blocks, SPAN, SPAN), f32),
            ]
            + [pltpu.VMEM(piece, bf16)] * 6
            + [pltpu.VMEM((8, HEADS_PAD), f32)] * 4
            + [
                pltpu.VMEM((rows, width), bf16),
                pltpu.VMEM((width, out_width), bf16),
                pltpu.VMEM((width, out_width), bf16),
                pltpu.VMEM((rows, width), bf16),
                pltpu.VMEM((state_size, width), bf16),
                pltpu.VMEM((rows, out_width), bf16),
                pltpu.VMEM((count, chunk, out_width), bf16),
                pltpu.VMEM((count, chunk, out_width), bf16),
                pltpu.VMEM((count, 8, chunk), f32),
                pltpu.VMEM((count, 8, chunk), f32),
                pltpu.SemaphoreType.DMA((2, 3)),
                pltpu.SemaphoreType.DMA((5,)),
                pltpu.SemaphoreType.DMA((4,)),
            ]
            + [pltpu.SemaphoreType.DMA((2, pieces))] * 4
            + [pltpu.SemaphoreType.DMA((count,))] * 4,
            compiler_params=pltpu.CompilerParams(
                collective_id=0, has_side_effects=True, vmem_limit_bytes=FUSED_VMEM_BYTES
            ),
            cost_estimate=pl.CostEstimate(
                flops=2 * rows * width * w_out.shape[1],
                bytes_accessed=2 * width * w_out.shape[1],
                transcendentals=0,
            ),
        )(
            x_stream, bc_stream, z_gate, w_out, dt_stream, doc_ids[None, :], conv_x, conv_bc,
            jnp.concatenate(
                [padded(a_log), padded(dt_bias), padded(d_skip), norm_gain]
            )[None, :],
        )
    own_ids = doc_ids.astype(f32)
    tail_ids = jnp.broadcast_to(own_ids[edge:].astype(bf16)[:, None], (taps - 1, 128))
    rim = shifted(
        jnp.concatenate([x_stream[edge:], bc_stream[edge:], tail_ids], axis=1), "seq", 1
    )
    step = jax.nn.softplus(dt_stream.astype(f32) + dt_bias[:, None])
    rate = -jnp.exp(a_log)[:, None] * step
    step = jnp.pad(step, ((0, HEADS_PAD - heads), (0, 0)))
    rate = jnp.pad(rate, ((0, HEADS_PAD - heads), (0, 0)))
    rim_wide = jnp.pad(rim.astype(f32), ((8 - taps + 1, 0), (0, 0)))
    rim_ids = jnp.where(lax.axis_index("seq") == 0, -1.0, rim[:, width + bc_width].astype(f32))
    ext_ids = jnp.concatenate([rim_ids, own_ids])
    block_ids = own_ids.reshape(blocks, SPAN)
    prior = jnp.concatenate([ext_ids[taps - 2][None], own_ids[SPAN - 1 :: SPAN][: blocks - 1]])
    columns = [(ext_ids[taps - 1 - k : taps - 1 - k + rows] == own_ids) for k in range(1, taps)]
    columns.append((block_ids == prior[:, None]).reshape(rows))
    columns.append((block_ids == block_ids[:, -1:]).reshape(rows))
    flags = jnp.stack([c.astype(f32) for c in columns], axis=1)

    mixed, mixed_bc, cum, cum_t, step_t, gain_t, fresh, decay, message = call(
        functools.partial(states_kernel, head_size),
        (
            shape((rows, width), bf16),
            shape((rows, bc_width), bf16),
            shape((HEADS_PAD, rows), f32),
            shape((rows, HEADS_PAD), f32),
            shape((rows, HEADS_PAD), f32),
            shape((rows, HEADS_PAD), f32),
            shape((blocks, state_size, width), f32),
            shape((blocks, 8, width), f32),
            shape((state_size + EXTRA, width), bf16),
        ),
        [
            pltpu.VMEM((rows + 8, max(bc_width, group_lanes(width))), f32),
            pltpu.VMEM((rows, HEADS_PAD), f32),
            pltpu.VMEM((state_size, rows), bf16),
        ],
        2 * rows * state_size * width,
        8 * rows * width,
        x_stream, rim_wide[:, :width], bc_stream, rim_wide[:, width : width + bc_width], step, rate,
        flags, conv_x.astype(f32), conv_bc.astype(f32),
    )
    skip_row = jnp.repeat(d_skip, head_size)[None, :]
    parts = []
    for b in range(blocks):
        span = slice(b * SPAN, (b + 1) * SPAN)
        parts.append(
            call(
                functools.partial(mix_kernel, head_size),
                shape((SPAN, width), f32),
                [pltpu.VMEM((SPAN, SPAN), f32)],
                2 * SPAN * SPAN * width * 16,
                8 * SPAN * width,
                mixed[span], mixed_bc[span], cum[:, span], cum_t[span], step_t[span],
                own_ids[span][:, None], own_ids[span][None, :], skip_row,
            )
        )
    state = pass_state(message)

    members = lax.axis_size("tensor")
    member = lax.axis_index("tensor")
    pieces = []
    for b in range(blocks):
        span = slice(b * SPAN, (b + 1) * SPAN)
        scaled, squares = call(
            functools.partial(gate_kernel, head_size),
            (shape((SPAN, width), bf16), shape((SPAN, 128), f32)),
            [],
            2 * SPAN * state_size * width,
            12 * SPAN * width,
            state.astype(bf16), mixed_bc[span], gain_t[span], parts[b], z_gate[span],
            norm_gain[None, :],
        )
        if b + 1 < blocks:
            state = decay[b, 0:1] * state + fresh[b]
        product = jnp.dot(scaled, w_out, preferred_element_type=f32).astype(bf16)
        total = lax.dynamic_slice_in_dim(product, member * out_width, out_width, 1).astype(f32)
        square = jnp.sum(squares, axis=1, keepdims=True)
        high = square.astype(bf16)
        low = (square - high.astype(f32)).astype(bf16)
        lane = lax.broadcasted_iota(jnp.int32, (SPAN, 128), 1)
        aside = jnp.where(lane == 0, high, jnp.where(lane == 1, low, jnp.zeros_like(low)))
        for distance in range(1, members):
            target = (member + distance) % members
            block = lax.dynamic_slice_in_dim(product, target * out_width, out_width, 1)
            route = [(i, (i + distance) % members) for i in range(members)]
            got = lax.ppermute(jnp.concatenate([block, aside], axis=1), "tensor", route)
            total = total + got[:, :out_width].astype(f32)
            square = square + jnp.sum(got[:, out_width : out_width + 2].astype(f32), axis=1, keepdims=True)
        inv_norm = lax.rsqrt(square / (width * members) + 1e-05)
        pieces.append((total * inv_norm).astype(bf16))
    return jnp.concatenate(pieces)


def solution(mesh):
    return jax.shard_map(
        local,
        mesh=mesh,
        in_specs=(
            P(("dp", "seq"), "tensor"),
            P(("dp", "seq"), None),
            P(("dp", "seq"), "tensor"),
            P("tensor", ("dp", "seq")),
            P(("dp", "seq")),
            P(None, "tensor"),
            P(),
            P("tensor"),
            P("tensor"),
            P("tensor"),
            P("tensor"),
            P("tensor", None),
        ),
        out_specs=P(("dp", "seq"), "tensor"),
        check_vma=False,
    )
```

```python
import functools

import jax
import jax.numpy as jnp
from jax import lax
from jax.experimental import pallas as pl
from jax.experimental.pallas import tpu as pltpu
from jax.sharding import PartitionSpec as P

SPAN = 256
HEADS_PAD = 128
EXTRA = 16
VMEM_BYTES = 48 * 1024 * 1024
FUSED_VMEM_BYTES = 61 * 1024 * 1024


def shifted(block, axis, distance):
    count = lax.axis_size(axis)
    return lax.ppermute(block, axis, [(i, i + distance) for i in range(count - distance)])


def group_lanes(width):
    return 256 if width % 256 == 0 else 128


def silu(v):
    scaled = 0.5 * v
    return scaled + scaled * jnp.tanh(scaled)


def spread_heads(columns, width, lanes):
    rows = columns.shape[0]
    lane = lax.broadcasted_iota(jnp.int32, (rows, 128), 1)
    per_tile = 128 // width
    tiles = []
    for tile in range(lanes // 128):
        value = jnp.broadcast_to(columns[:, tile * per_tile : tile * per_tile + 1], (rows, 128))
        for k in range(1, per_tile):
            head = tile * per_tile + k
            value = jnp.where(
                lane >= k * width, jnp.broadcast_to(columns[:, head : head + 1], (rows, 128)), value
            )
        tiles.append(value)
    return jnp.concatenate(tiles, axis=1)


def conv_taps(ext, weights, keeps, rows):
    wide = weights.shape[1]
    total = weights[0:1] * ext[pl.ds(8, rows), :wide]
    for k in range(1, weights.shape[0]):
        total = total + jnp.where(keeps[k - 1][:, :wide], weights[k : k + 1] * ext[pl.ds(8 - k, rows), :wide], 0.0)
    return silu(total)


def states_kernel(
    head_size,
    x_ref, rim_x_ref, bc_ref, rim_bc_ref, step_ref, rate_ref, flags_ref, conv_x_ref, conv_bc_ref,
    mixed_ref, bc_out_ref, cum_ref, cum_t_ref, step_t_ref, gain_t_ref, fresh_ref, decay_ref, msg_ref,
    ext, tail_t, b_t,
):
    rows, width = x_ref.shape
    blocks = rows // SPAN
    size = group_lanes(width)
    per_group = size // head_size
    state_size = bc_ref.shape[1] // 2
    flags = flags_ref[...]
    taps = conv_x_ref.shape[0]
    keeps = [
        jnp.broadcast_to(flags[:, k : k + 1], (rows, ext.shape[1])) > 0.5 for k in range(taps - 1)
    ]
    carried = jnp.broadcast_to(flags[:, 3:4], (rows, HEADS_PAD)) > 0.5
    in_tail = jnp.broadcast_to(flags[:, 4:5], (rows, HEADS_PAD)) > 0.5

    ext[0:8, :] = rim_bc_ref[...]
    ext[8 : 8 + rows, :] = bc_ref[...].astype(jnp.float32)
    mixed_bc = conv_taps(ext, conv_bc_ref[...], keeps, rows)
    bc_out_ref[...] = mixed_bc.astype(jnp.bfloat16)
    row_id = lax.broadcasted_iota(jnp.int32, (SPAN, SPAN), 0)
    col_id = lax.broadcasted_iota(jnp.int32, (SPAN, SPAN), 1)
    upper = (row_id <= col_id).astype(jnp.float32)
    for b in range(blocks):
        span = slice(b * SPAN, (b + 1) * SPAN)
        b_t[:, span] = mixed_bc[span, :state_size].T.astype(jnp.bfloat16)
        cum = jnp.dot(
            rate_ref[:, span], upper,
            precision=lax.Precision.HIGHEST, preferred_element_type=jnp.float32,
        )
        cum_ref[:, span] = cum
        cum_t = cum.T
        step_t = step_ref[:, span].T
        cum_t_ref[span, :] = cum_t
        step_t_ref[span, :] = step_t
        gain_t_ref[span, :] = jnp.where(carried[span], jnp.exp(cum_t), 0.0)
        tail_t[span, :] = jnp.where(
            in_tail[span], jnp.exp(cum_t[SPAN - 1 : SPAN] - cum_t), 0.0
        ) * step_t

    def group(c, unused):
        lanes = pl.ds(pl.multiple_of(c * size, size), size)
        turn = lax.rem(HEADS_PAD - c * per_group, HEADS_PAD)
        ext[0:8, :size] = rim_x_ref[:, lanes]
        ext[8 : 8 + rows, :size] = x_ref[:, lanes].astype(jnp.float32)
        mixed = conv_taps(ext, conv_x_ref[:, lanes], keeps, rows).astype(jnp.bfloat16)
        mixed_ref[:, lanes] = mixed
        weight = spread_heads(pltpu.roll(tail_t[...], turn, 1), head_size, size)
        weighted = (mixed.astype(jnp.float32) * weight).astype(jnp.bfloat16)
        running = None
        through = None
        for b in range(blocks):
            span = slice(b * SPAN, (b + 1) * SPAN)
            fresh = jnp.dot(b_t[:, span], weighted[span], preferred_element_type=jnp.float32)
            ends = gain_t_ref[(b + 1) * SPAN - 8 : (b + 1) * SPAN, :]
            decay = spread_heads(pltpu.roll(ends, turn, 1), head_size, size)[7:8]
            fresh_ref[b, :, lanes] = fresh
            decay_ref[b, :, lanes] = jnp.broadcast_to(decay, (8, size))
            running = fresh if b == 0 else decay * running + fresh
            through = decay if b == 0 else through * decay
        msg_ref[0:state_size, lanes] = running.astype(jnp.bfloat16)
        high = through.astype(jnp.bfloat16)
        low = through - high.astype(jnp.float32)
        both = jnp.concatenate(
            [
                jnp.broadcast_to(high.astype(jnp.float32), (8, size)),
                jnp.broadcast_to(low, (8, size)),
            ]
        )
        msg_ref[state_size : state_size + EXTRA, lanes] = both.astype(jnp.bfloat16)
        return unused

    lax.fori_loop(0, width // size, group, 0)


def mix_kernel(
    head_size,
    mixed_ref, bc_ref, cum_ref, cum_t_ref, step_t_ref, ids_col_ref, ids_row_ref, skip_ref,
    out_ref,
    scores,
):
    width = mixed_ref.shape[1]
    size = group_lanes(width)
    per_group = size // head_size
    state_size = bc_ref.shape[1] // 2
    half = SPAN // 2
    row_id = lax.broadcasted_iota(jnp.int32, (SPAN, SPAN), 0)
    col_id = lax.broadcasted_iota(jnp.int32, (SPAN, SPAN), 1)
    raw = lax.dot_general(
        bc_ref[:, state_size:], bc_ref[:, :state_size], (((1,), (1,)), ((), ())),
        preferred_element_type=jnp.float32,
    )
    same = (ids_col_ref[...] == ids_row_ref[...]) & (col_id <= row_id)
    scores[...] = jnp.where(same, raw, 0.0)

    def group(c, unused):
        lanes = pl.ds(pl.multiple_of(c * size, size), size)
        turn = lax.rem(HEADS_PAD - c * per_group, HEADS_PAD)
        cum_t = pltpu.roll(cum_t_ref[...], turn, 1)
        steps = spread_heads(pltpu.roll(step_t_ref[...], turn, 1), head_size, size)
        x = mixed_ref[:, lanes].astype(jnp.float32)
        stepped = (x * steps).astype(jnp.bfloat16)
        tops, bottoms = [], []
        for k in range(per_group):
            own = slice(k * head_size, (k + 1) * head_size)
            column = cum_t[:, k : k + 1]
            row = cum_ref[pl.ds(c * per_group + k, 1), :]
            top = scores[:half, :half] * jnp.exp(jnp.minimum(column[:half] - row[:, :half], 0.0))
            bottom = scores[half:, :] * jnp.exp(jnp.minimum(column[half:] - row, 0.0))
            tops.append(
                jnp.dot(
                    top.astype(jnp.bfloat16), stepped[:half, own],
                    preferred_element_type=jnp.float32,
                )
            )
            bottoms.append(
                jnp.dot(
                    bottom.astype(jnp.bfloat16), stepped[:, own],
                    preferred_element_type=jnp.float32,
                )
            )
        skip = skip_ref[:, lanes]
        out_ref[:half, lanes] = jnp.concatenate(tops, axis=1) + skip * x[:half]
        out_ref[half:, lanes] = jnp.concatenate(bottoms, axis=1) + skip * x[half:]
        return unused

    lax.fori_loop(0, width // size, group, 0)


def gate_kernel(
    head_size,
    state_ref, bc_ref, gain_t_ref, part_ref, z_ref, norm_ref,
    out_ref, squares_ref,
):
    width = part_ref.shape[1]
    size = group_lanes(width)
    per_group = size // head_size
    state_size = bc_ref.shape[1] // 2
    c_vals = bc_ref[:, state_size:]

    def group(c, squares):
        lanes = pl.ds(pl.multiple_of(c * size, size), size)
        turn = lax.rem(HEADS_PAD - c * per_group, HEADS_PAD)
        gain = spread_heads(pltpu.roll(gain_t_ref[...], turn, 1), head_size, size)
        reached = jnp.dot(c_vals, state_ref[:, lanes], preferred_element_type=jnp.float32)
        y = (part_ref[:, lanes] + gain * reached).astype(jnp.bfloat16).astype(jnp.float32)
        gated = y * silu(z_ref[:, lanes].astype(jnp.float32))
        out_ref[:, lanes] = (gated * norm_ref[:, lanes]).astype(jnp.bfloat16)
        square = gated * gated
        for tile in range(size // 128):
            squares = squares + square[:, tile * 128 : (tile + 1) * 128]
        return squares

    squares_ref[...] = lax.fori_loop(
        0, width // size, group, jnp.zeros((SPAN, 128), jnp.float32)
    )


def fused_kernel(
    head_size, chunk,
    x_hbm, bc_hbm, z_hbm, w_ref, dt_ref, ids_row_ref, conv_x_ref, conv_bc_ref, rows_ref,
    out_ref,
    x_ref, bc_in_ref,
    ext, ids_ext, rim_x, rim_bc, rim_ids, ids_sent, mixed_ref, bc_ref, cum_ref, cum_t_ref,
    step_t_ref, gain_t_ref, tail_t, b_t, fresh_ref, decay_ref, state_ref, part_ref, enter_ref,
    scores, got, whole, near, far, sent, landed, own_decay, got_decay, pair_decay, near_decay,
    z_ref, w_far, w_near, scaled, state, sums, sends, gots, row_sends, row_gots,
    halo_sems, load_sems, decay_sems, got_sems, whole_sems, far_sems, land_sems,
    send_sems, got_out_sems, row_send_sems, row_got_sems,
):
    rows, width = x_ref.shape
    size = group_lanes(width)
    per_group = size // head_size
    groups = width // size
    pieces = groups // 2
    blocks = rows // SPAN
    state_size = bc_in_ref.shape[1] // 2
    half = SPAN // 2
    out_width = out_ref.shape[1]
    heads = dt_ref.shape[0]
    f32, bf16 = jnp.float32, jnp.bfloat16
    seq_count = lax.axis_size("seq")
    me = lax.axis_index("seq")
    parity = lax.rem(me, 2)
    odd = parity == 1
    partner = me + 1 - 2 * parity
    beyond = lax.rem(me + seq_count - 1 + 2 * parity, seq_count)
    has_up = me < seq_count - 2
    has_down = me >= 2
    has_far = me >= 4
    has_next = me < seq_count - 1
    has_prev = me >= 1
    inside = has_next & has_prev
    above = lax.rem(me + 2, seq_count)
    below = lax.rem(me + seq_count - 2, seq_count)
    following = lax.rem(me + 1, seq_count)
    member = lax.axis_index("tensor")
    peer = 1 - member
    mesh_type = pl.DeviceIdType.MESH

    barrier = pltpu.get_barrier_semaphore()
    pl.semaphore_signal(barrier, inc=1, device_id={"seq": partner}, device_id_type=mesh_type)
    pl.semaphore_signal(barrier, inc=1, device_id={"tensor": peer}, device_id_type=mesh_type)

    @pl.when(has_up)
    def greet_above():
        pl.semaphore_signal(barrier, inc=1, device_id={"seq": above}, device_id_type=mesh_type)

    @pl.when(has_down)
    def greet_below():
        pl.semaphore_signal(barrier, inc=1, device_id={"seq": below}, device_id_type=mesh_type)

    @pl.when(inside)
    def greet_beyond():
        pl.semaphore_signal(barrier, inc=1, device_id={"seq": beyond}, device_id_type=mesh_type)

    first_loads = [
        pltpu.make_async_copy(source, place, load_sems.at[3 + k])
        for k, (source, place) in enumerate(
            ((bc_hbm, bc_in_ref), (x_hbm, x_ref))
        )
    ]
    for load in first_loads:
        load.start()
    loads = [pltpu.make_async_copy(z_hbm, z_ref, load_sems.at[0])]
    for k, (who, place) in enumerate(((peer, w_far), (member, w_near))):
        loads.append(
            pltpu.make_async_copy(
                w_ref.at[:, pl.ds(pl.multiple_of(who * out_width, 128), out_width)],
                place,
                load_sems.at[k + 1],
            )
        )
    for load in loads:
        load.start()
    ids_row = ids_row_ref[...].astype(f32)
    ids_sent[...] = jnp.broadcast_to(ids_row[:, rows - 128 :], ids_sent.shape)

    @pl.when(jnp.logical_not(has_down))
    def clear_near():
        near[...] = jnp.zeros_like(near)
        near_decay[...] = jnp.zeros_like(near_decay)

    @pl.when(jnp.logical_not(has_far))
    def clear_far():
        far[...] = jnp.zeros_like(far)

    @pl.when(jnp.logical_not(has_prev))
    def clear_rim():
        rim_x[...] = jnp.zeros_like(rim_x)
        rim_bc[...] = jnp.zeros_like(rim_bc)
        rim_ids[...] = jnp.full(rim_ids.shape, -1.0, f32)

    @pl.when(has_up & has_down)
    def meet_five():
        pl.semaphore_wait(barrier, 5)

    @pl.when(inside & jnp.logical_not(has_up & has_down))
    def meet_four():
        pl.semaphore_wait(barrier, 4)

    @pl.when(jnp.logical_not(inside))
    def meet_three():
        pl.semaphore_wait(barrier, 3)

    def lanes_of(which, k):
        return pl.ds(pl.multiple_of((which * pieces + k) * size, size), size)

    def remote(source, landing, send_sem, recv_sem, device):
        return pltpu.make_async_remote_copy(
            src_ref=source, dst_ref=landing, send_sem=send_sem, recv_sem=recv_sem,
            device_id={"seq": device}, device_id_type=mesh_type,
        )

    def decay_copy():
        return remote(own_decay, got_decay, decay_sems.at[0], decay_sems.at[1], partner)

    def pair_decay_copy():
        return remote(pair_decay, near_decay, decay_sems.at[2], decay_sems.at[3], above)

    def state_copy(k):
        return remote(
            state_ref.at[:, lanes_of(1 - parity, k)], got.at[k], got_sems.at[0, k],
            got_sems.at[1, k], partner,
        )

    def whole_copy(k):
        return remote(whole.at[k], near.at[k], whole_sems.at[0, k], whole_sems.at[1, k], above)

    def far_copy(k):
        return remote(near.at[k], far.at[k], far_sems.at[0, k], far_sems.at[1, k], above)

    def land_copy(k):
        return remote(sent.at[k], landed.at[k], land_sems.at[0, k], land_sems.at[1, k], partner)

    def halo_copies():
        last = pl.ds(rows - 16, 16)
        return [
            remote(x_hbm.at[last, :], rim_x, halo_sems.at[0, 0], halo_sems.at[1, 0], following),
            remote(bc_hbm.at[last, :], rim_bc, halo_sems.at[0, 1], halo_sems.at[1, 1], following),
            remote(ids_sent, rim_ids, halo_sems.at[0, 2], halo_sems.at[1, 2], following),
        ]

    @pl.when(has_next)
    def send_halo():
        for copy in halo_copies():
            copy.start()

    def column(row):
        return jnp.broadcast_to(row, (128, row.shape[1])).T

    logits = dt_ref[...].astype(f32) + column(rows_ref[:, HEADS_PAD : 2 * HEADS_PAD])[:heads, 0:1]
    step_size = jnp.maximum(logits, 0.0) + jnp.log1p(jnp.exp(-jnp.abs(logits)))
    rates = -jnp.exp(column(rows_ref[:, :HEADS_PAD])[:heads, 0:1]) * step_size
    spare = jnp.zeros((HEADS_PAD - heads, rows), f32)
    step_size = jnp.concatenate([step_size, spare])
    rates = jnp.concatenate([rates, spare])
    ids_ext[8 : 8 + rows, :] = column(ids_row)
    ids = ids_ext[8 : 8 + rows, :]

    for load in first_loads:
        load.wait()

    @pl.when(has_prev)
    def take_halo():
        for copy in halo_copies():
            copy.wait_recv()

    ids_ext[0:8, :] = column(rim_ids[0:1, :])[120:128, :]
    taps = conv_x_ref.shape[0]
    keeps = []
    for k in range(1, taps):
        same = ids_ext[8 - k : 8 - k + rows, :] == ids
        keeps.append(jnp.concatenate([same.astype(f32)] * (size // 128), axis=1) > 0.5)
    ext[0:8, :] = rim_bc[...].astype(f32)[8:16]
    ext[8 : 8 + rows, :] = bc_in_ref[...].astype(f32)
    mixed_bc = conv_taps(ext, conv_bc_ref[...].astype(f32), keeps, rows)
    bc_ref[...] = mixed_bc.astype(bf16)
    row_id = lax.broadcasted_iota(jnp.int32, (SPAN, SPAN), 0)
    col_id = lax.broadcasted_iota(jnp.int32, (SPAN, SPAN), 1)
    upper = (row_id <= col_id).astype(f32)
    for b in range(blocks):
        span = slice(b * SPAN, (b + 1) * SPAN)
        b_t[:, span] = mixed_bc[span, :state_size].T.astype(bf16)
        cum = jnp.dot(
            rates[:, span], upper,
            precision=lax.Precision.HIGHEST, preferred_element_type=f32,
        )
        cum_ref[:, span] = cum
        cum_t = cum.T
        step_t = step_size[:, span].T
        cum_t_ref[span, :] = cum_t
        step_t_ref[span, :] = step_t
        prior = ids_ext[8 + b * SPAN - 1 : 8 + b * SPAN, :]
        final = ids_ext[8 + (b + 1) * SPAN - 1 : 8 + (b + 1) * SPAN, :]
        gain_t_ref[span, :] = jnp.where(ids[span] == prior, jnp.exp(cum_t), 0.0)
        tail_t[span, :] = jnp.where(
            ids[span] == final, jnp.exp(cum_t[SPAN - 1 : SPAN] - cum_t), 0.0
        ) * step_t
    decay = gain_t_ref[SPAN - 1 : SPAN, :]
    for b in range(1, blocks):
        decay = decay * gain_t_ref[(b + 1) * SPAN - 1 : (b + 1) * SPAN, :]
    own_decay[...] = jnp.broadcast_to(decay, own_decay.shape)
    decay_copy().start()

    def decay_row(ref, k):
        turn = lax.rem(HEADS_PAD - (parity * pieces + k) * per_group, HEADS_PAD)
        turn = lax.rem(turn + HEADS_PAD, HEADS_PAD)
        return spread_heads(pltpu.roll(ref[...], turn, 1), head_size, size)[0:1]

    def first_state(k):
        mine = state_ref[:, lanes_of(parity, k)].astype(f32)
        theirs = got[k].astype(f32)
        return jnp.where(odd, theirs, mine), jnp.where(odd, mine, theirs)

    def states(j, unused):
        c = lax.rem(j + (1 - parity) * pieces, groups)
        lanes = pl.ds(pl.multiple_of(c * size, size), size)
        turn = lax.rem(HEADS_PAD - c * per_group, HEADS_PAD)
        ext[0:8, :] = rim_x[:, lanes].astype(f32)[8:16]
        ext[8 : 8 + rows, :] = x_ref[:, lanes].astype(f32)
        mixed = conv_taps(ext, conv_x_ref[:, lanes].astype(f32), keeps, rows).astype(bf16)
        mixed_ref[:, lanes] = mixed
        weight = spread_heads(pltpu.roll(tail_t[...], turn, 1), head_size, size)
        weighted = (mixed.astype(f32) * weight).astype(bf16)
        running = None
        for b in range(blocks):
            span = slice(b * SPAN, (b + 1) * SPAN)
            fresh = jnp.dot(b_t[:, span], weighted[span], preferred_element_type=f32)
            ends = gain_t_ref[(b + 1) * SPAN - 8 : (b + 1) * SPAN, :]
            block_decay = spread_heads(pltpu.roll(ends, turn, 1), head_size, size)[7:8]
            if b + 1 < blocks:
                fresh_ref[b, :, lanes] = fresh
                decay_ref[b, :, lanes] = jnp.broadcast_to(block_decay, (8, size))
            running = fresh if b == 0 else block_decay * running + fresh
        state_ref[:, lanes] = running.astype(bf16)

        @pl.when(j < pieces)
        def send_state():
            state_copy(j).start()

        @pl.when(j == pieces)
        def take_decay():
            decay_copy().wait_recv()
            pair_decay[...] = own_decay[...] * got_decay[...]

            @pl.when(has_up)
            def pass_decay():
                pair_decay_copy().start()

        @pl.when(j >= pieces)
        def join():
            k = j - pieces
            state_copy(k).wait_recv()

            @pl.when(has_up)
            def send_whole():
                first, second = first_state(k)
                odd_decay = jnp.where(odd, decay_row(own_decay, k), decay_row(got_decay, k))
                whole[k] = (second + odd_decay * first).astype(bf16)
                whole_copy(k).start()

        return unused

    lax.fori_loop(0, groups, states, 0)
    ids_wide = jnp.concatenate([ids] * (SPAN // 128), axis=1)
    skip_tile = jnp.broadcast_to(rows_ref[:, 2 * HEADS_PAD : 3 * HEADS_PAD], (8, HEADS_PAD))
    for b in range(blocks):
        span = slice(b * SPAN, (b + 1) * SPAN)
        raw = lax.dot_general(
            bc_ref[span, state_size:], bc_ref[span, :state_size], (((1,), (1,)), ((), ())),
            preferred_element_type=f32,
        )
        same = (ids_wide[span] == ids_row[:, span]) & (col_id <= row_id)
        scores[b] = jnp.where(same, raw, 0.0)

    def mix(c, b):
        lanes = pl.ds(pl.multiple_of(c * size, size), size)
        span = pl.ds(b * SPAN, SPAN)
        turn = lax.rem(HEADS_PAD - c * per_group, HEADS_PAD)
        cum_t = pltpu.roll(cum_t_ref[span, :], turn, 1)
        steps = spread_heads(pltpu.roll(step_t_ref[span, :], turn, 1), head_size, size)
        x = mixed_ref[span, lanes].astype(f32)
        stepped = (x * steps).astype(bf16)
        skip = spread_heads(pltpu.roll(skip_tile, turn, 1), head_size, size)[0:1]
        tops, bottoms = [], []
        for k in range(per_group):
            own = slice(k * head_size, (k + 1) * head_size)
            column = cum_t[:, k : k + 1]
            row = cum_ref[pl.ds(c * per_group + k, 1), span]
            top = scores[b, :half, :half] * jnp.exp(
                jnp.minimum(column[:half] - row[:, :half], 0.0)
            )
            bottom = scores[b, half:, :] * jnp.exp(jnp.minimum(column[half:] - row, 0.0))
            tops.append(
                jnp.dot(top.astype(bf16), stepped[:half, own], preferred_element_type=f32)
            )
            bottoms.append(
                jnp.dot(bottom.astype(bf16), stepped[:, own], preferred_element_type=f32)
            )
        both = jnp.concatenate(
            [jnp.concatenate(tops, axis=1), jnp.concatenate(bottoms, axis=1)], axis=0
        )
        part_ref[span, lanes] = both + skip * x

    def step(j, unused):
        @pl.when(j < pieces)
        def forward():
            @pl.when(has_down)
            def take_near():
                whole_copy(j).wait_recv()

                @pl.when(has_up)
                def pass_near():
                    far_copy(j).start()

        @pl.when(j >= pieces)
        def close():
            k = j - pieces

            @pl.when((k == 0) & has_down)
            def take_near_decay():
                pair_decay_copy().wait_recv()

            @pl.when(has_far)
            def take_far():
                far_copy(k).wait_recv()

            entering = near[k].astype(f32) + decay_row(near_decay, k) * far[k].astype(f32)
            first, _ = first_state(k)
            even_decay = jnp.where(odd, decay_row(got_decay, k), decay_row(own_decay, k))
            later = first + even_decay * entering
            enter_ref[:, lanes_of(parity, k)] = jnp.where(odd, later, entering).astype(bf16)
            sent[k] = jnp.where(odd, entering, later).astype(bf16)
            land_copy(k).start()

        mix(j, 0)
        return unused

    lax.fori_loop(0, groups, step, 0)
    for k in range(pieces):
        land_copy(k).wait_recv()
        enter_ref[:, lanes_of(1 - parity, k)] = landed[k]
    loads[0].wait()
    count = rows // chunk
    per_block = SPAN // chunk
    gate_size = 512
    gate_heads = gate_size // head_size
    tile = 256 if out_width % 256 == 0 else 128

    def product(here, weights, store):
        def columns(j, unused):
            lanes = pl.ds(pl.multiple_of(j * tile, tile), tile)
            store(
                lanes,
                jnp.dot(
                    scaled[here, :], weights[:, lanes],
                    preferred_element_type=jnp.float32,
                ).astype(jnp.bfloat16),
            )
            return unused

        lax.fori_loop(0, out_width // tile, columns, 0)

    copies = []
    for q in range(count):
        b, within = q // per_block, q % per_block
        here = slice(q * chunk, (q + 1) * chunk)

        def group(c, squares):
            lanes = pl.ds(pl.multiple_of(c * gate_size, gate_size), gate_size)
            turn = lax.rem(HEADS_PAD - c * gate_heads, HEADS_PAD)
            if q == 0:
                state[:, lanes] = enter_ref[:, lanes]
            elif within == 0:
                state[:, lanes] = (
                    decay_ref[b - 1, 0:1, lanes] * state[:, lanes].astype(jnp.float32)
                    + fresh_ref[b - 1, :, lanes]
                ).astype(jnp.bfloat16)
            gains = rows_ref[:, pl.ds(pl.multiple_of(3 * HEADS_PAD + c * gate_size, 128), gate_size)]
            gain = spread_heads(pltpu.roll(gain_t_ref[here, :], turn, 1), head_size, gate_size)
            reached = jnp.dot(
                bc_ref[here, state_size:], state[:, lanes], preferred_element_type=jnp.float32
            )
            y = part_ref[here, lanes] + gain * reached
            y = y.astype(jnp.bfloat16).astype(jnp.float32)
            gated = y * silu(z_ref[here, lanes].astype(jnp.float32))
            scaled[here, lanes] = (gated * gains).astype(jnp.bfloat16)
            square = gated * gated
            for k in range(gate_size // 128):
                squares = squares + square[:, k * 128 : (k + 1) * 128]
            return squares

        if b > 0 and within == 0:

            def mix_later(c, unused, b=b):
                mix(c, b)
                return unused

            lax.fori_loop(0, groups, mix_later, 0)

        squares = lax.fori_loop(0, width // gate_size, group, jnp.zeros((chunk, 128), jnp.float32))
        row = jnp.sum(squares.T, axis=0, keepdims=True)
        row_sends[q] = jnp.broadcast_to(row, (8, chunk))
        if q == 0:
            loads[1].wait()

        def put(lanes, value):
            sends[q, :, lanes] = value

        product(here, w_far, put)
        pair = [
            pltpu.make_async_remote_copy(
                src_ref=source.at[q],
                dst_ref=landing.at[q],
                send_sem=out_sems.at[q],
                recv_sem=in_sems.at[q],
                device_id={"tensor": peer},
                device_id_type=pl.DeviceIdType.MESH,
            )
            for source, landing, out_sems, in_sems in (
                (row_sends, row_gots, row_send_sems, row_got_sems),
                (sends, gots, send_sems, got_out_sems),
            )
        ]
        for copy in pair:
            copy.start()
        copies.append(pair)

    loads[2].wait()

    def keep(lanes, value):
        sums[:, lanes] = value

    product(slice(0, rows), w_near, keep)
    for q in range(count):
        here = slice(q * chunk, (q + 1) * chunk)
        for copy in copies[q]:
            copy.wait_recv()
        row = row_sends[q, 0:1, :] + row_gots[q, 0:1, :]
        inv_row = lax.rsqrt(row / (2 * width) + 1e-05)
        inv = jnp.broadcast_to(inv_row, (128, chunk)).T
        for j in range(out_width // 128):
            lanes = slice(j * 128, (j + 1) * 128)
            total = sums[here, lanes].astype(jnp.float32) + gots[q, :, lanes].astype(jnp.float32)
            out_ref[here, lanes] = (total * inv).astype(jnp.bfloat16)
    for pair in copies:
        for copy in pair:
            copy.wait_send()

    @pl.when(has_next)
    def finish_halo():
        for copy in halo_copies():
            copy.wait_send()

    decay_copy().wait_send()
    for k in range(pieces):
        state_copy(k).wait_send()
        land_copy(k).wait_send()

    @pl.when(has_up)
    def finish():
        pair_decay_copy().wait_send()
        for k in range(pieces):
            whole_copy(k).wait_send()

    @pl.when(has_up & has_down)
    def finish_far():
        for k in range(pieces):
            far_copy(k).wait_send()


def call(kernel, out_shape, scratch, flops, moved, *operands):
    return pl.pallas_call(
        kernel,
        out_shape=out_shape,
        in_specs=[pl.BlockSpec(memory_space=pltpu.VMEM)] * len(operands),
        out_specs=jax.tree.map(lambda _: pl.BlockSpec(memory_space=pltpu.VMEM), out_shape),
        scratch_shapes=scratch,
        compiler_params=pltpu.CompilerParams(vmem_limit_bytes=VMEM_BYTES),
        cost_estimate=pl.CostEstimate(flops=flops, bytes_accessed=moved, transcendentals=0),
    )(*operands)


def split_message(message):
    state_size = message.shape[0] - EXTRA
    wide = message.astype(jnp.float32)
    return wide[:state_size], wide[state_size : state_size + 1] + wide[state_size + 8 : state_size + 9]


def merge(near, far):
    near_state, near_decay = near
    far_state, far_decay = far
    return near_state + near_decay * far_state, near_decay * far_decay


def pack_message(pair):
    state, decay = pair
    width = state.shape[1]
    high = decay.astype(jnp.bfloat16)
    low = (decay - high.astype(jnp.float32)).astype(jnp.bfloat16)
    return jnp.concatenate(
        [
            state.astype(jnp.bfloat16),
            jnp.broadcast_to(high, (8, width)),
            jnp.broadcast_to(low, (8, width)),
        ]
    )


def pass_state(message):
    count = lax.axis_size("seq")
    odd = (lax.axis_index("seq") % 2) == 1
    other = lax.ppermute(message, "seq", [(i, i ^ 1) for i in range(count)])
    first = split_message(jnp.where(odd, other, message))
    second = split_message(jnp.where(odd, message, other))
    entering = shifted(pack_message(merge(second, first)), "seq", 2)
    reach = 1
    while reach < count // 4:
        farther = shifted(entering, "seq", 2 * reach)
        joined = merge(split_message(entering), split_message(farther))
        reach *= 2
        if reach < count // 4:
            entering = pack_message(joined)
        else:
            entering = joined
    if reach == 1:
        entering = split_message(entering)
    alone = split_message(other)
    return jnp.where(odd, merge(alone, entering)[0], entering[0])


def local(
    x_stream,
    bc_stream,
    z_gate,
    dt_stream,
    doc_ids,
    conv_x,
    conv_bc,
    a_log,
    dt_bias,
    d_skip,
    norm_gain,
    w_out,
):
    rows, width = x_stream.shape
    heads = dt_stream.shape[0]
    head_size = width // heads
    bc_width = bc_stream.shape[1]
    state_size = bc_width // 2
    taps = conv_x.shape[0]
    blocks = rows // SPAN
    edge = rows - taps + 1
    f32, bf16 = jnp.float32, jnp.bfloat16
    shape = jax.ShapeDtypeStruct
    out_width = w_out.shape[1] // lax.axis_size("tensor")
    if (
        lax.axis_size("seq") == 8
        and lax.axis_size("tensor") == 2
        and width % 512 == 0
        and width >= 1536
        and out_width % 128 == 0
        and bc_width == group_lanes(width)
        and heads <= HEADS_PAD
        and heads % 8 == 0
    ):
        vmem = pl.BlockSpec(memory_space=pltpu.VMEM)
        hbm = pl.BlockSpec(memory_space=pl.ANY)
        pieces = width // 512
        chunk = 128
        count = rows // chunk
        piece = (pieces, state_size, 256)

        def padded(values):
            return jnp.pad(values, (0, HEADS_PAD - heads))

        return pl.pallas_call(
            functools.partial(fused_kernel, head_size, chunk),
            out_shape=shape((rows, out_width), bf16),
            in_specs=[hbm] * 4 + [vmem] * 5,
            out_specs=vmem,
            scratch_shapes=[
                pltpu.VMEM((rows, width), bf16),
                pltpu.VMEM((rows, bc_width), bf16),
                pltpu.VMEM((rows + 8, 256), f32),
                pltpu.VMEM((rows + 8, 128), f32),
                pltpu.VMEM((16, width), bf16),
                pltpu.VMEM((16, bc_width), bf16),
                pltpu.VMEM((8, 128), f32),
                pltpu.VMEM((8, 128), f32),
                pltpu.VMEM((rows, width), bf16),
                pltpu.VMEM((rows, bc_width), bf16),
                pltpu.VMEM((HEADS_PAD, rows), f32),
                pltpu.VMEM((rows, HEADS_PAD), f32),
                pltpu.VMEM((rows, HEADS_PAD), f32),
                pltpu.VMEM((rows, HEADS_PAD), f32),
                pltpu.VMEM((rows, HEADS_PAD), f32),
                pltpu.VMEM((state_size, rows), bf16),
                pltpu.VMEM((blocks, state_size, width), f32),
                pltpu.VMEM((blocks, 8, width), f32),
                pltpu.VMEM((state_size, width), bf16),
                pltpu.VMEM((rows, width), f32),
                pltpu.VMEM((state_size, width), bf16),
                pltpu.VMEM((blocks, SPAN, SPAN), f32),
            ]
            + [pltpu.VMEM(piece, bf16)] * 6
            + [pltpu.VMEM((8, HEADS_PAD), f32)] * 4
            + [
                pltpu.VMEM((rows, width), bf16),
                pltpu.VMEM((width, out_width), bf16),
                pltpu.VMEM((width, out_width), bf16),
                pltpu.VMEM((rows, width), bf16),
                pltpu.VMEM((state_size, width), bf16),
                pltpu.VMEM((rows, out_width), bf16),
                pltpu.VMEM((count, chunk, out_width), bf16),
                pltpu.VMEM((count, chunk, out_width), bf16),
                pltpu.VMEM((count, 8, chunk), f32),
                pltpu.VMEM((count, 8, chunk), f32),
                pltpu.SemaphoreType.DMA((2, 3)),
                pltpu.SemaphoreType.DMA((5,)),
                pltpu.SemaphoreType.DMA((4,)),
            ]
            + [pltpu.SemaphoreType.DMA((2, pieces))] * 4
            + [pltpu.SemaphoreType.DMA((count,))] * 4,
            compiler_params=pltpu.CompilerParams(
                collective_id=0, has_side_effects=True, vmem_limit_bytes=FUSED_VMEM_BYTES
            ),
            cost_estimate=pl.CostEstimate(
                flops=2 * rows * width * w_out.shape[1],
                bytes_accessed=2 * width * w_out.shape[1],
                transcendentals=0,
            ),
        )(
            x_stream, bc_stream, z_gate, w_out, dt_stream, doc_ids[None, :], conv_x, conv_bc,
            jnp.concatenate(
                [padded(a_log), padded(dt_bias), padded(d_skip), norm_gain]
            )[None, :],
        )
    own_ids = doc_ids.astype(f32)
    tail_ids = jnp.broadcast_to(own_ids[edge:].astype(bf16)[:, None], (taps - 1, 128))
    rim = shifted(
        jnp.concatenate([x_stream[edge:], bc_stream[edge:], tail_ids], axis=1), "seq", 1
    )
    step = jax.nn.softplus(dt_stream.astype(f32) + dt_bias[:, None])
    rate = -jnp.exp(a_log)[:, None] * step
    step = jnp.pad(step, ((0, HEADS_PAD - heads), (0, 0)))
    rate = jnp.pad(rate, ((0, HEADS_PAD - heads), (0, 0)))
    rim_wide = jnp.pad(rim.astype(f32), ((8 - taps + 1, 0), (0, 0)))
    rim_ids = jnp.where(lax.axis_index("seq") == 0, -1.0, rim[:, width + bc_width].astype(f32))
    ext_ids = jnp.concatenate([rim_ids, own_ids])
    block_ids = own_ids.reshape(blocks, SPAN)
    prior = jnp.concatenate([ext_ids[taps - 2][None], own_ids[SPAN - 1 :: SPAN][: blocks - 1]])
    columns = [(ext_ids[taps - 1 - k : taps - 1 - k + rows] == own_ids) for k in range(1, taps)]
    columns.append((block_ids == prior[:, None]).reshape(rows))
    columns.append((block_ids == block_ids[:, -1:]).reshape(rows))
    flags = jnp.stack([c.astype(f32) for c in columns], axis=1)

    mixed, mixed_bc, cum, cum_t, step_t, gain_t, fresh, decay, message = call(
        functools.partial(states_kernel, head_size),
        (
            shape((rows, width), bf16),
            shape((rows, bc_width), bf16),
            shape((HEADS_PAD, rows), f32),
            shape((rows, HEADS_PAD), f32),
            shape((rows, HEADS_PAD), f32),
            shape((rows, HEADS_PAD), f32),
            shape((blocks, state_size, width), f32),
            shape((blocks, 8, width), f32),
            shape((state_size + EXTRA, width), bf16),
        ),
        [
            pltpu.VMEM((rows + 8, max(bc_width, group_lanes(width))), f32),
            pltpu.VMEM((rows, HEADS_PAD), f32),
            pltpu.VMEM((state_size, rows), bf16),
        ],
        2 * rows * state_size * width,
        8 * rows * width,
        x_stream, rim_wide[:, :width], bc_stream, rim_wide[:, width : width + bc_width], step, rate,
        flags, conv_x.astype(f32), conv_bc.astype(f32),
    )
    skip_row = jnp.repeat(d_skip, head_size)[None, :]
    parts = []
    for b in range(blocks):
        span = slice(b * SPAN, (b + 1) * SPAN)
        parts.append(
            call(
                functools.partial(mix_kernel, head_size),
                shape((SPAN, width), f32),
                [pltpu.VMEM((SPAN, SPAN), f32)],
                2 * SPAN * SPAN * width * 16,
                8 * SPAN * width,
                mixed[span], mixed_bc[span], cum[:, span], cum_t[span], step_t[span],
                own_ids[span][:, None], own_ids[span][None, :], skip_row,
            )
        )
    state = pass_state(message)

    members = lax.axis_size("tensor")
    member = lax.axis_index("tensor")
    pieces = []
    for b in range(blocks):
        span = slice(b * SPAN, (b + 1) * SPAN)
        scaled, squares = call(
            functools.partial(gate_kernel, head_size),
            (shape((SPAN, width), bf16), shape((SPAN, 128), f32)),
            [],
            2 * SPAN * state_size * width,
            12 * SPAN * width,
            state.astype(bf16), mixed_bc[span], gain_t[span], parts[b], z_gate[span],
            norm_gain[None, :],
        )
        if b + 1 < blocks:
            state = decay[b, 0:1] * state + fresh[b]
        product = jnp.dot(scaled, w_out, preferred_element_type=f32).astype(bf16)
        total = lax.dynamic_slice_in_dim(product, member * out_width, out_width, 1).astype(f32)
        square = jnp.sum(squares, axis=1, keepdims=True)
        high = square.astype(bf16)
        low = (square - high.astype(f32)).astype(bf16)
        lane = lax.broadcasted_iota(jnp.int32, (SPAN, 128), 1)
        aside = jnp.where(lane == 0, high, jnp.where(lane == 1, low, jnp.zeros_like(low)))
        for distance in range(1, members):
            target = (member + distance) % members
            block = lax.dynamic_slice_in_dim(product, target * out_width, out_width, 1)
            route = [(i, (i + distance) % members) for i in range(members)]
            got = lax.ppermute(jnp.concatenate([block, aside], axis=1), "tensor", route)
            total = total + got[:, :out_width].astype(f32)
            square = square + jnp.sum(got[:, out_width : out_width + 2].astype(f32), axis=1, keepdims=True)
        inv_norm = lax.rsqrt(square / (width * members) + 1e-05)
        pieces.append((total * inv_norm).astype(bf16))
    return jnp.concatenate(pieces)


def solution(mesh):
    return jax.shard_map(
        local,
        mesh=mesh,
        in_specs=(
            P(("dp", "seq"), "tensor"),
            P(("dp", "seq"), None),
            P(("dp", "seq"), "tensor"),
            P("tensor", ("dp", "seq")),
            P(("dp", "seq")),
            P(None, "tensor"),
            P(),
            P("tensor"),
            P("tensor"),
            P("tensor"),
            P("tensor"),
            P("tensor", None),
        ),
        out_specs=P(("dp", "seq"), "tensor"),
        check_vma=False,
    )
```

```python
import functools

import jax
import jax.numpy as jnp
from jax import lax
from jax.experimental import pallas as pl
from jax.experimental.pallas import tpu as pltpu
from jax.sharding import PartitionSpec as P

SPAN = 256
HEADS_PAD = 128
EXTRA = 16
VMEM_BYTES = 48 * 1024 * 1024
FUSED_VMEM_BYTES = 58 * 1024 * 1024


def shifted(block, axis, distance):
    count = lax.axis_size(axis)
    return lax.ppermute(block, axis, [(i, i + distance) for i in range(count - distance)])


def group_lanes(width):
    return 256 if width % 256 == 0 else 128


def silu(v):
    scaled = 0.5 * v
    return scaled + scaled * jnp.tanh(scaled)


def spread_heads(columns, width, lanes):
    rows = columns.shape[0]
    lane = lax.broadcasted_iota(jnp.int32, (rows, 128), 1)
    per_tile = 128 // width
    tiles = []
    for tile in range(lanes // 128):
        value = jnp.broadcast_to(columns[:, tile * per_tile : tile * per_tile + 1], (rows, 128))
        for k in range(1, per_tile):
            head = tile * per_tile + k
            value = jnp.where(
                lane >= k * width, jnp.broadcast_to(columns[:, head : head + 1], (rows, 128)), value
            )
        tiles.append(value)
    return jnp.concatenate(tiles, axis=1)


def conv_taps(ext, weights, keeps, rows):
    wide = weights.shape[1]
    total = weights[0:1] * ext[pl.ds(8, rows), :wide]
    for k in range(1, weights.shape[0]):
        total = total + jnp.where(keeps[k - 1][:, :wide], weights[k : k + 1] * ext[pl.ds(8 - k, rows), :wide], 0.0)
    return silu(total)


def states_kernel(
    head_size,
    x_ref, rim_x_ref, bc_ref, rim_bc_ref, step_ref, rate_ref, flags_ref, conv_x_ref, conv_bc_ref,
    mixed_ref, bc_out_ref, cum_ref, cum_t_ref, step_t_ref, gain_t_ref, fresh_ref, decay_ref, msg_ref,
    ext, tail_t, b_t,
):
    rows, width = x_ref.shape
    blocks = rows // SPAN
    size = group_lanes(width)
    per_group = size // head_size
    state_size = bc_ref.shape[1] // 2
    flags = flags_ref[...]
    taps = conv_x_ref.shape[0]
    keeps = [
        jnp.broadcast_to(flags[:, k : k + 1], (rows, ext.shape[1])) > 0.5 for k in range(taps - 1)
    ]
    carried = jnp.broadcast_to(flags[:, 3:4], (rows, HEADS_PAD)) > 0.5
    in_tail = jnp.broadcast_to(flags[:, 4:5], (rows, HEADS_PAD)) > 0.5

    ext[0:8, :] = rim_bc_ref[...]
    ext[8 : 8 + rows, :] = bc_ref[...].astype(jnp.float32)
    mixed_bc = conv_taps(ext, conv_bc_ref[...], keeps, rows)
    bc_out_ref[...] = mixed_bc.astype(jnp.bfloat16)
    row_id = lax.broadcasted_iota(jnp.int32, (SPAN, SPAN), 0)
    col_id = lax.broadcasted_iota(jnp.int32, (SPAN, SPAN), 1)
    upper = (row_id <= col_id).astype(jnp.float32)
    for b in range(blocks):
        span = slice(b * SPAN, (b + 1) * SPAN)
        b_t[:, span] = mixed_bc[span, :state_size].T.astype(jnp.bfloat16)
        cum = jnp.dot(
            rate_ref[:, span], upper,
            precision=lax.Precision.HIGHEST, preferred_element_type=jnp.float32,
        )
        cum_ref[:, span] = cum
        cum_t = cum.T
        step_t = step_ref[:, span].T
        cum_t_ref[span, :] = cum_t
        step_t_ref[span, :] = step_t
        gain_t_ref[span, :] = jnp.where(carried[span], jnp.exp(cum_t), 0.0)
        tail_t[span, :] = jnp.where(
            in_tail[span], jnp.exp(cum_t[SPAN - 1 : SPAN] - cum_t), 0.0
        ) * step_t

    def group(c, unused):
        lanes = pl.ds(pl.multiple_of(c * size, size), size)
        turn = lax.rem(HEADS_PAD - c * per_group, HEADS_PAD)
        ext[0:8, :size] = rim_x_ref[:, lanes]
        ext[8 : 8 + rows, :size] = x_ref[:, lanes].astype(jnp.float32)
        mixed = conv_taps(ext, conv_x_ref[:, lanes], keeps, rows).astype(jnp.bfloat16)
        mixed_ref[:, lanes] = mixed
        weight = spread_heads(pltpu.roll(tail_t[...], turn, 1), head_size, size)
        weighted = (mixed.astype(jnp.float32) * weight).astype(jnp.bfloat16)
        running = None
        through = None
        for b in range(blocks):
            span = slice(b * SPAN, (b + 1) * SPAN)
            fresh = jnp.dot(b_t[:, span], weighted[span], preferred_element_type=jnp.float32)
            ends = gain_t_ref[(b + 1) * SPAN - 8 : (b + 1) * SPAN, :]
            decay = spread_heads(pltpu.roll(ends, turn, 1), head_size, size)[7:8]
            fresh_ref[b, :, lanes] = fresh
            decay_ref[b, :, lanes] = jnp.broadcast_to(decay, (8, size))
            running = fresh if b == 0 else decay * running + fresh
            through = decay if b == 0 else through * decay
        msg_ref[0:state_size, lanes] = running.astype(jnp.bfloat16)
        high = through.astype(jnp.bfloat16)
        low = through - high.astype(jnp.float32)
        both = jnp.concatenate(
            [
                jnp.broadcast_to(high.astype(jnp.float32), (8, size)),
                jnp.broadcast_to(low, (8, size)),
            ]
        )
        msg_ref[state_size : state_size + EXTRA, lanes] = both.astype(jnp.bfloat16)
        return unused

    lax.fori_loop(0, width // size, group, 0)


def mix_kernel(
    head_size,
    mixed_ref, bc_ref, cum_ref, cum_t_ref, step_t_ref, ids_col_ref, ids_row_ref, skip_ref,
    out_ref,
    scores,
):
    width = mixed_ref.shape[1]
    size = group_lanes(width)
    per_group = size // head_size
    state_size = bc_ref.shape[1] // 2
    half = SPAN // 2
    row_id = lax.broadcasted_iota(jnp.int32, (SPAN, SPAN), 0)
    col_id = lax.broadcasted_iota(jnp.int32, (SPAN, SPAN), 1)
    raw = lax.dot_general(
        bc_ref[:, state_size:], bc_ref[:, :state_size], (((1,), (1,)), ((), ())),
        preferred_element_type=jnp.float32,
    )
    same = (ids_col_ref[...] == ids_row_ref[...]) & (col_id <= row_id)
    scores[...] = jnp.where(same, raw, 0.0)

    def group(c, unused):
        lanes = pl.ds(pl.multiple_of(c * size, size), size)
        turn = lax.rem(HEADS_PAD - c * per_group, HEADS_PAD)
        cum_t = pltpu.roll(cum_t_ref[...], turn, 1)
        steps = spread_heads(pltpu.roll(step_t_ref[...], turn, 1), head_size, size)
        x = mixed_ref[:, lanes].astype(jnp.float32)
        stepped = (x * steps).astype(jnp.bfloat16)
        tops, bottoms = [], []
        for k in range(per_group):
            own = slice(k * head_size, (k + 1) * head_size)
            column = cum_t[:, k : k + 1]
            row = cum_ref[pl.ds(c * per_group + k, 1), :]
            top = scores[:half, :half] * jnp.exp(jnp.minimum(column[:half] - row[:, :half], 0.0))
            bottom = scores[half:, :] * jnp.exp(jnp.minimum(column[half:] - row, 0.0))
            tops.append(
                jnp.dot(
                    top.astype(jnp.bfloat16), stepped[:half, own],
                    preferred_element_type=jnp.float32,
                )
            )
            bottoms.append(
                jnp.dot(
                    bottom.astype(jnp.bfloat16), stepped[:, own],
                    preferred_element_type=jnp.float32,
                )
            )
        skip = skip_ref[:, lanes]
        out_ref[:half, lanes] = jnp.concatenate(tops, axis=1) + skip * x[:half]
        out_ref[half:, lanes] = jnp.concatenate(bottoms, axis=1) + skip * x[half:]
        return unused

    lax.fori_loop(0, width // size, group, 0)


def gate_kernel(
    head_size,
    state_ref, bc_ref, gain_t_ref, part_ref, z_ref, norm_ref,
    out_ref, squares_ref,
):
    width = part_ref.shape[1]
    size = group_lanes(width)
    per_group = size // head_size
    state_size = bc_ref.shape[1] // 2
    c_vals = bc_ref[:, state_size:]

    def group(c, squares):
        lanes = pl.ds(pl.multiple_of(c * size, size), size)
        turn = lax.rem(HEADS_PAD - c * per_group, HEADS_PAD)
        gain = spread_heads(pltpu.roll(gain_t_ref[...], turn, 1), head_size, size)
        reached = jnp.dot(c_vals, state_ref[:, lanes], preferred_element_type=jnp.float32)
        y = (part_ref[:, lanes] + gain * reached).astype(jnp.bfloat16).astype(jnp.float32)
        gated = y * silu(z_ref[:, lanes].astype(jnp.float32))
        out_ref[:, lanes] = (gated * norm_ref[:, lanes]).astype(jnp.bfloat16)
        square = gated * gated
        for tile in range(size // 128):
            squares = squares + square[:, tile * 128 : (tile + 1) * 128]
        return squares

    squares_ref[...] = lax.fori_loop(
        0, width // size, group, jnp.zeros((SPAN, 128), jnp.float32)
    )


def fused_kernel(
    head_size, chunk,
    x_hbm, bc_hbm, z_hbm, w_ref, dt_ref, ids_row_ref, conv_x_ref, conv_bc_ref, rows_ref,
    out_ref,
    x_ref, bc_in_ref,
    ext, ids_ext, rim_x, rim_bc, rim_ids, ids_sent, mixed_ref, bc_ref, cum_ref, cum_t_ref,
    step_t_ref, gain_t_ref, tail_t, b_t, fresh_ref, decay_ref, state_ref, part_ref, enter_ref,
    scores, got, whole, near, far, sent, landed, own_decay, got_decay, pair_decay, near_decay,
    z_ref, w_far, w_near, scaled, state, sums, sends, gots, row_sends, row_gots,
    halo_sems, load_sems, decay_sems, got_sems, whole_sems, far_sems, land_sems,
    send_sems, got_out_sems, row_send_sems, row_got_sems,
):
    rows, width = x_ref.shape
    size = group_lanes(width)
    per_group = size // head_size
    groups = width // size
    pieces = groups // 2
    blocks = rows // SPAN
    state_size = bc_in_ref.shape[1] // 2
    half = SPAN // 2
    out_width = out_ref.shape[1]
    heads = dt_ref.shape[0]
    f32, bf16 = jnp.float32, jnp.bfloat16
    seq_count = lax.axis_size("seq")
    me = lax.axis_index("seq")
    parity = lax.rem(me, 2)
    odd = parity == 1
    partner = me + 1 - 2 * parity
    beyond = lax.rem(me + seq_count - 1 + 2 * parity, seq_count)
    has_up = me < seq_count - 2
    has_down = me >= 2
    has_far = me >= 4
    has_next = me < seq_count - 1
    has_prev = me >= 1
    inside = has_next & has_prev
    above = lax.rem(me + 2, seq_count)
    below = lax.rem(me + seq_count - 2, seq_count)
    following = lax.rem(me + 1, seq_count)
    member = lax.axis_index("tensor")
    peer = 1 - member
    mesh_type = pl.DeviceIdType.MESH

    barrier = pltpu.get_barrier_semaphore()
    pl.semaphore_signal(barrier, inc=1, device_id={"seq": partner}, device_id_type=mesh_type)
    pl.semaphore_signal(barrier, inc=1, device_id={"tensor": peer}, device_id_type=mesh_type)

    @pl.when(has_up)
    def greet_above():
        pl.semaphore_signal(barrier, inc=1, device_id={"seq": above}, device_id_type=mesh_type)

    @pl.when(has_down)
    def greet_below():
        pl.semaphore_signal(barrier, inc=1, device_id={"seq": below}, device_id_type=mesh_type)

    @pl.when(inside)
    def greet_beyond():
        pl.semaphore_signal(barrier, inc=1, device_id={"seq": beyond}, device_id_type=mesh_type)

    first_loads = [
        pltpu.make_async_copy(source, place, load_sems.at[3 + k])
        for k, (source, place) in enumerate(
            ((bc_hbm, bc_in_ref), (x_hbm, x_ref))
        )
    ]
    for load in first_loads:
        load.start()
    loads = [pltpu.make_async_copy(z_hbm, z_ref, load_sems.at[0])]
    for k, (who, place) in enumerate(((peer, w_far), (member, w_near))):
        loads.append(
            pltpu.make_async_copy(
                w_ref.at[:, pl.ds(pl.multiple_of(who * out_width, 128), out_width)],
                place,
                load_sems.at[k + 1],
            )
        )
    for load in loads:
        load.start()
    ids_row = ids_row_ref[...].astype(f32)
    ids_sent[...] = jnp.broadcast_to(ids_row[:, rows - 128 :], ids_sent.shape)

    @pl.when(jnp.logical_not(has_down))
    def clear_near():
        near[...] = jnp.zeros_like(near)
        near_decay[...] = jnp.zeros_like(near_decay)

    @pl.when(jnp.logical_not(has_far))
    def clear_far():
        far[...] = jnp.zeros_like(far)

    @pl.when(jnp.logical_not(has_prev))
    def clear_rim():
        rim_x[...] = jnp.zeros_like(rim_x)
        rim_bc[...] = jnp.zeros_like(rim_bc)
        rim_ids[...] = jnp.full(rim_ids.shape, -1.0, f32)

    @pl.when(has_up & has_down)
    def meet_five():
        pl.semaphore_wait(barrier, 5)

    @pl.when(inside & jnp.logical_not(has_up & has_down))
    def meet_four():
        pl.semaphore_wait(barrier, 4)

    @pl.when(jnp.logical_not(inside))
    def meet_three():
        pl.semaphore_wait(barrier, 3)

    def lanes_of(which, k):
        return pl.ds(pl.multiple_of((which * pieces + k) * size, size), size)

    def remote(source, landing, send_sem, recv_sem, device):
        return pltpu.make_async_remote_copy(
            src_ref=source, dst_ref=landing, send_sem=send_sem, recv_sem=recv_sem,
            device_id={"seq": device}, device_id_type=mesh_type,
        )

    def decay_copy():
        return remote(own_decay, got_decay, decay_sems.at[0], decay_sems.at[1], partner)

    def pair_decay_copy():
        return remote(pair_decay, near_decay, decay_sems.at[2], decay_sems.at[3], above)

    def state_copy(k):
        return remote(
            state_ref.at[:, lanes_of(1 - parity, k)], got.at[k], got_sems.at[0, k],
            got_sems.at[1, k], partner,
        )

    def whole_copy(k):
        return remote(whole.at[k], near.at[k], whole_sems.at[0, k], whole_sems.at[1, k], above)

    def far_copy(k):
        return remote(near.at[k], far.at[k], far_sems.at[0, k], far_sems.at[1, k], above)

    def land_copy(k):
        return remote(sent.at[k], landed.at[k], land_sems.at[0, k], land_sems.at[1, k], partner)

    def halo_copies():
        last = pl.ds(rows - 16, 16)
        return [
            remote(x_hbm.at[last, :], rim_x, halo_sems.at[0, 0], halo_sems.at[1, 0], following),
            remote(bc_hbm.at[last, :], rim_bc, halo_sems.at[0, 1], halo_sems.at[1, 1], following),
            remote(ids_sent, rim_ids, halo_sems.at[0, 2], halo_sems.at[1, 2], following),
        ]

    @pl.when(has_next)
    def send_halo():
        for copy in halo_copies():
            copy.start()

    def column(row):
        return jnp.broadcast_to(row, (128, row.shape[1])).T

    logits = dt_ref[...].astype(f32) + column(rows_ref[:, HEADS_PAD : 2 * HEADS_PAD])[:heads, 0:1]
    step_size = jnp.maximum(logits, 0.0) + jnp.log1p(jnp.exp(-jnp.abs(logits)))
    rates = -jnp.exp(column(rows_ref[:, :HEADS_PAD])[:heads, 0:1]) * step_size
    spare = jnp.zeros((HEADS_PAD - heads, rows), f32)
    step_size = jnp.concatenate([step_size, spare])
    rates = jnp.concatenate([rates, spare])
    ids_ext[8 : 8 + rows, :] = column(ids_row)
    ids = ids_ext[8 : 8 + rows, :]

    for load in first_loads:
        load.wait()

    @pl.when(has_prev)
    def take_halo():
        for copy in halo_copies():
            copy.wait_recv()

    ids_ext[0:8, :] = column(rim_ids[0:1, :])[120:128, :]
    taps = conv_x_ref.shape[0]
    keeps = []
    for k in range(1, taps):
        same = ids_ext[8 - k : 8 - k + rows, :] == ids
        keeps.append(jnp.concatenate([same.astype(f32)] * (size // 128), axis=1) > 0.5)
    ext[0:8, :] = rim_bc[...].astype(f32)[8:16]
    ext[8 : 8 + rows, :] = bc_in_ref[...].astype(f32)
    mixed_bc = conv_taps(ext, conv_bc_ref[...].astype(f32), keeps, rows)
    bc_ref[...] = mixed_bc.astype(bf16)
    row_id = lax.broadcasted_iota(jnp.int32, (SPAN, SPAN), 0)
    col_id = lax.broadcasted_iota(jnp.int32, (SPAN, SPAN), 1)
    upper = (row_id <= col_id).astype(f32)
    for b in range(blocks):
        span = slice(b * SPAN, (b + 1) * SPAN)
        b_t[:, span] = mixed_bc[span, :state_size].T.astype(bf16)
        cum = jnp.dot(
            rates[:, span], upper,
            precision=lax.Precision.HIGHEST, preferred_element_type=f32,
        )
        cum_ref[:, span] = cum
        cum_t = cum.T
        step_t = step_size[:, span].T
        cum_t_ref[span, :] = cum_t
        step_t_ref[span, :] = step_t
        prior = ids_ext[8 + b * SPAN - 1 : 8 + b * SPAN, :]
        final = ids_ext[8 + (b + 1) * SPAN - 1 : 8 + (b + 1) * SPAN, :]
        gain_t_ref[span, :] = jnp.where(ids[span] == prior, jnp.exp(cum_t), 0.0)
        tail_t[span, :] = jnp.where(
            ids[span] == final, jnp.exp(cum_t[SPAN - 1 : SPAN] - cum_t), 0.0
        ) * step_t
    decay = gain_t_ref[SPAN - 1 : SPAN, :]
    for b in range(1, blocks):
        decay = decay * gain_t_ref[(b + 1) * SPAN - 1 : (b + 1) * SPAN, :]
    own_decay[...] = jnp.broadcast_to(decay, own_decay.shape)
    decay_copy().start()

    def decay_row(ref, k):
        turn = lax.rem(HEADS_PAD - (parity * pieces + k) * per_group, HEADS_PAD)
        turn = lax.rem(turn + HEADS_PAD, HEADS_PAD)
        return spread_heads(pltpu.roll(ref[...], turn, 1), head_size, size)[0:1]

    def first_state(k):
        mine = state_ref[:, lanes_of(parity, k)].astype(f32)
        theirs = got[k].astype(f32)
        return jnp.where(odd, theirs, mine), jnp.where(odd, mine, theirs)

    def states(j, unused):
        c = lax.rem(j + (1 - parity) * pieces, groups)
        lanes = pl.ds(pl.multiple_of(c * size, size), size)
        turn = lax.rem(HEADS_PAD - c * per_group, HEADS_PAD)
        ext[0:8, :] = rim_x[:, lanes].astype(f32)[8:16]
        ext[8 : 8 + rows, :] = x_ref[:, lanes].astype(f32)
        mixed = conv_taps(ext, conv_x_ref[:, lanes].astype(f32), keeps, rows).astype(bf16)
        mixed_ref[:, lanes] = mixed
        weight = spread_heads(pltpu.roll(tail_t[...], turn, 1), head_size, size)
        weighted = (mixed.astype(f32) * weight).astype(bf16)
        running = None
        for b in range(blocks):
            span = slice(b * SPAN, (b + 1) * SPAN)
            fresh = jnp.dot(b_t[:, span], weighted[span], preferred_element_type=f32)
            ends = gain_t_ref[(b + 1) * SPAN - 8 : (b + 1) * SPAN, :]
            block_decay = spread_heads(pltpu.roll(ends, turn, 1), head_size, size)[7:8]
            if b + 1 < blocks:
                fresh_ref[b, :, lanes] = fresh
                decay_ref[b, :, lanes] = jnp.broadcast_to(block_decay, (8, size))
            running = fresh if b == 0 else block_decay * running + fresh
        state_ref[:, lanes] = running.astype(bf16)

        @pl.when(j < pieces)
        def send_state():
            state_copy(j).start()

        @pl.when(j == pieces)
        def take_decay():
            decay_copy().wait_recv()
            pair_decay[...] = own_decay[...] * got_decay[...]

            @pl.when(has_up)
            def pass_decay():
                pair_decay_copy().start()

        @pl.when(j >= pieces)
        def join():
            k = j - pieces
            state_copy(k).wait_recv()

            @pl.when(has_up)
            def send_whole():
                first, second = first_state(k)
                odd_decay = jnp.where(odd, decay_row(own_decay, k), decay_row(got_decay, k))
                whole[k] = (second + odd_decay * first).astype(bf16)
                whole_copy(k).start()

        return unused

    lax.fori_loop(0, groups, states, 0)
    ids_wide = jnp.concatenate([ids] * (SPAN // 128), axis=1)
    skip_tile = jnp.broadcast_to(rows_ref[:, 2 * HEADS_PAD : 3 * HEADS_PAD], (8, HEADS_PAD))
    for b in range(blocks):
        span = slice(b * SPAN, (b + 1) * SPAN)
        raw = lax.dot_general(
            bc_ref[span, state_size:], bc_ref[span, :state_size], (((1,), (1,)), ((), ())),
            preferred_element_type=f32,
        )
        same = (ids_wide[span] == ids_row[:, span]) & (col_id <= row_id)
        scores[b] = jnp.where(same, raw, 0.0)

    def mix(c, b):
        lanes = pl.ds(pl.multiple_of(c * size, size), size)
        span = pl.ds(b * SPAN, SPAN)
        turn = lax.rem(HEADS_PAD - c * per_group, HEADS_PAD)
        cum_t = pltpu.roll(cum_t_ref[span, :], turn, 1)
        steps = spread_heads(pltpu.roll(step_t_ref[span, :], turn, 1), head_size, size)
        x = mixed_ref[span, lanes].astype(f32)
        stepped = (x * steps).astype(bf16)
        skip = spread_heads(pltpu.roll(skip_tile, turn, 1), head_size, size)[0:1]
        tops, bottoms = [], []
        for k in range(per_group):
            own = slice(k * head_size, (k + 1) * head_size)
            column = cum_t[:, k : k + 1]
            row = cum_ref[pl.ds(c * per_group + k, 1), span]
            top = scores[b, :half, :half] * jnp.exp(
                jnp.minimum(column[:half] - row[:, :half], 0.0)
            )
            bottom = scores[b, half:, :] * jnp.exp(jnp.minimum(column[half:] - row, 0.0))
            tops.append(
                jnp.dot(top.astype(bf16), stepped[:half, own], preferred_element_type=f32)
            )
            bottoms.append(
                jnp.dot(bottom.astype(bf16), stepped[:, own], preferred_element_type=f32)
            )
        both = jnp.concatenate(
            [jnp.concatenate(tops, axis=1), jnp.concatenate(bottoms, axis=1)], axis=0
        )
        part_ref[span, lanes] = both + skip * x

    def step(j, unused):
        @pl.when(j < pieces)
        def forward():
            @pl.when(has_down)
            def take_near():
                whole_copy(j).wait_recv()

                @pl.when(has_up)
                def pass_near():
                    far_copy(j).start()

        @pl.when(j >= pieces)
        def close():
            k = j - pieces

            @pl.when((k == 0) & has_down)
            def take_near_decay():
                pair_decay_copy().wait_recv()

            @pl.when(has_far)
            def take_far():
                far_copy(k).wait_recv()

            entering = near[k].astype(f32) + decay_row(near_decay, k) * far[k].astype(f32)
            first, _ = first_state(k)
            even_decay = jnp.where(odd, decay_row(got_decay, k), decay_row(own_decay, k))
            later = first + even_decay * entering
            enter_ref[:, lanes_of(parity, k)] = jnp.where(odd, later, entering).astype(bf16)
            sent[k] = jnp.where(odd, entering, later).astype(bf16)
            land_copy(k).start()

        mix(j, 0)
        return unused

    lax.fori_loop(0, groups, step, 0)
    for k in range(pieces):
        land_copy(k).wait_recv()
        enter_ref[:, lanes_of(1 - parity, k)] = landed[k]
    loads[0].wait()
    count = rows // chunk
    per_block = SPAN // chunk
    gate_size = 512
    gate_heads = gate_size // head_size
    tile = 256 if out_width % 256 == 0 else 128

    def product(here, weights, store):
        def columns(j, unused):
            lanes = pl.ds(pl.multiple_of(j * tile, tile), tile)
            store(
                lanes,
                jnp.dot(
                    scaled[here, :], weights[:, lanes],
                    preferred_element_type=jnp.float32,
                ).astype(jnp.bfloat16),
            )
            return unused

        lax.fori_loop(0, out_width // tile, columns, 0)

    copies = []
    for q in range(count):
        b, within = q // per_block, q % per_block
        here = slice(q * chunk, (q + 1) * chunk)

        def group(c, squares):
            lanes = pl.ds(pl.multiple_of(c * gate_size, gate_size), gate_size)
            turn = lax.rem(HEADS_PAD - c * gate_heads, HEADS_PAD)
            if q == 0:
                state[:, lanes] = enter_ref[:, lanes]
            elif within == 0:
                state[:, lanes] = (
                    decay_ref[b - 1, 0:1, lanes] * state[:, lanes].astype(jnp.float32)
                    + fresh_ref[b - 1, :, lanes]
                ).astype(jnp.bfloat16)
            gains = rows_ref[:, pl.ds(pl.multiple_of(3 * HEADS_PAD + c * gate_size, 128), gate_size)]
            gain = spread_heads(pltpu.roll(gain_t_ref[here, :], turn, 1), head_size, gate_size)
            reached = jnp.dot(
                bc_ref[here, state_size:], state[:, lanes], preferred_element_type=jnp.float32
            )
            y = part_ref[here, lanes] + gain * reached
            y = y.astype(jnp.bfloat16).astype(jnp.float32)
            gated = y * silu(z_ref[here, lanes].astype(jnp.float32))
            scaled[here, lanes] = (gated * gains).astype(jnp.bfloat16)
            square = gated * gated
            for k in range(gate_size // 128):
                squares = squares + square[:, k * 128 : (k + 1) * 128]
            return squares

        if b > 0 and within == 0:

            def mix_later(c, unused, b=b):
                mix(c, b)
                return unused

            lax.fori_loop(0, groups, mix_later, 0)

        squares = lax.fori_loop(0, width // gate_size, group, jnp.zeros((chunk, 128), jnp.float32))
        row = jnp.sum(squares.T, axis=0, keepdims=True)
        row_sends[q] = jnp.broadcast_to(row, (8, chunk))
        if q == 0:
            loads[1].wait()

        def put(lanes, value):
            sends[q, :, lanes] = value

        product(here, w_far, put)
        pair = [
            pltpu.make_async_remote_copy(
                src_ref=source.at[q],
                dst_ref=landing.at[q],
                send_sem=out_sems.at[q],
                recv_sem=in_sems.at[q],
                device_id={"tensor": peer},
                device_id_type=pl.DeviceIdType.MESH,
            )
            for source, landing, out_sems, in_sems in (
                (row_sends, row_gots, row_send_sems, row_got_sems),
                (sends, gots, send_sems, got_out_sems),
            )
        ]
        for copy in pair:
            copy.start()
        copies.append(pair)

    loads[2].wait()

    def keep(lanes, value):
        sums[:, lanes] = value

    product(slice(0, rows), w_near, keep)
    for q in range(count):
        here = slice(q * chunk, (q + 1) * chunk)
        for copy in copies[q]:
            copy.wait_recv()
        row = row_sends[q, 0:1, :] + row_gots[q, 0:1, :]
        inv_row = lax.rsqrt(row / (2 * width) + 1e-05)
        inv = jnp.broadcast_to(inv_row, (128, chunk)).T
        for j in range(out_width // 128):
            lanes = slice(j * 128, (j + 1) * 128)
            total = sums[here, lanes].astype(jnp.float32) + gots[q, :, lanes].astype(jnp.float32)
            out_ref[here, lanes] = (total * inv).astype(jnp.bfloat16)
    for pair in copies:
        for copy in pair:
            copy.wait_send()

    @pl.when(has_next)
    def finish_halo():
        for copy in halo_copies():
            copy.wait_send()

    decay_copy().wait_send()
    for k in range(pieces):
        state_copy(k).wait_send()
        land_copy(k).wait_send()

    @pl.when(has_up)
    def finish():
        pair_decay_copy().wait_send()
        for k in range(pieces):
            whole_copy(k).wait_send()

    @pl.when(has_up & has_down)
    def finish_far():
        for k in range(pieces):
            far_copy(k).wait_send()


def call(kernel, out_shape, scratch, flops, moved, *operands):
    return pl.pallas_call(
        kernel,
        out_shape=out_shape,
        in_specs=[pl.BlockSpec(memory_space=pltpu.VMEM)] * len(operands),
        out_specs=jax.tree.map(lambda _: pl.BlockSpec(memory_space=pltpu.VMEM), out_shape),
        scratch_shapes=scratch,
        compiler_params=pltpu.CompilerParams(vmem_limit_bytes=VMEM_BYTES),
        cost_estimate=pl.CostEstimate(flops=flops, bytes_accessed=moved, transcendentals=0),
    )(*operands)


def split_message(message):
    state_size = message.shape[0] - EXTRA
    wide = message.astype(jnp.float32)
    return wide[:state_size], wide[state_size : state_size + 1] + wide[state_size + 8 : state_size + 9]


def merge(near, far):
    near_state, near_decay = near
    far_state, far_decay = far
    return near_state + near_decay * far_state, near_decay * far_decay


def pack_message(pair):
    state, decay = pair
    width = state.shape[1]
    high = decay.astype(jnp.bfloat16)
    low = (decay - high.astype(jnp.float32)).astype(jnp.bfloat16)
    return jnp.concatenate(
        [
            state.astype(jnp.bfloat16),
            jnp.broadcast_to(high, (8, width)),
            jnp.broadcast_to(low, (8, width)),
        ]
    )


def pass_state(message):
    count = lax.axis_size("seq")
    odd = (lax.axis_index("seq") % 2) == 1
    other = lax.ppermute(message, "seq", [(i, i ^ 1) for i in range(count)])
    first = split_message(jnp.where(odd, other, message))
    second = split_message(jnp.where(odd, message, other))
    entering = shifted(pack_message(merge(second, first)), "seq", 2)
    reach = 1
    while reach < count // 4:
        farther = shifted(entering, "seq", 2 * reach)
        joined = merge(split_message(entering), split_message(farther))
        reach *= 2
        if reach < count // 4:
            entering = pack_message(joined)
        else:
            entering = joined
    if reach == 1:
        entering = split_message(entering)
    alone = split_message(other)
    return jnp.where(odd, merge(alone, entering)[0], entering[0])


def local(
    x_stream,
    bc_stream,
    z_gate,
    dt_stream,
    doc_ids,
    conv_x,
    conv_bc,
    a_log,
    dt_bias,
    d_skip,
    norm_gain,
    w_out,
):
    rows, width = x_stream.shape
    heads = dt_stream.shape[0]
    head_size = width // heads
    bc_width = bc_stream.shape[1]
    state_size = bc_width // 2
    taps = conv_x.shape[0]
    blocks = rows // SPAN
    edge = rows - taps + 1
    f32, bf16 = jnp.float32, jnp.bfloat16
    shape = jax.ShapeDtypeStruct
    out_width = w_out.shape[1] // lax.axis_size("tensor")
    if (
        lax.axis_size("seq") == 8
        and lax.axis_size("tensor") == 2
        and width % 512 == 0
        and width >= 1536
        and out_width % 128 == 0
        and bc_width == group_lanes(width)
        and heads <= HEADS_PAD
        and heads % 8 == 0
    ):
        vmem = pl.BlockSpec(memory_space=pltpu.VMEM)
        hbm = pl.BlockSpec(memory_space=pl.ANY)
        pieces = width // 512
        chunk = 128
        count = rows // chunk
        piece = (pieces, state_size, 256)

        def padded(values):
            return jnp.pad(values, (0, HEADS_PAD - heads))

        return pl.pallas_call(
            functools.partial(fused_kernel, head_size, chunk),
            out_shape=shape((rows, out_width), bf16),
            in_specs=[hbm] * 4 + [vmem] * 5,
            out_specs=vmem,
            scratch_shapes=[
                pltpu.VMEM((rows, width), bf16),
                pltpu.VMEM((rows, bc_width), bf16),
                pltpu.VMEM((rows + 8, 256), f32),
                pltpu.VMEM((rows + 8, 128), f32),
                pltpu.VMEM((16, width), bf16),
                pltpu.VMEM((16, bc_width), bf16),
                pltpu.VMEM((8, 128), f32),
                pltpu.VMEM((8, 128), f32),
                pltpu.VMEM((rows, width), bf16),
                pltpu.VMEM((rows, bc_width), bf16),
                pltpu.VMEM((HEADS_PAD, rows), f32),
                pltpu.VMEM((rows, HEADS_PAD), f32),
                pltpu.VMEM((rows, HEADS_PAD), f32),
                pltpu.VMEM((rows, HEADS_PAD), f32),
                pltpu.VMEM((rows, HEADS_PAD), f32),
                pltpu.VMEM((state_size, rows), bf16),
                pltpu.VMEM((blocks, state_size, width), f32),
                pltpu.VMEM((blocks, 8, width), f32),
                pltpu.VMEM((state_size, width), bf16),
                pltpu.VMEM((rows, width), f32),
                pltpu.VMEM((state_size, width), bf16),
                pltpu.VMEM((blocks, SPAN, SPAN), f32),
            ]
            + [pltpu.VMEM(piece, bf16)] * 6
            + [pltpu.VMEM((8, HEADS_PAD), f32)] * 4
            + [
                pltpu.VMEM((rows, width), bf16),
                pltpu.VMEM((width, out_width), bf16),
                pltpu.VMEM((width, out_width), bf16),
                pltpu.VMEM((rows, width), bf16),
                pltpu.VMEM((state_size, width), bf16),
                pltpu.VMEM((rows, out_width), bf16),
                pltpu.VMEM((count, chunk, out_width), bf16),
                pltpu.VMEM((count, chunk, out_width), bf16),
                pltpu.VMEM((count, 8, chunk), f32),
                pltpu.VMEM((count, 8, chunk), f32),
                pltpu.SemaphoreType.DMA((2, 3)),
                pltpu.SemaphoreType.DMA((5,)),
                pltpu.SemaphoreType.DMA((4,)),
            ]
            + [pltpu.SemaphoreType.DMA((2, pieces))] * 4
            + [pltpu.SemaphoreType.DMA((count,))] * 4,
            compiler_params=pltpu.CompilerParams(
                collective_id=0, has_side_effects=True, vmem_limit_bytes=FUSED_VMEM_BYTES
            ),
            cost_estimate=pl.CostEstimate(
                flops=2 * rows * width * w_out.shape[1],
                bytes_accessed=2 * width * w_out.shape[1],
                transcendentals=0,
            ),
        )(
            x_stream, bc_stream, z_gate, w_out, dt_stream, doc_ids[None, :], conv_x, conv_bc,
            jnp.concatenate(
                [padded(a_log), padded(dt_bias), padded(d_skip), norm_gain]
            )[None, :],
        )
    own_ids = doc_ids.astype(f32)
    tail_ids = jnp.broadcast_to(own_ids[edge:].astype(bf16)[:, None], (taps - 1, 128))
    rim = shifted(
        jnp.concatenate([x_stream[edge:], bc_stream[edge:], tail_ids], axis=1), "seq", 1
    )
    step = jax.nn.softplus(dt_stream.astype(f32) + dt_bias[:, None])
    rate = -jnp.exp(a_log)[:, None] * step
    step = jnp.pad(step, ((0, HEADS_PAD - heads), (0, 0)))
    rate = jnp.pad(rate, ((0, HEADS_PAD - heads), (0, 0)))
    rim_wide = jnp.pad(rim.astype(f32), ((8 - taps + 1, 0), (0, 0)))
    rim_ids = jnp.where(lax.axis_index("seq") == 0, -1.0, rim[:, width + bc_width].astype(f32))
    ext_ids = jnp.concatenate([rim_ids, own_ids])
    block_ids = own_ids.reshape(blocks, SPAN)
    prior = jnp.concatenate([ext_ids[taps - 2][None], own_ids[SPAN - 1 :: SPAN][: blocks - 1]])
    columns = [(ext_ids[taps - 1 - k : taps - 1 - k + rows] == own_ids) for k in range(1, taps)]
    columns.append((block_ids == prior[:, None]).reshape(rows))
    columns.append((block_ids == block_ids[:, -1:]).reshape(rows))
    flags = jnp.stack([c.astype(f32) for c in columns], axis=1)

    mixed, mixed_bc, cum, cum_t, step_t, gain_t, fresh, decay, message = call(
        functools.partial(states_kernel, head_size),
        (
            shape((rows, width), bf16),
            shape((rows, bc_width), bf16),
            shape((HEADS_PAD, rows), f32),
            shape((rows, HEADS_PAD), f32),
            shape((rows, HEADS_PAD), f32),
            shape((rows, HEADS_PAD), f32),
            shape((blocks, state_size, width), f32),
            shape((blocks, 8, width), f32),
            shape((state_size + EXTRA, width), bf16),
        ),
        [
            pltpu.VMEM((rows + 8, max(bc_width, group_lanes(width))), f32),
            pltpu.VMEM((rows, HEADS_PAD), f32),
            pltpu.VMEM((state_size, rows), bf16),
        ],
        2 * rows * state_size * width,
        8 * rows * width,
        x_stream, rim_wide[:, :width], bc_stream, rim_wide[:, width : width + bc_width], step, rate,
        flags, conv_x.astype(f32), conv_bc.astype(f32),
    )
    skip_row = jnp.repeat(d_skip, head_size)[None, :]
    parts = []
    for b in range(blocks):
        span = slice(b * SPAN, (b + 1) * SPAN)
        parts.append(
            call(
                functools.partial(mix_kernel, head_size),
                shape((SPAN, width), f32),
                [pltpu.VMEM((SPAN, SPAN), f32)],
                2 * SPAN * SPAN * width * 16,
                8 * SPAN * width,
                mixed[span], mixed_bc[span], cum[:, span], cum_t[span], step_t[span],
                own_ids[span][:, None], own_ids[span][None, :], skip_row,
            )
        )
    state = pass_state(message)

    members = lax.axis_size("tensor")
    member = lax.axis_index("tensor")
    pieces = []
    for b in range(blocks):
        span = slice(b * SPAN, (b + 1) * SPAN)
        scaled, squares = call(
            functools.partial(gate_kernel, head_size),
            (shape((SPAN, width), bf16), shape((SPAN, 128), f32)),
            [],
            2 * SPAN * state_size * width,
            12 * SPAN * width,
            state.astype(bf16), mixed_bc[span], gain_t[span], parts[b], z_gate[span],
            norm_gain[None, :],
        )
        if b + 1 < blocks:
            state = decay[b, 0:1] * state + fresh[b]
        product = jnp.dot(scaled, w_out, preferred_element_type=f32).astype(bf16)
        total = lax.dynamic_slice_in_dim(product, member * out_width, out_width, 1).astype(f32)
        square = jnp.sum(squares, axis=1, keepdims=True)
        high = square.astype(bf16)
        low = (square - high.astype(f32)).astype(bf16)
        lane = lax.broadcasted_iota(jnp.int32, (SPAN, 128), 1)
        aside = jnp.where(lane == 0, high, jnp.where(lane == 1, low, jnp.zeros_like(low)))
        for distance in range(1, members):
            target = (member + distance) % members
            block = lax.dynamic_slice_in_dim(product, target * out_width, out_width, 1)
            route = [(i, (i + distance) % members) for i in range(members)]
            got = lax.ppermute(jnp.concatenate([block, aside], axis=1), "tensor", route)
            total = total + got[:, :out_width].astype(f32)
            square = square + jnp.sum(got[:, out_width : out_width + 2].astype(f32), axis=1, keepdims=True)
        inv_norm = lax.rsqrt(square / (width * members) + 1e-05)
        pieces.append((total * inv_norm).astype(bf16))
    return jnp.concatenate(pieces)


def solution(mesh):
    return jax.shard_map(
        local,
        mesh=mesh,
        in_specs=(
            P(("dp", "seq"), "tensor"),
            P(("dp", "seq"), None),
            P(("dp", "seq"), "tensor"),
            P("tensor", ("dp", "seq")),
            P(("dp", "seq")),
            P(None, "tensor"),
            P(),
            P("tensor"),
            P("tensor"),
            P("tensor"),
            P("tensor"),
            P("tensor", None),
        ),
        out_specs=P(("dp", "seq"), "tensor"),
        check_vma=False,
    )
```
